32 devices in a mesh: dp: 4 (over z), leaf: 8 (over y, x, core).
Axes of the slice: x: 2, y: 2, z: 4, core: 2. Of those that a mesh axis runs over, the one named last changes fastest.
Arguments:
- queries: bfloat16 [64, 128, 1024], P(('dp', 'leaf')), parts along dimension 0, may hold values from -99 to 99
- key_states: bfloat16 [64, 128, 128], P(('dp', 'leaf')), parts along dimension 0, may hold values from -4 to 4
- value_states: bfloat16 [64, 128, 128], P(('dp', 'leaf')), parts along dimension 0, may hold values from -6 to 6
- grad_output: bfloat16 [64, 128, 1024], P(('dp', 'leaf')), parts along dimension 0, may hold values from -120 to 120
- lengths: int32 [64], P(('dp', 'leaf')), parts along dimension 0, may hold values from 16 to 128, as said below
Outputs:
- grad_queries: bfloat16 [64, 128, 1024], P(('dp', 'leaf')), parts along dimension 0
- grad_keys: bfloat16 [64, 128, 128], P(('dp', 'leaf')), parts along dimension 0
- grad_values: bfloat16 [64, 128, 128], P(('dp', 'leaf')), parts along dimension 0
The draws below stay inside these ranges and needn't reach their ends.
There are 4 independent parts, one for each index of `dp`. The reference program is written for one: setup_inputs(seed, part) draws one part's arguments, and reference() takes and returns one part's arrays. A program takes and returns all parts, laid end to end along the dimension named above; each array names one. Nothing has to cross between parts.
Inputs may be any that keep to these rules, and one draw needn't show every extreme that they name: `lengths`: every entry is at least 1; entry 0 (the prompt) is always 128.
All inputs are finite; a program needn't handle non-finite values.
Results may differ from the reference program's by a relative error of at most 0.0095.
Values may be sent and summed in bfloat16 or wider, within the bound.
No kernel may reach another device: no remote copies, remote signals or barrier semaphores. Data moves between devices by JAX's collectives and lax.ppermute only.
A program may use at most 64 MiB of HBM per device.

```python
import jax
import jax.numpy as jnp
import numpy as np
from jax import lax

HEADS = 8
HD = 128
SEG = 128
SEGS = 16
N_LEAF = 8


def shared_keys(key):
    base_keys = jnp.clip(jax.random.normal(key, (SEGS, SEG, HD), jnp.float32), -4.0, 4.0)
    return base_keys


def draw_key_states(key, part):
    base_keys = shared_keys(key)
    return base_keys.astype(jnp.bfloat16)


def draw_queries(key, part):
    key = jax.random.fold_in(key, 5)
    normal = jnp.clip(jax.random.normal(key, (SEGS, SEG, HEADS, HD), jnp.float32), -5.0, 5.0)
    return normal.reshape(SEGS, SEG, HEADS * HD).astype(jnp.bfloat16)


def draw_lengths(key, part):
    key = jax.random.fold_in(key, 11)
    drawn_lengths = jax.random.randint(key, (SEGS,), max(1, SEG // 8), SEG + 1)
    return drawn_lengths.at[0].set(SEG).astype(jnp.int32)


def block_levels(stream_key, dims, split, low, top_value):
    def one(axis_at, shards_of):
        steps = jax.random.uniform(jax.random.fold_in(jax.random.fold_in(stream_key, 6), axis_at), (shards_of,), jnp.float32, low / len(split), top_value / len(split))
        return jnp.repeat(jnp.exp(steps), dims[axis_at] // shards_of).reshape((-1,) + (1,) * (len(dims) - axis_at - 1))

    level = one(*split[0])
    for cut in split[1:]:
        level = level * one(*cut)
    return level


def normal_values(key, extent, spread, limit, pieces=(), kind=jnp.bfloat16):
    drawn = jax.random.normal(key, extent, jnp.float32) * spread
    if len(pieces) > 0:
        drawn = block_levels(key, extent, pieces, -0.22, 0.18) * drawn
    return jnp.clip(drawn, min=-limit, max=limit).astype(kind)


def setup_inputs(seed: int = 0, part: int = 0) -> dict:
    seeds = jax.random.split(jax.random.key(seed), 6)
    part_keys = jax.random.split(jax.random.fold_in(seeds[5], part), 6)
    return {
        "queries": draw_queries(jax.random.fold_in(jax.random.fold_in(seeds[5], part), 71), part),
        "key_states": draw_key_states(jax.random.fold_in(jax.random.fold_in(seeds[5], part), 71), part),
        "value_states": normal_values(part_keys[2], (SEGS, SEG, HD), 1.0, 6.0, ((0, 8),)),
        "grad_output": normal_values(part_keys[3], (SEGS, SEG, HEADS * HD), 20.0, 120.0, ((0, 8),)),
        "lengths": draw_lengths(jax.random.fold_in(jax.random.fold_in(seeds[5], part), 71), part),
    }


def tree_tables(leaf_count):
    tree_depth = leaf_count.bit_length() - 1
    path_rows = np.zeros((2 * leaf_count, tree_depth + 2), np.int32)
    segment_level = np.zeros((2 * leaf_count,), np.int32)
    for leaf_index in range(leaf_count):
        owners = [0]
        for depth_level in range(1, tree_depth + 1):
            shift_by = tree_depth - depth_level + 1
            owners.append((leaf_index >> shift_by << shift_by) + (1 << tree_depth - depth_level))
        path_list = [2 * owner for owner in owners] + [2 * leaf_index + 1]
        path_rows[2 * leaf_index] = path_list
        path_rows[2 * leaf_index + 1] = path_list
        if leaf_index == 0:
            trailing = tree_depth
        else:
            trailing = (leaf_index & -leaf_index).bit_length() - 1
        segment_level[2 * leaf_index] = tree_depth - trailing
        segment_level[2 * leaf_index + 1] = tree_depth + 1
    return (path_rows, segment_level)

def build_mask(query_level, query_length, path_length, seg_rows):
    path_slots = path_length.shape[0]
    levels = jnp.arange(path_slots, dtype=jnp.int32)[:, None]
    position = jnp.arange(seg_rows, dtype=jnp.int32)
    key_live = position[None, :] < path_length[:, None]
    before = (levels < query_level) & key_live
    same_level = (levels == query_level) & (position[None, :] < query_length)
    causal = position[None, None, :] <= position[:, None, None]
    allowed = before[None] | same_level[None] & causal
    return allowed.reshape(seg_rows, path_slots * seg_rows)

def attend_grad(query_block, grad_block, path_keys, path_values, allowed, head_count):
    query_rows = query_block.shape[0]
    head_width = path_keys.shape[-1]
    score_scale = head_width ** (-0.5)
    query_heads = query_block.reshape(query_rows, head_count, head_width).astype(jnp.float32)
    grad_heads = grad_block.reshape(query_rows, head_count, head_width).astype(jnp.float32)
    key_flat = path_keys.reshape(-1, head_width).astype(jnp.float32)
    value_flat = path_values.reshape(-1, head_width).astype(jnp.float32)
    scores = jnp.einsum('qhd,kd->hqk', query_heads, key_flat) * score_scale
    scores = jnp.where(allowed[None], scores, -1e+30)
    row_top = lax.optimization_barrier(jnp.max(scores, axis=2, keepdims=True))
    row_total = lax.optimization_barrier(jnp.sum(jnp.exp(scores - row_top), axis=2, keepdims=True))
    weights = jnp.exp(scores - (row_top + jnp.log(row_total)))
    weights_low = weights.astype(jnp.bfloat16).astype(jnp.float32)
    output = jnp.einsum('hqk,kd->qhd', weights_low, value_flat)
    row_delta = lax.optimization_barrier(jnp.sum(grad_heads * output, axis=2))
    grad_value_terms = jnp.einsum('hqk,qhd->kd', weights_low, grad_heads)
    grad_weights = jnp.einsum('qhd,kd->hqk', grad_heads, value_flat)
    grad_scores = (weights * (grad_weights - row_delta.T[:, :, None]) * score_scale).astype(jnp.bfloat16)
    grad_scores = grad_scores.astype(jnp.float32)
    grad_query_block = jnp.einsum('hqk,kd->qhd', grad_scores, key_flat)
    grad_query_block = grad_query_block.reshape(query_rows, head_count * head_width).astype(jnp.bfloat16)
    grad_key_terms = jnp.einsum('hqk,qhd->kd', grad_scores, query_heads)
    return (grad_query_block, grad_key_terms.reshape(path_keys.shape), grad_value_terms.reshape(path_keys.shape))

def reference(queries, key_states, value_states, grad_output, lengths):
    table_rows, table_level = tree_tables(N_LEAF)
    path_rows = jnp.asarray(table_rows)
    segment_level = jnp.asarray(table_level)
    position = jnp.arange(SEG, dtype=jnp.int32)

    def segment_grads(segment):
        path_list = path_rows[segment]
        path_keys = key_states[path_list]
        path_values = value_states[path_list]
        path_length = lengths[path_list]
        query_length = lengths[segment]
        allowed = build_mask(segment_level[segment], query_length, path_length, SEG)
        live_rows = (position < query_length)[:, None]
        cotangent = jnp.where(live_rows, grad_output[segment], jnp.zeros((), jnp.bfloat16))
        return attend_grad(queries[segment], cotangent, path_keys, path_values, allowed, HEADS)
    grad_queries, key_terms, value_terms = lax.map(segment_grads, jnp.arange(2 * N_LEAF, dtype=jnp.int32))
    flat_rows = path_rows.reshape(-1)
    grad_keys = jnp.zeros((2 * N_LEAF, SEG, HD), jnp.float32).at[flat_rows].add(key_terms.reshape(-1, SEG, HD))
    grad_values = jnp.zeros((2 * N_LEAF, SEG, HD), jnp.float32).at[flat_rows].add(value_terms.reshape(-1, SEG, HD))
    return (grad_queries, grad_keys.astype(jnp.bfloat16), grad_values.astype(jnp.bfloat16))
```

```python
import functools

import jax
import jax.numpy as jnp
from jax import lax
from jax.experimental import pallas as pl
from jax.experimental.pallas import tpu as pltpu
from jax.sharding import PartitionSpec as P

BF16 = jnp.bfloat16
F32 = jnp.float32
TAIL = 16
BIG = -1e30
LOG2E = 1.4426950408889634
NT = (((1,), (1,)), ((), ()))
NN = (((1,), (0,)), ((), ()))


def depth_of(count):
    return count.bit_length() - 1


def trailing_zeros(index, depth):
    total = jnp.zeros((), jnp.int32)
    for bit in range(depth):
        total = total + jnp.where((index & ((2 << bit) - 1)) == 0, 1, 0)
    return total


def owner_of(index, level, depth):
    if level == 0:
        return index * 0
    shift = depth - level + 1
    return ((index >> shift) << shift) + (1 << (depth - level))


def on_path(reader, owner, depth):
    return any(owner_of(reader, level, depth) == owner for level in range(depth + 1))


def down_pairs(mask, count):
    depth = depth_of(count)
    pairs = []
    for owner in range(0, count, 2):
        reader = owner ^ (mask << 1)
        if on_path(reader, owner, depth):
            pairs.append((owner, reader))
    return pairs


def pack_kernel(lengths_ref, key_ref, value_ref, pack_ref):
    rows = key_ref.shape[1]
    pack_ref[0:rows, :] = key_ref[0]
    pack_ref[rows : 2 * rows, :] = value_ref[0]
    length = lengths_ref[0].astype(F32)
    pack_ref[2 * rows :, :] = jnp.full((TAIL, pack_ref.shape[1]), length, F32).astype(BF16)


def make_pack(lengths, keys, values):
    rows, width = keys.shape[1:]
    first = pl.BlockSpec((1, rows, width), lambda step: (0, 0, 0))
    return pl.pallas_call(
        pack_kernel,
        grid=(1,),
        out_shape=jax.ShapeDtypeStruct((2 * rows + TAIL, width), BF16),
        in_specs=[pl.BlockSpec(memory_space=pltpu.SMEM), first, first],
        out_specs=pl.BlockSpec((2 * rows + TAIL, width), lambda step: (0, 0)),
        name="pack",
    )(lengths, keys, values)


def main_kernel(depth, heads, *refs):
    masks = (1 << (depth - 1)) - 1
    lengths_ref, query_ref, grad_ref, key_ref, value_ref, own_ref, mate_ref = refs[:7]
    near = refs[7 : 7 + masks]
    far = refs[7 + masks : 7 + 2 * masks]
    (
        grad_query_ref,
        leaf_ref,
        swap_ref,
        part_ref,
        keys_s,
        values_s,
        extra_s,
        keys_t,
        low_s,
        ds_s,
        query_s,
        cot_s,
    ) = refs[7 + 2 * masks :]
    rows, width = key_ref.shape[1:]
    index = lax.axis_index("leaf")
    parity = index & 1
    own_level = depth - trailing_zeros(index, depth)
    scale = width ** (-0.5)
    lane = lax.broadcasted_iota(jnp.int32, (rows, width), 1)
    row = lax.broadcasted_iota(jnp.int32, (rows, width), 0)
    row_f = row.astype(F32)

    levels = depth + 2
    for level in range(levels):
        span = slice(level * rows, (level + 1) * rows)
        if level == depth + 1:
            key_block, value_block = key_ref[1], value_ref[1]
            length = jnp.full((1, width), lengths_ref[1].astype(F32), F32)
        else:
            if level == depth:
                block = jnp.where(parity == 1, own_ref[...], mate_ref[...])
            else:
                even = index - parity
                pick = (even ^ owner_of(even, level, depth)) >> 1
                block = jnp.where(parity == 1, mate_ref[...], own_ref[...])
                for mask in range(1, masks + 1):
                    other = jnp.where(parity == 1, far[mask - 1][...], near[mask - 1][...])
                    block = jnp.where(pick == mask, other, block)
            key_block, value_block = block[:rows], block[rows : 2 * rows]
            length = block[2 * rows : 2 * rows + 1].astype(F32)
        keys_s[span, :] = key_block
        values_s[span, :] = value_block
        keys_t[:, span] = key_block.T
        dead = row_f >= length
        for segment in range(2):
            if segment == 0 and level == depth + 1:
                continue
            level_of = own_level if segment == 0 else depth + 1
            diagonal = jnp.where(row > 0, row, -1)
            column = jnp.where(level == level_of, diagonal, -1)
            column = jnp.where(dead | (level > level_of), 0, column)
            extra_s[segment, span, :] = jnp.where(lane == column, 1.0, 0.0).astype(BF16)

    ruled = jnp.where((lane > row) | (lane == 0), BIG, 0.0).astype(BF16)
    ruled = jnp.concatenate([ruled, ruled], 0)

    step_rows = 2 * rows
    for segment in range(2):
        count = (depth + 1 + segment) * rows
        live = row < lengths_ref[segment]
        keys_wide = jnp.concatenate([keys_s[:count, :], extra_s[segment, :count, :]], 1)
        for pair in range(heads // 2):
            at = (segment * (heads // 2) + pair) * step_rows
            here = slice(at, at + step_rows)
            columns = [slice(h * width, (h + 1) * width) for h in (2 * pair, 2 * pair + 1)]
            query = jnp.concatenate([query_ref[segment, :, c] for c in columns], 0)
            cot = jnp.concatenate(
                [jnp.where(live, grad_ref[segment, :, c], jnp.zeros((), BF16)) for c in columns], 0
            )
            query_s[here, :] = query
            cot_s[here, :] = cot
            scores = lax.dot_general(
                keys_wide,
                jnp.concatenate([query, ruled], 1),
                NT,
                preferred_element_type=F32,
            )
            top = jnp.max(scores, axis=0, keepdims=True)
            weights = jnp.exp2((scores - top) * (scale * LOG2E))
            total = jnp.sum(weights, axis=0, keepdims=True)
            weights = weights * (1.0 / total)
            low_s[:count, here] = weights.astype(BF16)
            grad_weights = lax.dot_general(
                values_s[:count, :], cot, NT, preferred_element_type=F32
            )
            delta = jnp.sum(weights * grad_weights, axis=0, keepdims=True)
            grad_scores = (weights * (grad_weights - delta)).astype(BF16)
            ds_s[:count, here] = grad_scores
            grad_query = lax.dot_general(
                keys_t[:, :count], grad_scores, NN, preferred_element_type=F32
            )
            grad_query = (grad_query * scale).astype(BF16).T
            for n, c in enumerate(columns):
                grad_query_ref[segment, :, c] = grad_query[n * rows : (n + 1) * rows]

    inner = (depth + 1) * rows
    half = heads * rows
    grad_keys = lax.dot_general(ds_s[:inner, :], query_s[...], NN, preferred_element_type=F32)
    grad_keys = grad_keys * scale
    grad_values = lax.dot_general(low_s[:inner, :], cot_s[...], NN, preferred_element_type=F32)
    leaf_keys = lax.dot_general(
        ds_s[inner:, half:], query_s[half:, :], NN, preferred_element_type=F32
    )
    leaf_values = lax.dot_general(
        low_s[inner:, half:], cot_s[half:, :], NN, preferred_element_type=F32
    )
    leaf_ref[0:rows, :] = (leaf_keys * scale).astype(BF16)
    leaf_ref[rows : 2 * rows, :] = leaf_values.astype(BF16)

    def put(ref, levels_at):
        for place, level in enumerate(levels_at):
            span = slice(level * rows, (level + 1) * rows)
            at = place * 2 * rows
            ref[at : at + rows, :] = grad_keys[span].astype(ref.dtype)
            ref[at + rows : at + 2 * rows, :] = grad_values[span].astype(ref.dtype)

    @pl.when(parity == 1)
    def _():
        put(swap_ref, range(depth))
        put(part_ref, [depth])

    @pl.when(parity == 0)
    def _():
        put(swap_ref, [depth])
        put(part_ref, range(depth))


def main_call(lengths, queries, grads, keys, values, own, mate, near, far, depth):
    rows, width = keys.shape[1:]
    heads = queries.shape[2] // width
    slots = (depth + 2) * rows
    total = 2 * heads * rows
    vmem = pl.BlockSpec(memory_space=pltpu.VMEM)
    return pl.pallas_call(
        functools.partial(main_kernel, depth, heads),
        out_shape=(
            jax.ShapeDtypeStruct(queries.shape, BF16),
            jax.ShapeDtypeStruct((2 * rows, width), BF16),
            jax.ShapeDtypeStruct((depth * 2 * rows, width), BF16),
            jax.ShapeDtypeStruct((depth * 2 * rows, width), F32),
        ),
        in_specs=[pl.BlockSpec(memory_space=pltpu.SMEM)] + [vmem] * (6 + len(near) + len(far)),
        out_specs=(vmem,) * 4,
        scratch_shapes=[
            pltpu.VMEM((slots, width), BF16),
            pltpu.VMEM((slots, width), BF16),
            pltpu.VMEM((2, slots, width), BF16),
            pltpu.VMEM((width, slots), BF16),
            pltpu.VMEM((slots, total), BF16),
            pltpu.VMEM((slots, total), BF16),
            pltpu.VMEM((total, width), BF16),
            pltpu.VMEM((total, width), BF16),
        ],
        compiler_params=pltpu.CompilerParams(vmem_limit_bytes=40 * 1024 * 1024),
        name="attend",
    )(lengths, queries, grads, keys, values, own, mate, *near, *far)


def combine_kernel(depth, part_ref, other_ref, own_ref, *rest):
    sends, both = rest[:-1], rest[-1]
    block = own_ref.shape[0]
    index = lax.axis_index("leaf")
    both[...] = part_ref[...] + other_ref[...].astype(F32)

    def take(level):
        return both[pl.ds(pl.multiple_of(level * block, block), block), :]

    own_level = depth - trailing_zeros(index, depth)
    own_ref[...] = take(jnp.where(index & 1 == 1, 0, own_level))
    for mask, ref in enumerate(sends, 1):
        target = (index - (index & 1)) ^ (mask << 1)
        ref[...] = take(depth - trailing_zeros(target, depth)).astype(BF16)


def combine_call(part, other, depth):
    masks = (1 << (depth - 1)) - 1
    block = part.shape[0] // depth
    width = part.shape[1]
    vmem = pl.BlockSpec(memory_space=pltpu.VMEM)
    return pl.pallas_call(
        functools.partial(combine_kernel, depth),
        out_shape=[jax.ShapeDtypeStruct((block, width), F32)]
        + [jax.ShapeDtypeStruct((block, width), BF16)] * masks,
        in_specs=[vmem] * 2,
        out_specs=[vmem] * (1 + masks),
        scratch_shapes=[pltpu.VMEM(part.shape, F32)],
        name="combine",
    )(part, other)


def final_kernel(leaf_ref, own_ref, *refs):
    arrived, (keys_ref, values_ref) = refs[:-2], refs[-2:]
    rows = keys_ref.shape[1]
    total = own_ref[...]
    for ref in arrived:
        total = total + ref[...].astype(F32)
    total = total.astype(BF16)
    keys_ref[0] = total[:rows]
    values_ref[0] = total[rows:]
    keys_ref[1] = leaf_ref[:rows, :]
    values_ref[1] = leaf_ref[rows:, :]


def final_call(leaf, own, arrived, shape):
    vmem = pl.BlockSpec(memory_space=pltpu.VMEM)
    return pl.pallas_call(
        final_kernel,
        out_shape=[jax.ShapeDtypeStruct(shape, BF16)] * 2,
        in_specs=[vmem] * (2 + len(arrived)),
        out_specs=[vmem] * 2,
        name="final",
    )(leaf, own, *arrived)


def body(queries, key_states, value_states, grad_output, lengths):
    count = lax.axis_size("leaf")
    depth = depth_of(count)
    masks = range(1, count // 2)
    swap_pairs = [(i, i ^ 1) for i in range(count)]
    forward_pairs = [(i, i + 1) for i in range(0, count, 2)]

    pack = make_pack(lengths, key_states, value_states)
    near = [lax.ppermute(pack, "leaf", down_pairs(m, count)) for m in masks]
    mate = lax.ppermute(pack, "leaf", swap_pairs)
    far = [lax.ppermute(block, "leaf", forward_pairs) for block in near]
    grad_queries, leaf, swap, part = main_call(
        lengths, queries, grad_output, key_states, value_states, pack, mate, near, far, depth
    )
    other = lax.ppermute(swap, "leaf", swap_pairs)
    own, *sends = combine_call(part, other, depth)
    arrived = [
        lax.ppermute(block, "leaf", [(b, a) for a, b in down_pairs(m, count)])
        for m, block in zip(masks, sends)
    ]
    grad_keys, grad_values = final_call(leaf, own, arrived, key_states.shape)
    return grad_queries, grad_keys, grad_values


def solution(mesh):
    segments = P(("dp", "leaf"), None, None)
    return jax.shard_map(
        body,
        mesh=mesh,
        in_specs=(segments, segments, segments, segments, P(("dp", "leaf"))),
        out_specs=(segments, segments, segments),
        check_vma=False,
    )
```

```python
import functools

import jax
import jax.numpy as jnp
from jax import lax
from jax.experimental import pallas as pl
from jax.experimental.pallas import tpu as pltpu
from jax.sharding import PartitionSpec as P

BF16 = jnp.bfloat16
F32 = jnp.float32
TAIL = 16
BIG = -1e30
LOG2E = 1.4426950408889634
NT = (((1,), (1,)), ((), ()))
NN = (((1,), (0,)), ((), ()))


def depth_of(count):
    return count.bit_length() - 1


def trailing_zeros(index, depth):
    total = jnp.zeros((), jnp.int32)
    for bit in range(depth):
        total = total + jnp.where((index & ((2 << bit) - 1)) == 0, 1, 0)
    return total


def owner_of(index, level, depth):
    if level == 0:
        return index * 0
    shift = depth - level + 1
    return ((index >> shift) << shift) + (1 << (depth - level))


def owner_at(index, level, depth):
    owner = owner_of(index, 0, depth)
    for place in range(1, depth + 1):
        owner = jnp.where(level == place, owner_of(index, place, depth), owner)
    return owner


def chip_pairs(mask, count):
    return [(i, i ^ (mask << 1)) for i in range(0, count, 2)]


def limit(mib):
    return pltpu.CompilerParams(vmem_limit_bytes=mib * 1024 * 1024)


def pack_kernel(lengths_ref, key_ref, value_ref, pack_ref):
    rows = key_ref.shape[1]
    pack_ref[0:rows, :] = key_ref[0]
    pack_ref[rows : 2 * rows, :] = value_ref[0]
    length = lengths_ref[0].astype(F32)
    pack_ref[2 * rows :, :] = jnp.full((TAIL, pack_ref.shape[1]), length, F32).astype(BF16)


def make_pack(lengths, keys, values):
    rows, width = keys.shape[1:]
    first = pl.BlockSpec((1, rows, width), lambda step: (0, 0, 0))
    return pl.pallas_call(
        pack_kernel,
        grid=(1,),
        out_shape=jax.ShapeDtypeStruct((2 * rows + TAIL, width), BF16),
        in_specs=[pl.BlockSpec(memory_space=pltpu.SMEM), first, first],
        out_specs=pl.BlockSpec((2 * rows + TAIL, width), lambda step: (0, 0)),
        compiler_params=limit(1),
        name="pack",
    )(lengths, keys, values)


def main_kernel(depth, heads, *refs):
    masks = (1 << (depth - 1)) - 1
    lengths_ref, query_ref, grad_ref, key_ref, value_ref, own_ref, mate_ref = refs[:7]
    near = refs[7 : 7 + masks]
    far = refs[7 + masks : 7 + 2 * masks]
    (
        grad_query_ref,
        leaf_ref,
        swap_ref,
        part_ref,
        keys_s,
        values_s,
        extra_s,
        keys_t,
        low_s,
        ds_s,
        query_s,
        cot_s,
    ) = refs[7 + 2 * masks :]
    rows, width = key_ref.shape[1:]
    index = lax.axis_index("leaf")
    parity = index & 1
    own_level = depth - trailing_zeros(index, depth)
    scale = width ** (-0.5)
    lane = lax.broadcasted_iota(jnp.int32, (rows, width), 1)
    row = lax.broadcasted_iota(jnp.int32, (rows, width), 0)
    row_f = row.astype(F32)

    levels = depth + 2
    for level in range(levels):
        span = slice(level * rows, (level + 1) * rows)
        if level == depth + 1:
            key_block, value_block = key_ref[1], value_ref[1]
            length = jnp.full((1, width), lengths_ref[1].astype(F32), F32)
        else:
            if level == depth:
                block = jnp.where(parity == 1, own_ref[...], mate_ref[...])
            else:
                even = index - parity
                pick = (even ^ owner_of(even, level, depth)) >> 1
                block = jnp.where(parity == 1, mate_ref[...], own_ref[...])
                for mask in range(1, masks + 1):
                    other = jnp.where(parity == 1, far[mask - 1][...], near[mask - 1][...])
                    block = jnp.where(pick == mask, other, block)
            key_block, value_block = block[:rows], block[rows : 2 * rows]
            length = block[2 * rows : 2 * rows + 1].astype(F32)
        keys_s[span, :] = key_block
        values_s[span, :] = value_block
        keys_t[:, span] = key_block.T
        dead = row_f >= length
        for segment in range(2):
            if segment == 0 and level == depth + 1:
                continue
            level_of = own_level if segment == 0 else depth + 1
            diagonal = jnp.where(row > 0, row, -1)
            column = jnp.where(level == level_of, diagonal, -1)
            column = jnp.where(dead | (level > level_of), 0, column)
            extra_s[segment, span, :] = jnp.where(lane == column, 1.0, 0.0).astype(BF16)

    ruled = jnp.where((lane > row) | (lane == 0), BIG, 0.0).astype(BF16)
    ruled = jnp.concatenate([ruled, ruled], 0)

    step_rows = 2 * rows
    for segment in range(2):
        count = (depth + 1 + segment) * rows
        live = row < lengths_ref[segment]
        keys_wide = jnp.concatenate([keys_s[:count, :], extra_s[segment, :count, :]], 1)
        for pair in range(heads // 2):
            at = (segment * (heads // 2) + pair) * step_rows
            here = slice(at, at + step_rows)
            columns = [slice(h * width, (h + 1) * width) for h in (2 * pair, 2 * pair + 1)]
            query = jnp.concatenate([query_ref[segment, :, c] for c in columns], 0)
            cot = jnp.concatenate(
                [jnp.where(live, grad_ref[segment, :, c], jnp.zeros((), BF16)) for c in columns], 0
            )
            query_s[here, :] = query
            cot_s[here, :] = cot
            scores = lax.dot_general(
                keys_wide,
                jnp.concatenate([query, ruled], 1),
                NT,
                preferred_element_type=F32,
            )
            top = jnp.max(scores, axis=0, keepdims=True)
            weights = jnp.exp2((scores - top) * (scale * LOG2E))
            total = jnp.sum(weights, axis=0, keepdims=True)
            weights = weights * (1.0 / total)
            low_s[:count, here] = weights.astype(BF16)
            grad_weights = lax.dot_general(
                values_s[:count, :], cot, NT, preferred_element_type=F32
            )
            delta = jnp.sum(weights * grad_weights, axis=0, keepdims=True)
            grad_scores = (weights * (grad_weights - delta)).astype(BF16)
            ds_s[:count, here] = grad_scores
            grad_query = lax.dot_general(
                keys_t[:, :count], grad_scores, NN, preferred_element_type=F32
            )
            grad_query = (grad_query * scale).astype(BF16).T
            for n, c in enumerate(columns):
                grad_query_ref[segment, :, c] = grad_query[n * rows : (n + 1) * rows]

    inner = (depth + 1) * rows
    half = heads * rows
    grad_keys = lax.dot_general(ds_s[:inner, :], query_s[...], NN, preferred_element_type=F32)
    grad_keys = grad_keys * scale
    grad_values = lax.dot_general(low_s[:inner, :], cot_s[...], NN, preferred_element_type=F32)
    leaf_keys = lax.dot_general(
        ds_s[inner:, half:], query_s[half:, :], NN, preferred_element_type=F32
    )
    leaf_values = lax.dot_general(
        low_s[inner:, half:], cot_s[half:, :], NN, preferred_element_type=F32
    )
    leaf_ref[0:rows, :] = (leaf_keys * scale).astype(BF16)
    leaf_ref[rows : 2 * rows, :] = leaf_values.astype(BF16)

    def put(ref, levels_at):
        for place, level in enumerate(levels_at):
            span = slice(level * rows, (level + 1) * rows)
            at = place * 2 * rows
            ref[at : at + rows, :] = grad_keys[span].astype(ref.dtype)
            ref[at + rows : at + 2 * rows, :] = grad_values[span].astype(ref.dtype)

    @pl.when(parity == 1)
    def _():
        put(swap_ref, range(depth))
        put(part_ref, [depth])

    @pl.when(parity == 0)
    def _():
        put(swap_ref, [depth])
        put(part_ref, range(depth))


def main_call(lengths, queries, grads, keys, values, own, mate, near, far, depth):
    rows, width = keys.shape[1:]
    heads = queries.shape[2] // width
    slots = (depth + 2) * rows
    total = 2 * heads * rows
    vmem = pl.BlockSpec(memory_space=pltpu.VMEM)
    return pl.pallas_call(
        functools.partial(main_kernel, depth, heads),
        out_shape=(
            jax.ShapeDtypeStruct(queries.shape, BF16),
            jax.ShapeDtypeStruct((2 * rows, width), BF16),
            jax.ShapeDtypeStruct((depth * 2 * rows, width), BF16),
            jax.ShapeDtypeStruct((depth * 2 * rows, width), F32),
        ),
        in_specs=[pl.BlockSpec(memory_space=pltpu.SMEM)] + [vmem] * (6 + len(near) + len(far)),
        out_specs=(vmem,) * 4,
        scratch_shapes=[
            pltpu.VMEM((slots, width), BF16),
            pltpu.VMEM((slots, width), BF16),
            pltpu.VMEM((2, slots, width), BF16),
            pltpu.VMEM((width, slots), BF16),
            pltpu.VMEM((slots, total), BF16),
            pltpu.VMEM((slots, total), BF16),
            pltpu.VMEM((total, width), BF16),
            pltpu.VMEM((total, width), BF16),
        ],
        compiler_params=limit(24),
        name="attend",
    )(lengths, queries, grads, keys, values, own, mate, *near, *far)


def combine_kernel(depth, part_ref, other_ref, own_ref, *rest):
    sends, both = rest[:-1], rest[-1]
    block = own_ref.shape[0]
    index = lax.axis_index("leaf")
    both[...] = part_ref[...] + other_ref[...].astype(F32)

    def take(level):
        return both[pl.ds(pl.multiple_of(level * block, block), block), :]

    own_level = depth - trailing_zeros(index, depth)
    own_ref[...] = take(jnp.where(index & 1 == 1, 0, own_level))
    for mask, ref in enumerate(sends, 1):
        target = (index - (index & 1)) ^ (mask << 1)
        ref[...] = take(depth - trailing_zeros(target, depth)).astype(BF16)


def combine_call(part, other, depth):
    masks = (1 << (depth - 1)) - 1
    block = part.shape[0] // depth
    width = part.shape[1]
    vmem = pl.BlockSpec(memory_space=pltpu.VMEM)
    return pl.pallas_call(
        functools.partial(combine_kernel, depth),
        out_shape=[jax.ShapeDtypeStruct((block, width), F32)]
        + [jax.ShapeDtypeStruct((block, width), BF16)] * masks,
        in_specs=[vmem] * 2,
        out_specs=[vmem] * (1 + masks),
        scratch_shapes=[pltpu.VMEM(part.shape, F32)],
        compiler_params=limit(4),
        name="combine",
    )(part, other)


def final_kernel(depth, leaf_ref, own_ref, *refs):
    arrived, (keys_ref, values_ref) = refs[:-2], refs[-2:]
    rows = keys_ref.shape[1]
    index = lax.axis_index("leaf")
    parity = index & 1
    level = depth - trailing_zeros(index, depth)
    total = own_ref[...]
    for mask, ref in enumerate(arrived, 1):
        mine = (parity == 0) & (owner_at(index ^ (mask << 1), level, depth) == index)
        total = total + jnp.where(mine, ref[...].astype(F32), 0.0)
    total = total.astype(BF16)
    keys_ref[0] = total[:rows]
    values_ref[0] = total[rows:]
    keys_ref[1] = leaf_ref[:rows, :]
    values_ref[1] = leaf_ref[rows:, :]


def final_call(leaf, own, arrived, shape, depth):
    vmem = pl.BlockSpec(memory_space=pltpu.VMEM)
    return pl.pallas_call(
        functools.partial(final_kernel, depth),
        out_shape=[jax.ShapeDtypeStruct(shape, BF16)] * 2,
        in_specs=[vmem] * (2 + len(arrived)),
        out_specs=[vmem] * 2,
        compiler_params=limit(2),
        name="final",
    )(leaf, own, *arrived)


def body(queries, key_states, value_states, grad_output, lengths):
    count = lax.axis_size("leaf")
    depth = depth_of(count)
    masks = range(1, count // 2)
    swap_pairs = [(i, i ^ 1) for i in range(count)]

    pack = make_pack(lengths, key_states, value_states)
    near = [lax.ppermute(pack, "leaf", chip_pairs(m, count)) for m in masks]
    mate = lax.ppermute(pack, "leaf", swap_pairs)
    far = [lax.ppermute(block, "leaf", swap_pairs) for block in near]
    grad_queries, leaf, swap, part = main_call(
        lengths, queries, grad_output, key_states, value_states, pack, mate, near, far, depth
    )
    other = lax.ppermute(swap, "leaf", swap_pairs)
    own, *sends = combine_call(part, other, depth)
    arrived = [
        lax.ppermute(block, "leaf", chip_pairs(m, count))
        for m, block in zip(masks, sends)
    ]
    grad_keys, grad_values = final_call(leaf, own, arrived, key_states.shape, depth)
    return grad_queries, grad_keys, grad_values


def solution(mesh):
    segments = P(("dp", "leaf"), None, None)
    return jax.shard_map(
        body,
        mesh=mesh,
        in_specs=(segments, segments, segments, segments, P(("dp", "leaf"))),
        out_specs=(segments, segments, segments),
        check_vma=False,
    )
```

```python
import functools

import jax
import jax.numpy as jnp
from jax import lax
from jax.experimental import pallas as pl
from jax.experimental.pallas import tpu as pltpu
from jax.sharding import PartitionSpec as P

BF16 = jnp.bfloat16
F32 = jnp.float32
TAIL = 16
BIG = -1e30
LOG2E = 1.4426950408889634
NT = (((1,), (1,)), ((), ()))
NN = (((1,), (0,)), ((), ()))


def depth_of(count):
    return count.bit_length() - 1


def trailing_zeros(index, depth):
    total = jnp.zeros((), jnp.int32)
    for bit in range(depth):
        total = total + jnp.where((index & ((2 << bit) - 1)) == 0, 1, 0)
    return total


def owner_of(index, level, depth):
    if level == 0:
        return index * 0
    shift = depth - level + 1
    return ((index >> shift) << shift) + (1 << (depth - level))


def owner_at(index, level, depth):
    owner = owner_of(index, 0, depth)
    for place in range(1, depth + 1):
        owner = jnp.where(level == place, owner_of(index, place, depth), owner)
    return owner


def chip_pairs(mask, count):
    return [(i, i ^ (mask << 1)) for i in range(count)]


def limit(mib):
    return pltpu.CompilerParams(vmem_limit_bytes=mib * 1024 * 1024)


def pack_kernel(lengths_ref, key_ref, value_ref, pack_ref):
    rows = key_ref.shape[1]
    pack_ref[0:rows, :] = key_ref[0]
    pack_ref[rows : 2 * rows, :] = value_ref[0]
    length = lengths_ref[0].astype(F32)
    pack_ref[2 * rows :, :] = jnp.full((TAIL, pack_ref.shape[1]), length, F32).astype(BF16)


def make_pack(lengths, keys, values):
    rows, width = keys.shape[1:]
    first = pl.BlockSpec((1, rows, width), lambda step: (0, 0, 0))
    return pl.pallas_call(
        pack_kernel,
        grid=(1,),
        out_shape=jax.ShapeDtypeStruct((2 * rows + TAIL, width), BF16),
        in_specs=[pl.BlockSpec(memory_space=pltpu.SMEM), first, first],
        out_specs=pl.BlockSpec((2 * rows + TAIL, width), lambda step: (0, 0)),
        name="pack",
    )(lengths, keys, values)


def rows_kernel(heads, lengths_ref, query_ref, grad_ref, query_s, cot_s):
    rows = query_ref.shape[1]
    width = query_ref.shape[2] // heads
    row = lax.broadcasted_iota(jnp.int32, (rows, width), 0)
    for segment in range(2):
        live = row < lengths_ref[segment]
        for head in range(heads):
            here = pl.ds((segment * heads + head) * rows, rows)
            columns = slice(head * width, (head + 1) * width)
            query_s[here, :] = query_ref[segment, :, columns]
            cot = grad_ref[segment, :, columns]
            cot_s[here, :] = jnp.where(live, cot, jnp.zeros((), BF16))


def rows_call(lengths, queries, grads, width):
    heads = queries.shape[2] // width
    rows = queries.shape[1]
    vmem = pl.BlockSpec(memory_space=pltpu.VMEM)
    shape = jax.ShapeDtypeStruct((2 * heads * rows, width), BF16)
    return pl.pallas_call(
        functools.partial(rows_kernel, heads),
        out_shape=(shape, shape),
        in_specs=[pl.BlockSpec(memory_space=pltpu.SMEM), vmem, vmem],
        out_specs=(vmem, vmem),
        compiler_params=limit(8),
        cost_estimate=pl.CostEstimate(flops=0, bytes_accessed=4 << 20, transcendentals=0),
        name="rows",
    )(lengths, queries, grads)


def main_kernel(depth, heads, *refs):
    masks = (1 << (depth - 1)) - 1
    lengths_ref, query_s, cot_s, key_ref, value_ref, own_ref, mate_ref = refs[:7]
    near = refs[7 : 7 + masks]
    far = refs[7 + masks : 7 + 2 * masks]
    (
        grad_query_ref,
        leaf_ref,
        swap_ref,
        part_ref,
        keys_s,
        values_s,
        extra_s,
        keys_t,
        low_s,
        ds_s,
    ) = refs[7 + 2 * masks :]
    rows, width = key_ref.shape[1:]
    index = lax.axis_index("leaf")
    parity = index & 1
    own_level = depth - trailing_zeros(index, depth)
    scale = width ** (-0.5)
    lane = lax.broadcasted_iota(jnp.int32, (rows, width), 1)
    row = lax.broadcasted_iota(jnp.int32, (rows, width), 0)
    row_f = row.astype(F32)

    levels = depth + 2
    for level in range(levels):
        span = slice(level * rows, (level + 1) * rows)
        if level == depth + 1:
            key_block, value_block = key_ref[1], value_ref[1]
            length = jnp.full((1, width), lengths_ref[1].astype(F32), F32)
        else:
            if level == depth:
                block = jnp.where(parity == 1, own_ref[...], mate_ref[...])
            else:
                even = index - parity
                pick = (even ^ owner_of(even, level, depth)) >> 1
                block = jnp.where(parity == 1, mate_ref[...], own_ref[...])
                for mask in range(1, masks + 1):
                    other = jnp.where(parity == 1, far[mask - 1][...], near[mask - 1][...])
                    block = jnp.where(pick == mask, other, block)
            key_block, value_block = block[:rows], block[rows : 2 * rows]
            length = block[2 * rows : 2 * rows + 1].astype(F32)
        keys_s[span, :] = key_block
        values_s[span, :] = value_block
        keys_t[:, span] = key_block.T
        dead = row_f >= length
        for segment in range(2):
            if segment == 0 and level == depth + 1:
                continue
            level_of = own_level if segment == 0 else depth + 1
            diagonal = jnp.where(row > 0, row, -1)
            column = jnp.where(level == level_of, diagonal, -1)
            column = jnp.where(dead | (level > level_of), 0, column)
            extra_s[segment, span, :] = jnp.where(lane == column, 1.0, 0.0).astype(BF16)

    ruled = jnp.where((lane > row) | (lane == 0), BIG, 0.0).astype(BF16)
    ruled = jnp.concatenate([ruled, ruled], 0)

    step_rows = 2 * rows
    for segment in range(2):
        count = (depth + 1 + segment) * rows
        keys_wide = jnp.concatenate([keys_s[:count, :], extra_s[segment, :count, :]], 1)
        for pair in range(heads // 2):
            at = (segment * (heads // 2) + pair) * step_rows
            here = slice(at, at + step_rows)
            columns = [slice(h * width, (h + 1) * width) for h in (2 * pair, 2 * pair + 1)]
            query, cot = query_s[here, :], cot_s[here, :]
            scores = lax.dot_general(
                keys_wide,
                jnp.concatenate([query, ruled], 1),
                NT,
                preferred_element_type=F32,
            )
            top = jnp.max(scores, axis=0, keepdims=True)
            weights = jnp.exp2((scores - top) * (scale * LOG2E))
            total = jnp.sum(weights, axis=0, keepdims=True)
            weights = weights * (1.0 / total)
            low_s[:count, here] = weights.astype(BF16)
            grad_weights = lax.dot_general(
                values_s[:count, :], cot, NT, preferred_element_type=F32
            )
            delta = jnp.sum(weights * grad_weights, axis=0, keepdims=True)
            grad_scores = (weights * (grad_weights - delta)).astype(BF16)
            ds_s[:count, here] = grad_scores
            grad_query = lax.dot_general(
                keys_t[:, :count], grad_scores, NN, preferred_element_type=F32
            )
            grad_query = (grad_query * scale).astype(BF16).T
            for n, c in enumerate(columns):
                grad_query_ref[segment, :, c] = grad_query[n * rows : (n + 1) * rows]

    inner = (depth + 1) * rows
    half = heads * rows
    grad_keys = lax.dot_general(ds_s[:inner, :], query_s[...], NN, preferred_element_type=F32)
    grad_keys = grad_keys * scale
    grad_values = lax.dot_general(low_s[:inner, :], cot_s[...], NN, preferred_element_type=F32)
    leaf_keys = lax.dot_general(
        ds_s[inner:, half:], query_s[half:, :], NN, preferred_element_type=F32
    )
    leaf_values = lax.dot_general(
        low_s[inner:, half:], cot_s[half:, :], NN, preferred_element_type=F32
    )
    leaf_ref[0:rows, :] = (leaf_keys * scale).astype(BF16)
    leaf_ref[rows : 2 * rows, :] = leaf_values.astype(BF16)

    def put(ref, levels_at):
        for place, level in enumerate(levels_at):
            span = slice(level * rows, (level + 1) * rows)
            at = place * 2 * rows
            ref[at : at + rows, :] = grad_keys[span].astype(ref.dtype)
            ref[at + rows : at + 2 * rows, :] = grad_values[span].astype(ref.dtype)

    @pl.when(parity == 1)
    def _():
        put(swap_ref, range(depth))
        put(part_ref, [depth])

    @pl.when(parity == 0)
    def _():
        put(swap_ref, [depth])
        put(part_ref, range(depth))


def main_call(lengths, queries, cot, keys, values, own, mate, near, far, depth):
    rows, width = keys.shape[1:]
    heads = queries.shape[0] // (2 * rows)
    slots = (depth + 2) * rows
    total = 2 * heads * rows
    vmem = pl.BlockSpec(memory_space=pltpu.VMEM)
    return pl.pallas_call(
        functools.partial(main_kernel, depth, heads),
        out_shape=(
            jax.ShapeDtypeStruct((2, rows, heads * width), BF16),
            jax.ShapeDtypeStruct((2 * rows, width), BF16),
            jax.ShapeDtypeStruct((depth * 2 * rows, width), BF16),
            jax.ShapeDtypeStruct((depth * 2 * rows, width), F32),
        ),
        in_specs=[pl.BlockSpec(memory_space=pltpu.SMEM)] + [vmem] * (6 + len(near) + len(far)),
        out_specs=(vmem,) * 4,
        scratch_shapes=[
            pltpu.VMEM((slots, width), BF16),
            pltpu.VMEM((slots, width), BF16),
            pltpu.VMEM((2, slots, width), BF16),
            pltpu.VMEM((width, slots), BF16),
            pltpu.VMEM((slots, total), BF16),
            pltpu.VMEM((slots, total), BF16),
        ],
        compiler_params=limit(24),
        name="attend",
    )(lengths, queries, cot, keys, values, own, mate, *near, *far)


def combine_kernel(depth, part_ref, other_ref, own_ref, *rest):
    sends, both = rest[:-1], rest[-1]
    block = own_ref.shape[0]
    index = lax.axis_index("leaf")
    both[...] = part_ref[...] + other_ref[...].astype(F32)

    def take(level):
        return both[pl.ds(pl.multiple_of(level * block, block), block), :]

    own_level = depth - trailing_zeros(index, depth)
    own_ref[...] = take(jnp.where(index & 1 == 1, 0, own_level))
    for mask, ref in enumerate(sends, 1):
        target = (index - (index & 1)) ^ (mask << 1)
        ref[...] = take(depth - trailing_zeros(target, depth)).astype(BF16)


def combine_call(part, other, depth):
    masks = (1 << (depth - 1)) - 1
    block = part.shape[0] // depth
    width = part.shape[1]
    vmem = pl.BlockSpec(memory_space=pltpu.VMEM)
    return pl.pallas_call(
        functools.partial(combine_kernel, depth),
        out_shape=[jax.ShapeDtypeStruct((block, width), F32)]
        + [jax.ShapeDtypeStruct((block, width), BF16)] * masks,
        in_specs=[vmem] * 2,
        out_specs=[vmem] * (1 + masks),
        scratch_shapes=[pltpu.VMEM(part.shape, F32)],
        compiler_params=limit(4),
        name="combine",
    )(part, other)


def final_kernel(depth, leaf_ref, own_ref, *refs):
    arrived, (keys_ref, values_ref) = refs[:-2], refs[-2:]
    rows = keys_ref.shape[1]
    index = lax.axis_index("leaf")
    parity = index & 1
    level = depth - trailing_zeros(index, depth)
    total = own_ref[...]
    for mask, ref in enumerate(arrived, 1):
        mine = (parity == 0) & (owner_at(index ^ (mask << 1), level, depth) == index)
        total = total + jnp.where(mine, ref[...].astype(F32), 0.0)
    total = total.astype(BF16)
    keys_ref[0] = total[:rows]
    values_ref[0] = total[rows:]
    keys_ref[1] = leaf_ref[:rows, :]
    values_ref[1] = leaf_ref[rows:, :]


def final_call(leaf, own, arrived, shape, depth):
    vmem = pl.BlockSpec(memory_space=pltpu.VMEM)
    return pl.pallas_call(
        functools.partial(final_kernel, depth),
        out_shape=[jax.ShapeDtypeStruct(shape, BF16)] * 2,
        in_specs=[vmem] * (2 + len(arrived)),
        out_specs=[vmem] * 2,
        compiler_params=limit(2),
        name="final",
    )(leaf, own, *arrived)


def body(queries, key_states, value_states, grad_output, lengths):
    count = lax.axis_size("leaf")
    depth = depth_of(count)
    masks = range(1, count // 2)
    swap_pairs = [(i, i ^ 1) for i in range(count)]

    pack = make_pack(lengths, key_states, value_states)
    near = [lax.ppermute(pack, "leaf", chip_pairs(m, count)) for m in masks]
    mate = lax.ppermute(pack, "leaf", swap_pairs)
    query_rows, cot = rows_call(lengths, queries, grad_output, key_states.shape[2])
    near, query_rows, cot = lax.optimization_barrier((near, query_rows, cot))
    far = [lax.ppermute(block, "leaf", swap_pairs) for block in near]
    grad_queries, leaf, swap, part = main_call(
        lengths, query_rows, cot, key_states, value_states, pack, mate, near, far, depth
    )
    other = lax.ppermute(swap, "leaf", swap_pairs)
    own, *sends = combine_call(part, other, depth)
    arrived = [
        lax.ppermute(block, "leaf", chip_pairs(m, count))
        for m, block in zip(masks, sends)
    ]
    grad_keys, grad_values = final_call(leaf, own, arrived, key_states.shape, depth)
    return grad_queries, grad_keys, grad_values


def solution(mesh):
    segments = P(("dp", "leaf"), None, None)
    return jax.shard_map(
        body,
        mesh=mesh,
        in_specs=(segments, segments, segments, segments, P(("dp", "leaf"))),
        out_specs=(segments, segments, segments),
        check_vma=False,
    )
```

```python
import functools

import jax
import jax.numpy as jnp
from jax import lax
from jax.experimental import pallas as pl
from jax.experimental.pallas import tpu as pltpu
from jax.sharding import PartitionSpec as P

BF16 = jnp.bfloat16
F32 = jnp.float32
TAIL = 16
BIG = -1e30
LOG2E = 1.4426950408889634
NT = (((1,), (1,)), ((), ()))
NN = (((1,), (0,)), ((), ()))


def depth_of(count):
    return count.bit_length() - 1


def trailing_zeros(index, depth):
    total = jnp.zeros((), jnp.int32)
    for bit in range(depth):
        total = total + jnp.where((index & ((2 << bit) - 1)) == 0, 1, 0)
    return total


def owner_of(index, level, depth):
    if level == 0:
        return index * 0
    shift = depth - level + 1
    return ((index >> shift) << shift) + (1 << (depth - level))


def owner_at(index, level, depth):
    owner = owner_of(index, 0, depth)
    for place in range(1, depth + 1):
        owner = jnp.where(level == place, owner_of(index, place, depth), owner)
    return owner


def chip_pairs(mask, count):
    return [(i, i if i & 1 else i ^ (mask << 1)) for i in range(count)]


def limit(mib):
    return pltpu.CompilerParams(vmem_limit_bytes=mib * 1024 * 1024)


def pack_kernel(lengths_ref, key_ref, value_ref, pack_ref):
    rows = key_ref.shape[1]
    pack_ref[0:rows, :] = key_ref[0]
    pack_ref[rows : 2 * rows, :] = value_ref[0]
    length = lengths_ref[0].astype(F32)
    pack_ref[2 * rows :, :] = jnp.full((TAIL, pack_ref.shape[1]), length, F32).astype(BF16)


def make_pack(lengths, keys, values):
    rows, width = keys.shape[1:]
    first = pl.BlockSpec((1, rows, width), lambda step: (0, 0, 0))
    return pl.pallas_call(
        pack_kernel,
        grid=(1,),
        out_shape=jax.ShapeDtypeStruct((2 * rows + TAIL, width), BF16),
        in_specs=[pl.BlockSpec(memory_space=pltpu.SMEM), first, first],
        out_specs=pl.BlockSpec((2 * rows + TAIL, width), lambda step: (0, 0)),
        name="pack",
    )(lengths, keys, values)


def rows_kernel(heads, lengths_ref, query_ref, grad_ref, query_s, cot_s):
    rows = query_ref.shape[1]
    width = query_ref.shape[2] // heads
    row = lax.broadcasted_iota(jnp.int32, (rows, width), 0)
    for segment in range(2):
        live = row < lengths_ref[segment]
        for head in range(heads):
            here = pl.ds((segment * heads + head) * rows, rows)
            columns = slice(head * width, (head + 1) * width)
            query_s[here, :] = query_ref[segment, :, columns]
            cot = grad_ref[segment, :, columns]
            cot_s[here, :] = jnp.where(live, cot, jnp.zeros((), BF16))


def rows_call(lengths, queries, grads, width):
    heads = queries.shape[2] // width
    rows = queries.shape[1]
    vmem = pl.BlockSpec(memory_space=pltpu.VMEM)
    shape = jax.ShapeDtypeStruct((2 * heads * rows, width), BF16)
    return pl.pallas_call(
        functools.partial(rows_kernel, heads),
        out_shape=(shape, shape),
        in_specs=[pl.BlockSpec(memory_space=pltpu.SMEM), vmem, vmem],
        out_specs=(vmem, vmem),
        compiler_params=limit(8),
        cost_estimate=pl.CostEstimate(flops=0, bytes_accessed=4 << 20, transcendentals=0),
        name="rows",
    )(lengths, queries, grads)


def main_kernel(depth, heads, *refs):
    masks = (1 << (depth - 1)) - 1
    lengths_ref, query_s, cot_s, key_ref, value_ref, own_ref, mate_ref = refs[:7]
    near = refs[7 : 7 + masks]
    far = refs[7 + masks : 7 + 2 * masks]
    (
        grad_query_ref,
        leaf_ref,
        swap_ref,
        part_ref,
        keys_s,
        values_s,
        extra_s,
        keys_t,
        low_s,
        ds_s,
    ) = refs[7 + 2 * masks :]
    rows, width = key_ref.shape[1:]
    index = lax.axis_index("leaf")
    parity = index & 1
    own_level = depth - trailing_zeros(index, depth)
    scale = width ** (-0.5)
    lane = lax.broadcasted_iota(jnp.int32, (rows, width), 1)
    row = lax.broadcasted_iota(jnp.int32, (rows, width), 0)
    row_f = row.astype(F32)

    levels = depth + 2
    for level in range(levels):
        span = slice(level * rows, (level + 1) * rows)
        if level == depth + 1:
            key_block, value_block = key_ref[1], value_ref[1]
            length = jnp.full((1, width), lengths_ref[1].astype(F32), F32)
        else:
            if level == depth:
                block = jnp.where(parity == 1, own_ref[...], mate_ref[...])
            else:
                even = index - parity
                pick = (even ^ owner_of(even, level, depth)) >> 1
                block = jnp.where(parity == 1, mate_ref[...], own_ref[...])
                for mask in range(1, masks + 1):
                    other = jnp.where(parity == 1, far[mask - 1][...], near[mask - 1][...])
                    block = jnp.where(pick == mask, other, block)
            key_block, value_block = block[:rows], block[rows : 2 * rows]
            length = block[2 * rows : 2 * rows + 1].astype(F32)
        keys_s[span, :] = key_block
        values_s[span, :] = value_block
        keys_t[:, span] = key_block.T
        dead = row_f >= length
        for segment in range(2):
            if segment == 0 and level == depth + 1:
                continue
            level_of = own_level if segment == 0 else depth + 1
            diagonal = jnp.where(row > 0, row, -1)
            column = jnp.where(level == level_of, diagonal, -1)
            column = jnp.where(dead | (level > level_of), 0, column)
            extra_s[segment, span, :] = jnp.where(lane == column, 1.0, 0.0).astype(BF16)

    ruled = jnp.where((lane > row) | (lane == 0), BIG, 0.0).astype(BF16)
    ruled = jnp.concatenate([ruled, ruled], 0)

    step_rows = 2 * rows
    for segment in range(2):
        count = (depth + 1 + segment) * rows
        keys_wide = jnp.concatenate([keys_s[:count, :], extra_s[segment, :count, :]], 1)
        for pair in range(heads // 2):
            at = (segment * (heads // 2) + pair) * step_rows
            here = slice(at, at + step_rows)
            columns = [slice(h * width, (h + 1) * width) for h in (2 * pair, 2 * pair + 1)]
            query, cot = query_s[here, :], cot_s[here, :]
            scores = lax.dot_general(
                keys_wide,
                jnp.concatenate([query, ruled], 1),
                NT,
                preferred_element_type=F32,
            )
            top = jnp.max(scores, axis=0, keepdims=True)
            weights = jnp.exp2((scores - top) * (scale * LOG2E))
            total = jnp.sum(weights, axis=0, keepdims=True)
            weights = weights * (1.0 / total)
            low_s[:count, here] = weights.astype(BF16)
            grad_weights = lax.dot_general(
                values_s[:count, :], cot, NT, preferred_element_type=F32
            )
            delta = jnp.sum(weights * grad_weights, axis=0, keepdims=True)
            grad_scores = (weights * (grad_weights - delta)).astype(BF16)
            ds_s[:count, here] = grad_scores
            grad_query = lax.dot_general(
                keys_t[:, :count], grad_scores, NN, preferred_element_type=F32
            )
            grad_query = (grad_query * scale).astype(BF16).T
            for n, c in enumerate(columns):
                grad_query_ref[segment, :, c] = grad_query[n * rows : (n + 1) * rows]

    inner = (depth + 1) * rows
    half = heads * rows
    grad_keys = lax.dot_general(ds_s[:inner, :], query_s[...], NN, preferred_element_type=F32)
    grad_keys = grad_keys * scale
    grad_values = lax.dot_general(low_s[:inner, :], cot_s[...], NN, preferred_element_type=F32)
    leaf_keys = lax.dot_general(
        ds_s[inner:, half:], query_s[half:, :], NN, preferred_element_type=F32
    )
    leaf_values = lax.dot_general(
        low_s[inner:, half:], cot_s[half:, :], NN, preferred_element_type=F32
    )
    leaf_ref[0:rows, :] = (leaf_keys * scale).astype(BF16)
    leaf_ref[rows : 2 * rows, :] = leaf_values.astype(BF16)

    def put(ref, levels_at):
        for place, level in enumerate(levels_at):
            span = slice(level * rows, (level + 1) * rows)
            at = place * 2 * rows
            ref[at : at + rows, :] = grad_keys[span].astype(ref.dtype)
            ref[at + rows : at + 2 * rows, :] = grad_values[span].astype(ref.dtype)

    @pl.when(parity == 1)
    def _():
        put(swap_ref, range(depth))
        put(part_ref, [depth])

    @pl.when(parity == 0)
    def _():
        put(swap_ref, [depth])
        put(part_ref, range(depth))


def main_call(lengths, queries, cot, keys, values, own, mate, near, far, depth):
    rows, width = keys.shape[1:]
    heads = queries.shape[0] // (2 * rows)
    slots = (depth + 2) * rows
    total = 2 * heads * rows
    vmem = pl.BlockSpec(memory_space=pltpu.VMEM)
    return pl.pallas_call(
        functools.partial(main_kernel, depth, heads),
        out_shape=(
            jax.ShapeDtypeStruct((2, rows, heads * width), BF16),
            jax.ShapeDtypeStruct((2 * rows, width), BF16),
            jax.ShapeDtypeStruct((depth * 2 * rows, width), BF16),
            jax.ShapeDtypeStruct((depth * 2 * rows, width), F32),
        ),
        in_specs=[pl.BlockSpec(memory_space=pltpu.SMEM)] + [vmem] * (6 + len(near) + len(far)),
        out_specs=(vmem,) * 4,
        scratch_shapes=[
            pltpu.VMEM((slots, width), BF16),
            pltpu.VMEM((slots, width), BF16),
            pltpu.VMEM((2, slots, width), BF16),
            pltpu.VMEM((width, slots), BF16),
            pltpu.VMEM((slots, total), BF16),
            pltpu.VMEM((slots, total), BF16),
        ],
        compiler_params=limit(24),
        name="attend",
    )(lengths, queries, cot, keys, values, own, mate, *near, *far)


def combine_kernel(depth, part_ref, other_ref, own_ref, *rest):
    sends, both = rest[:-1], rest[-1]
    block = own_ref.shape[0]
    index = lax.axis_index("leaf")
    both[...] = part_ref[...] + other_ref[...].astype(F32)

    def take(level):
        return both[pl.ds(pl.multiple_of(level * block, block), block), :]

    own_level = depth - trailing_zeros(index, depth)
    own_ref[...] = take(jnp.where(index & 1 == 1, 0, own_level))
    for mask, ref in enumerate(sends, 1):
        target = (index - (index & 1)) ^ (mask << 1)
        ref[...] = take(depth - trailing_zeros(target, depth)).astype(BF16)


def combine_call(part, other, depth):
    masks = (1 << (depth - 1)) - 1
    block = part.shape[0] // depth
    width = part.shape[1]
    vmem = pl.BlockSpec(memory_space=pltpu.VMEM)
    return pl.pallas_call(
        functools.partial(combine_kernel, depth),
        out_shape=[jax.ShapeDtypeStruct((block, width), F32)]
        + [jax.ShapeDtypeStruct((block, width), BF16)] * masks,
        in_specs=[vmem] * 2,
        out_specs=[vmem] * (1 + masks),
        scratch_shapes=[pltpu.VMEM(part.shape, F32)],
        compiler_params=limit(4),
        name="combine",
    )(part, other)


def final_kernel(depth, leaf_ref, own_ref, *refs):
    arrived, (keys_ref, values_ref) = refs[:-2], refs[-2:]
    rows = keys_ref.shape[1]
    index = lax.axis_index("leaf")
    parity = index & 1
    level = depth - trailing_zeros(index, depth)
    total = own_ref[...]
    for mask, ref in enumerate(arrived, 1):
        mine = (parity == 0) & (owner_at(index ^ (mask << 1), level, depth) == index)
        total = total + jnp.where(mine, ref[...].astype(F32), 0.0)
    total = total.astype(BF16)
    keys_ref[0] = total[:rows]
    values_ref[0] = total[rows:]
    keys_ref[1] = leaf_ref[:rows, :]
    values_ref[1] = leaf_ref[rows:, :]


def final_call(leaf, own, arrived, shape, depth):
    vmem = pl.BlockSpec(memory_space=pltpu.VMEM)
    return pl.pallas_call(
        functools.partial(final_kernel, depth),
        out_shape=[jax.ShapeDtypeStruct(shape, BF16)] * 2,
        in_specs=[vmem] * (2 + len(arrived)),
        out_specs=[vmem] * 2,
        compiler_params=limit(2),
        name="final",
    )(leaf, own, *arrived)


def body(queries, key_states, value_states, grad_output, lengths):
    count = lax.axis_size("leaf")
    depth = depth_of(count)
    masks = range(1, count // 2)
    swap_pairs = [(i, i ^ 1) for i in range(count)]

    pack = make_pack(lengths, key_states, value_states)
    near = [lax.ppermute(pack, "leaf", chip_pairs(m, count)) for m in masks]
    mate = lax.ppermute(pack, "leaf", swap_pairs)
    query_rows, cot = rows_call(lengths, queries, grad_output, key_states.shape[2])
    near, query_rows, cot = lax.optimization_barrier((near, query_rows, cot))
    far = [lax.ppermute(block, "leaf", swap_pairs) for block in near]
    grad_queries, leaf, swap, part = main_call(
        lengths, query_rows, cot, key_states, value_states, pack, mate, near, far, depth
    )
    other = lax.ppermute(swap, "leaf", swap_pairs)
    own, *sends = combine_call(part, other, depth)
    arrived = [
        lax.ppermute(block, "leaf", chip_pairs(m, count))
        for m, block in zip(masks, sends)
    ]
    grad_keys, grad_values = final_call(leaf, own, arrived, key_states.shape, depth)
    return grad_queries, grad_keys, grad_values


def solution(mesh):
    segments = P(("dp", "leaf"), None, None)
    return jax.shard_map(
        body,
        mesh=mesh,
        in_specs=(segments, segments, segments, segments, P(("dp", "leaf"))),
        out_specs=(segments, segments, segments),
        check_vma=False,
    )
```

```python
import functools

import jax
import jax.numpy as jnp
from jax import lax
from jax.experimental import pallas as pl
from jax.experimental.pallas import tpu as pltpu
from jax.sharding import PartitionSpec as P

BF16 = jnp.bfloat16
F32 = jnp.float32
TAIL = 16
BIG = -1e30
LOG2E = 1.4426950408889634
NT = (((1,), (1,)), ((), ()))
NN = (((1,), (0,)), ((), ()))


def depth_of(count):
    return count.bit_length() - 1


def trailing_zeros(index, depth):
    total = jnp.zeros((), jnp.int32)
    for bit in range(depth):
        total = total + jnp.where((index & ((2 << bit) - 1)) == 0, 1, 0)
    return total


def owner_of(index, level, depth):
    if level == 0:
        return index * 0
    shift = depth - level + 1
    return ((index >> shift) << shift) + (1 << (depth - level))


def owner_at(index, level, depth):
    owner = owner_of(index, 0, depth)
    for place in range(1, depth + 1):
        owner = jnp.where(level == place, owner_of(index, place, depth), owner)
    return owner


def limit(mib):
    return pltpu.CompilerParams(vmem_limit_bytes=mib * 1024 * 1024)


def pack_kernel(lengths_ref, key_ref, value_ref, pack_ref, length_s, tail_s, sems):
    rows = key_ref.shape[1]
    copies = [
        pltpu.make_async_copy(lengths_ref, length_s, sems.at[0]),
        pltpu.make_async_copy(key_ref.at[0], pack_ref.at[pl.ds(0, rows)], sems.at[1]),
        pltpu.make_async_copy(value_ref.at[0], pack_ref.at[pl.ds(rows, rows)], sems.at[2]),
    ]
    for copy in copies:
        copy.start()
    copies[0].wait()
    tail_s[...] = jnp.full(tail_s.shape, length_s[0].astype(F32), F32).astype(BF16)
    last = pltpu.make_async_copy(tail_s, pack_ref.at[pl.ds(2 * rows, TAIL)], sems.at[3])
    last.start()
    for copy in copies[1:] + [last]:
        copy.wait()


def make_pack(lengths, keys, values):
    rows, width = keys.shape[1:]
    hbm = pl.BlockSpec(memory_space=pltpu.HBM)
    return pl.pallas_call(
        pack_kernel,
        out_shape=jax.ShapeDtypeStruct((2 * rows + TAIL, width), BF16),
        in_specs=[hbm, hbm, hbm],
        out_specs=hbm,
        scratch_shapes=[
            pltpu.SMEM((2,), jnp.int32),
            pltpu.VMEM((TAIL, width), BF16),
            pltpu.SemaphoreType.DMA((4,)),
        ],
        name="pack",
    )(lengths, keys, values)


def pass_on_kernel(first, *refs):
    other_ref, arrived_ref, out_ref = refs
    index = lax.axis_index("leaf")
    core, x = index & 1, (index >> 1) & 1
    take = core == 1 if first else (core == 0) | (x == 1)
    out_ref[...] = jnp.where(take, arrived_ref[...], other_ref[...])


def pass_on(first, other, arrived):
    vmem = pl.BlockSpec(memory_space=pltpu.VMEM)
    return pl.pallas_call(
        functools.partial(pass_on_kernel, first),
        out_shape=jax.ShapeDtypeStruct(other.shape, other.dtype),
        in_specs=[vmem, vmem],
        out_specs=vmem,
        compiler_params=limit(1),
        name="pass_on",
    )(other, arrived)


def rows_kernel(heads, lengths_ref, query_ref, grad_ref, query_s, cot_s):
    rows = query_ref.shape[1]
    width = query_ref.shape[2] // heads
    row = lax.broadcasted_iota(jnp.int32, (rows, width), 0)
    for segment in range(2):
        live = row < lengths_ref[segment]
        for head in range(heads):
            here = pl.ds((segment * heads + head) * rows, rows)
            columns = slice(head * width, (head + 1) * width)
            query_s[here, :] = query_ref[segment, :, columns]
            cot = grad_ref[segment, :, columns]
            cot_s[here, :] = jnp.where(live, cot, jnp.zeros((), BF16))


def rows_call(lengths, queries, grads, width):
    heads = queries.shape[2] // width
    rows = queries.shape[1]
    vmem = pl.BlockSpec(memory_space=pltpu.VMEM)
    shape = jax.ShapeDtypeStruct((2 * heads * rows, width), BF16)
    return pl.pallas_call(
        functools.partial(rows_kernel, heads),
        out_shape=(shape, shape),
        in_specs=[pl.BlockSpec(memory_space=pltpu.SMEM), vmem, vmem],
        out_specs=(vmem, vmem),
        compiler_params=limit(8),
        cost_estimate=pl.CostEstimate(flops=0, bytes_accessed=4 << 20, transcendentals=0),
        name="rows",
    )(lengths, queries, grads)


def direct_path(depth, index, refs):
    masks = (1 << (depth - 1)) - 1
    own, mate = refs[0][...], refs[1][...]
    near, far = refs[2 : 2 + masks], refs[2 + masks :]
    odd = index & 1 == 1
    even = index - (index & 1)
    blocks = []
    for level in range(depth):
        pick = (even ^ owner_of(even, level, depth)) >> 1
        block = jnp.where(odd, mate, own)
        for mask in range(1, masks + 1):
            other = jnp.where(odd, far[mask - 1][...], near[mask - 1][...])
            block = jnp.where(pick == mask, other, block)
        blocks.append(block)
    return blocks + [jnp.where(odd, own, mate)]


def two_step_path(index, refs):
    own, mate, along_x, sent_on, swapped = [ref[...] for ref in refs]
    odd, x, y = index & 1 == 1, (index >> 1) & 1 == 1, (index >> 2) & 1 == 1
    even_own = jnp.where(odd, mate, own)
    odd_own = jnp.where(odd, own, mate)
    even_other = jnp.where(odd, swapped, along_x)
    odd_other = jnp.where(odd, sent_on, swapped)
    same = jnp.where(x, even_other, even_own)
    second = jnp.where(x, even_own, even_other)
    return [jnp.where(y, odd_other, same), jnp.where(y, same, odd_other), second, odd_own]


def main_kernel(depth, heads, sources, *refs):
    lengths_ref, query_s, cot_s, key_ref, value_ref = refs[:5]
    path_refs = refs[5 : 5 + sources]
    (
        grad_query_ref,
        leaf_ref,
        swap_ref,
        part_ref,
        keys_s,
        values_s,
        extra_s,
        keys_t,
        low_s,
        ds_s,
    ) = refs[5 + sources :]
    rows, width = key_ref.shape[1:]
    index = lax.axis_index("leaf")
    parity = index & 1
    own_level = depth - trailing_zeros(index, depth)
    scale = width ** (-0.5)
    lane = lax.broadcasted_iota(jnp.int32, (rows, width), 1)
    row = lax.broadcasted_iota(jnp.int32, (rows, width), 0)
    row_f = row.astype(F32)
    if depth == 3:
        path = two_step_path(index, path_refs)
    else:
        path = direct_path(depth, index, path_refs)

    levels = depth + 2
    for level in range(levels):
        span = slice(level * rows, (level + 1) * rows)
        if level == depth + 1:
            key_block, value_block = key_ref[1], value_ref[1]
            length = jnp.full((1, width), lengths_ref[1].astype(F32), F32)
        else:
            block = path[level]
            key_block, value_block = block[:rows], block[rows : 2 * rows]
            length = block[2 * rows : 2 * rows + 1].astype(F32)
        keys_s[span, :] = key_block
        values_s[span, :] = value_block
        keys_t[:, span] = key_block.T
        dead = row_f >= length
        for segment in range(2):
            if segment == 0 and level == depth + 1:
                continue
            level_of = own_level if segment == 0 else depth + 1
            diagonal = jnp.where(row > 0, row, -1)
            column = jnp.where(level == level_of, diagonal, -1)
            column = jnp.where(dead | (level > level_of), 0, column)
            extra_s[segment, span, :] = jnp.where(lane == column, 1.0, 0.0).astype(BF16)

    ruled = jnp.where((lane > row) | (lane == 0), BIG, 0.0).astype(BF16)
    ruled = jnp.concatenate([ruled, ruled], 0)

    step_rows = 2 * rows
    for segment in range(2):
        count = (depth + 1 + segment) * rows
        keys_wide = jnp.concatenate([keys_s[:count, :], extra_s[segment, :count, :]], 1)
        for pair in range(heads // 2):
            at = (segment * (heads // 2) + pair) * step_rows
            here = slice(at, at + step_rows)
            columns = [slice(h * width, (h + 1) * width) for h in (2 * pair, 2 * pair + 1)]
            query, cot = query_s[here, :], cot_s[here, :]
            scores = lax.dot_general(
                keys_wide,
                jnp.concatenate([query, ruled], 1),
                NT,
                preferred_element_type=F32,
            )
            top = jnp.max(scores, axis=0, keepdims=True)
            weights = jnp.exp2((scores - top) * (scale * LOG2E))
            total = jnp.sum(weights, axis=0, keepdims=True)
            weights = weights * (1.0 / total)
            low_s[:count, here] = weights.astype(BF16)
            grad_weights = lax.dot_general(
                values_s[:count, :], cot, NT, preferred_element_type=F32
            )
            delta = jnp.sum(weights * grad_weights, axis=0, keepdims=True)
            grad_scores = (weights * (grad_weights - delta)).astype(BF16)
            ds_s[:count, here] = grad_scores
            grad_query = lax.dot_general(
                keys_t[:, :count], grad_scores, NN, preferred_element_type=F32
            )
            grad_query = (grad_query * scale).astype(BF16).T
            for n, c in enumerate(columns):
                grad_query_ref[segment, :, c] = grad_query[n * rows : (n + 1) * rows]

    inner = (depth + 1) * rows
    half = heads * rows
    grad_keys = lax.dot_general(ds_s[:inner, :], query_s[...], NN, preferred_element_type=F32)
    grad_keys = grad_keys * scale
    grad_values = lax.dot_general(low_s[:inner, :], cot_s[...], NN, preferred_element_type=F32)
    leaf_keys = lax.dot_general(
        ds_s[inner:, half:], query_s[half:, :], NN, preferred_element_type=F32
    )
    leaf_values = lax.dot_general(
        low_s[inner:, half:], cot_s[half:, :], NN, preferred_element_type=F32
    )
    leaf_ref[0:rows, :] = (leaf_keys * scale).astype(BF16)
    leaf_ref[rows : 2 * rows, :] = leaf_values.astype(BF16)

    def put(ref, levels_at):
        for place, level in enumerate(levels_at):
            span = slice(level * rows, (level + 1) * rows)
            at = place * 2 * rows
            ref[at : at + rows, :] = grad_keys[span].astype(ref.dtype)
            ref[at + rows : at + 2 * rows, :] = grad_values[span].astype(ref.dtype)

    if depth == 3:
        y = (index >> 2) & 1
        for odd in range(2):
            for side in range(2):

                @pl.when((parity == odd) & (y == side))
                def _():
                    put(swap_ref, [side ^ odd ^ 1, 3 - odd])
                    put(part_ref, [side ^ odd, 2 + odd])

    else:

        @pl.when(parity == 1)
        def _():
            put(swap_ref, range(depth))
            put(part_ref, [depth])

        @pl.when(parity == 0)
        def _():
            put(swap_ref, [depth])
            put(part_ref, range(depth))


def main_call(lengths, queries, cot, keys, values, path, depth):
    rows, width = keys.shape[1:]
    heads = queries.shape[0] // (2 * rows)
    slots = (depth + 2) * rows
    total = 2 * heads * rows
    parts = 2 if depth == 3 else depth
    vmem = pl.BlockSpec(memory_space=pltpu.VMEM)
    return pl.pallas_call(
        functools.partial(main_kernel, depth, heads, len(path)),
        out_shape=(
            jax.ShapeDtypeStruct((2, rows, heads * width), BF16),
            jax.ShapeDtypeStruct((2 * rows, width), BF16),
            jax.ShapeDtypeStruct((parts * 2 * rows, width), BF16),
            jax.ShapeDtypeStruct((parts * 2 * rows, width), F32),
        ),
        in_specs=[pl.BlockSpec(memory_space=pltpu.SMEM)] + [vmem] * (4 + len(path)),
        out_specs=(vmem,) * 4,
        scratch_shapes=[
            pltpu.VMEM((slots, width), BF16),
            pltpu.VMEM((slots, width), BF16),
            pltpu.VMEM((2, slots, width), BF16),
            pltpu.VMEM((width, slots), BF16),
            pltpu.VMEM((slots, total), BF16),
            pltpu.VMEM((slots, total), BF16),
        ],
        compiler_params=limit(24),
        name="attend",
    )(lengths, queries, cot, keys, values, *path)


def combine_kernel(depth, part_ref, other_ref, own_ref, *rest):
    sends, both = rest[:-1], rest[-1]
    block = own_ref.shape[0]
    index = lax.axis_index("leaf")
    both[...] = part_ref[...] + other_ref[...].astype(F32)

    def take(level):
        return both[pl.ds(pl.multiple_of(level * block, block), block), :]

    own_level = depth - trailing_zeros(index, depth)
    own_ref[...] = take(jnp.where(index & 1 == 1, 0, own_level))
    for mask, ref in enumerate(sends, 1):
        target = (index - (index & 1)) ^ (mask << 1)
        ref[...] = take(depth - trailing_zeros(target, depth)).astype(BF16)


def combine_call(part, other, depth):
    masks = (1 << (depth - 1)) - 1
    block = part.shape[0] // depth
    width = part.shape[1]
    vmem = pl.BlockSpec(memory_space=pltpu.VMEM)
    return pl.pallas_call(
        functools.partial(combine_kernel, depth),
        out_shape=[jax.ShapeDtypeStruct((block, width), F32)]
        + [jax.ShapeDtypeStruct((block, width), BF16)] * masks,
        in_specs=[vmem] * 2,
        out_specs=[vmem] * (1 + masks),
        scratch_shapes=[pltpu.VMEM(part.shape, F32)],
        compiler_params=limit(4),
        name="combine",
    )(part, other)


def fold_kernel(part_ref, other_ref, keep_ref, send_ref):
    half = send_ref.shape[0]
    x = (lax.axis_index("leaf") >> 1) & 1
    both = part_ref[...] + other_ref[...].astype(F32)
    keep_ref[...] = both
    send_ref[...] = jnp.where(x == 1, both[:half], both[half:]).astype(BF16)


def fold_call(part, other):
    vmem = pl.BlockSpec(memory_space=pltpu.VMEM)
    return pl.pallas_call(
        fold_kernel,
        out_shape=[
            jax.ShapeDtypeStruct(part.shape, F32),
            jax.ShapeDtypeStruct((part.shape[0] // 2, part.shape[1]), BF16),
        ],
        in_specs=[vmem] * 2,
        out_specs=[vmem] * 2,
        compiler_params=limit(4),
        name="fold",
    )(part, other)


def fold_x_kernel(keep_ref, other_ref, own_ref, send_ref):
    half = send_ref.shape[0]
    index = lax.axis_index("leaf")
    odd, x = index & 1 == 1, (index >> 1) & 1 == 1
    other = other_ref[...].astype(F32)
    first = keep_ref[:half, :] + other
    second = keep_ref[half:, :] + jnp.where(odd, 0.0, other)
    send_ref[...] = first.astype(BF16)
    own_ref[...] = jnp.where(odd, keep_ref[half:, :], jnp.where(x, second, first))


def fold_x_call(keep, other):
    vmem = pl.BlockSpec(memory_space=pltpu.VMEM)
    return pl.pallas_call(
        fold_x_kernel,
        out_shape=[
            jax.ShapeDtypeStruct(other.shape, F32),
            jax.ShapeDtypeStruct(other.shape, BF16),
        ],
        in_specs=[vmem] * 2,
        out_specs=[vmem] * 2,
        compiler_params=limit(4),
        name="fold_x",
    )(keep, other)


def final_kernel(depth, leaf_ref, own_ref, *refs):
    arrived, (keys_ref, values_ref) = refs[:-2], refs[-2:]
    rows = keys_ref.shape[1]
    index = lax.axis_index("leaf")
    parity = index & 1
    level = depth - trailing_zeros(index, depth)
    total = own_ref[...]
    for mask, ref in enumerate(arrived, 1):
        if depth == 3:
            mine = index & 3 == 0
            total = total + jnp.where(mine, ref[...].astype(F32), 0.0)
            continue
        mine = (parity == 0) & (owner_at(index ^ (mask << 1), level, depth) == index)
        total = total + jnp.where(mine, ref[...].astype(F32), 0.0)
    total = total.astype(BF16)
    keys_ref[0] = total[:rows]
    values_ref[0] = total[rows:]
    keys_ref[1] = leaf_ref[:rows, :]
    values_ref[1] = leaf_ref[rows:, :]


def final_call(leaf, own, arrived, shape, depth):
    vmem = pl.BlockSpec(memory_space=pltpu.VMEM)
    return pl.pallas_call(
        functools.partial(final_kernel, depth),
        out_shape=[jax.ShapeDtypeStruct(shape, BF16)] * 2,
        in_specs=[vmem] * (2 + len(arrived)),
        out_specs=[vmem] * 2,
        compiler_params=limit(2),
        name="final",
    )(leaf, own, *arrived)


def body(queries, key_states, value_states, grad_output, lengths):
    count = lax.axis_size("leaf")
    depth = depth_of(count)
    masks = range(1, count // 2)

    def move(block, flip):
        return lax.ppermute(block, "leaf", [(i, i ^ flip) for i in range(count)])

    pack = make_pack(lengths, key_states, value_states)
    if depth == 3:
        along_y = move(pack, 5)
        mate = move(pack, 1)
        query_rows, cot = rows_call(lengths, queries, grad_output, key_states.shape[2])
        along_x = move(pass_on(True, pack, along_y), 2)
        sent_on = pass_on(False, along_y, along_x)
        swapped = move(sent_on, 1)
        path = [pack, mate, along_x, sent_on, swapped]
    else:
        near = [move(pack, m << 1) for m in masks]
        mate = move(pack, 1)
        query_rows, cot = rows_call(lengths, queries, grad_output, key_states.shape[2])
        path = [pack, mate, *near, *[move(block, 1) for block in near]]
    grad_queries, leaf, swap, part = main_call(
        lengths, query_rows, cot, key_states, value_states, path, depth
    )
    other = move(swap, 1)
    if depth == 3:
        keep, send = fold_call(part, other)
        own, send = fold_x_call(keep, move(send, 2))
        arrived = [move(send, 5)]
    else:
        own, *sends = combine_call(part, other, depth)
        arrived = [move(block, m << 1) for m, block in zip(masks, sends)]
    grad_keys, grad_values = final_call(leaf, own, arrived, key_states.shape, depth)
    return grad_queries, grad_keys, grad_values


def solution(mesh):
    segments = P(("dp", "leaf"), None, None)
    return jax.shard_map(
        body,
        mesh=mesh,
        in_specs=(segments, segments, segments, segments, P(("dp", "leaf"))),
        out_specs=(segments, segments, segments),
        check_vma=False,
    )
```

```python
import functools

import jax
import jax.numpy as jnp
from jax import lax
from jax.experimental import pallas as pl
from jax.experimental.pallas import tpu as pltpu
from jax.sharding import PartitionSpec as P

BF16 = jnp.bfloat16
F32 = jnp.float32
TAIL = 16
BIG = -1e30
LOG2E = 1.4426950408889634
NT = (((1,), (1,)), ((), ()))
NN = (((1,), (0,)), ((), ()))


def depth_of(count):
    return count.bit_length() - 1


def trailing_zeros(index, depth):
    total = jnp.zeros((), jnp.int32)
    for bit in range(depth):
        total = total + jnp.where((index & ((2 << bit) - 1)) == 0, 1, 0)
    return total


def owner_of(index, level, depth):
    if level == 0:
        return index * 0
    shift = depth - level + 1
    return ((index >> shift) << shift) + (1 << (depth - level))


def owner_at(index, level, depth):
    owner = owner_of(index, 0, depth)
    for place in range(1, depth + 1):
        owner = jnp.where(level == place, owner_of(index, place, depth), owner)
    return owner


def chip_groups(count):
    return [list(range(core, count, 2)) for core in range(2)]


def limit(mib):
    return pltpu.CompilerParams(vmem_limit_bytes=mib * 1024 * 1024)


def pack_kernel(chips, lengths_ref, key_ref, value_ref, pack_ref, packs_ref):
    rows = key_ref.shape[1]
    length = jnp.full((TAIL, pack_ref.shape[1]), lengths_ref[0].astype(F32), F32)
    block = jnp.concatenate([key_ref[0], value_ref[0], length.astype(BF16)], 0)
    pack_ref[...] = block
    for chip in range(chips):
        packs_ref[chip] = block


def make_packs(lengths, keys, values, chips):
    rows, width = keys.shape[1:]
    first = pl.BlockSpec((1, rows, width), lambda step: (0, 0, 0))
    height = 2 * rows + TAIL
    return pl.pallas_call(
        functools.partial(pack_kernel, chips),
        grid=(1,),
        out_shape=(
            jax.ShapeDtypeStruct((height, width), BF16),
            jax.ShapeDtypeStruct((chips, height, width), BF16),
        ),
        in_specs=[pl.BlockSpec(memory_space=pltpu.SMEM), first, first],
        out_specs=(
            pl.BlockSpec((height, width), lambda step: (0, 0)),
            pl.BlockSpec((chips, height, width), lambda step: (0, 0, 0)),
        ),
        name="pack",
    )(lengths, keys, values)


def levels_kernel(depth, packs_ref, out_ref):
    index = lax.axis_index("leaf")
    for level in range(depth):
        out_ref[level] = packs_ref[owner_of(index, level, depth) >> 1]


def levels_call(packs, depth):
    vmem = pl.BlockSpec(memory_space=pltpu.VMEM)
    return pl.pallas_call(
        functools.partial(levels_kernel, depth),
        out_shape=jax.ShapeDtypeStruct((depth,) + packs.shape[1:], BF16),
        in_specs=[vmem],
        out_specs=vmem,
        compiler_params=limit(1 + depth // 4),
        name="levels",
    )(packs)


def rows_kernel(heads, lengths_ref, query_ref, grad_ref, query_s, cot_s):
    rows = query_ref.shape[1]
    width = query_ref.shape[2] // heads
    row = lax.broadcasted_iota(jnp.int32, (rows, width), 0)
    for segment in range(2):
        live = row < lengths_ref[segment]
        for head in range(heads):
            here = pl.ds((segment * heads + head) * rows, rows)
            columns = slice(head * width, (head + 1) * width)
            query_s[here, :] = query_ref[segment, :, columns]
            cot = grad_ref[segment, :, columns]
            cot_s[here, :] = jnp.where(live, cot, jnp.zeros((), BF16))


def rows_call(lengths, queries, grads, width):
    heads = queries.shape[2] // width
    rows = queries.shape[1]
    vmem = pl.BlockSpec(memory_space=pltpu.VMEM)
    shape = jax.ShapeDtypeStruct((2 * heads * rows, width), BF16)
    return pl.pallas_call(
        functools.partial(rows_kernel, heads),
        out_shape=(shape, shape),
        in_specs=[pl.BlockSpec(memory_space=pltpu.SMEM), vmem, vmem],
        out_specs=(vmem, vmem),
        compiler_params=limit(8),
        cost_estimate=pl.CostEstimate(flops=0, bytes_accessed=4 << 20, transcendentals=0),
        name="rows",
    )(lengths, queries, grads)


def main_kernel(depth, heads, *refs):
    lengths_ref, query_s, cot_s, key_ref, value_ref, own_ref, mate_ref, near, far = refs[:9]
    (
        grad_query_ref,
        leaf_ref,
        swap_ref,
        part_ref,
        keys_s,
        values_s,
        extra_s,
        keys_t,
        low_s,
        ds_s,
    ) = refs[9:]
    rows, width = key_ref.shape[1:]
    index = lax.axis_index("leaf")
    parity = index & 1
    own_level = depth - trailing_zeros(index, depth)
    scale = width ** (-0.5)
    lane = lax.broadcasted_iota(jnp.int32, (rows, width), 1)
    row = lax.broadcasted_iota(jnp.int32, (rows, width), 0)
    row_f = row.astype(F32)

    levels = depth + 2
    for level in range(levels):
        span = slice(level * rows, (level + 1) * rows)
        if level == depth + 1:
            key_block, value_block = key_ref[1], value_ref[1]
            length = jnp.full((1, width), lengths_ref[1].astype(F32), F32)
        else:
            if level == depth:
                block = jnp.where(parity == 1, own_ref[...], mate_ref[...])
            else:
                block = jnp.where(parity == 1, far[level], near[level])
            key_block, value_block = block[:rows], block[rows : 2 * rows]
            length = block[2 * rows : 2 * rows + 1].astype(F32)
        keys_s[span, :] = key_block
        values_s[span, :] = value_block
        keys_t[:, span] = key_block.T
        dead = row_f >= length
        for segment in range(2):
            if segment == 0 and level == depth + 1:
                continue
            level_of = own_level if segment == 0 else depth + 1
            diagonal = jnp.where(row > 0, row, -1)
            column = jnp.where(level == level_of, diagonal, -1)
            column = jnp.where(dead | (level > level_of), 0, column)
            extra_s[segment, span, :] = jnp.where(lane == column, 1.0, 0.0).astype(BF16)

    ruled = jnp.where((lane > row) | (lane == 0), BIG, 0.0).astype(BF16)
    ruled = jnp.concatenate([ruled, ruled], 0)

    step_rows = 2 * rows
    for segment in range(2):
        count = (depth + 1 + segment) * rows
        keys_wide = jnp.concatenate([keys_s[:count, :], extra_s[segment, :count, :]], 1)
        for pair in range(heads // 2):
            at = (segment * (heads // 2) + pair) * step_rows
            here = slice(at, at + step_rows)
            columns = [slice(h * width, (h + 1) * width) for h in (2 * pair, 2 * pair + 1)]
            query, cot = query_s[here, :], cot_s[here, :]
            scores = lax.dot_general(
                keys_wide,
                jnp.concatenate([query, ruled], 1),
                NT,
                preferred_element_type=F32,
            )
            top = jnp.max(scores, axis=0, keepdims=True)
            weights = jnp.exp2((scores - top) * (scale * LOG2E))
            total = jnp.sum(weights, axis=0, keepdims=True)
            weights = weights * (1.0 / total)
            low_s[:count, here] = weights.astype(BF16)
            grad_weights = lax.dot_general(
                values_s[:count, :], cot, NT, preferred_element_type=F32
            )
            delta = jnp.sum(weights * grad_weights, axis=0, keepdims=True)
            grad_scores = (weights * (grad_weights - delta)).astype(BF16)
            ds_s[:count, here] = grad_scores
            grad_query = lax.dot_general(
                keys_t[:, :count], grad_scores, NN, preferred_element_type=F32
            )
            grad_query = (grad_query * scale).astype(BF16).T
            for n, c in enumerate(columns):
                grad_query_ref[segment, :, c] = grad_query[n * rows : (n + 1) * rows]

    inner = (depth + 1) * rows
    half = heads * rows
    grad_keys = lax.dot_general(ds_s[:inner, :], query_s[...], NN, preferred_element_type=F32)
    grad_keys = grad_keys * scale
    grad_values = lax.dot_general(low_s[:inner, :], cot_s[...], NN, preferred_element_type=F32)
    leaf_keys = lax.dot_general(
        ds_s[inner:, half:], query_s[half:, :], NN, preferred_element_type=F32
    )
    leaf_values = lax.dot_general(
        low_s[inner:, half:], cot_s[half:, :], NN, preferred_element_type=F32
    )
    leaf_ref[0:rows, :] = (leaf_keys * scale).astype(BF16)
    leaf_ref[rows : 2 * rows, :] = leaf_values.astype(BF16)

    def put(ref, levels_at):
        for place, level in enumerate(levels_at):
            span = slice(level * rows, (level + 1) * rows)
            at = place * 2 * rows
            ref[at : at + rows, :] = grad_keys[span].astype(ref.dtype)
            ref[at + rows : at + 2 * rows, :] = grad_values[span].astype(ref.dtype)

    @pl.when(parity == 1)
    def _():
        put(swap_ref, range(depth))
        put(part_ref, [depth])

    @pl.when(parity == 0)
    def _():
        put(swap_ref, [depth])
        put(part_ref, range(depth))


def main_call(lengths, queries, cot, keys, values, own, mate, near, far, depth):
    rows, width = keys.shape[1:]
    heads = queries.shape[0] // (2 * rows)
    slots = (depth + 2) * rows
    total = 2 * heads * rows
    vmem = pl.BlockSpec(memory_space=pltpu.VMEM)
    return pl.pallas_call(
        functools.partial(main_kernel, depth, heads),
        out_shape=(
            jax.ShapeDtypeStruct((2, rows, heads * width), BF16),
            jax.ShapeDtypeStruct((2 * rows, width), BF16),
            jax.ShapeDtypeStruct((depth * 2 * rows, width), BF16),
            jax.ShapeDtypeStruct((depth * 2 * rows, width), F32),
        ),
        in_specs=[pl.BlockSpec(memory_space=pltpu.SMEM)] + [vmem] * 8,
        out_specs=(vmem,) * 4,
        scratch_shapes=[
            pltpu.VMEM((slots, width), BF16),
            pltpu.VMEM((slots, width), BF16),
            pltpu.VMEM((2, slots, width), BF16),
            pltpu.VMEM((width, slots), BF16),
            pltpu.VMEM((slots, total), BF16),
            pltpu.VMEM((slots, total), BF16),
        ],
        compiler_params=limit(24),
        name="attend",
    )(lengths, queries, cot, keys, values, own, mate, near, far)


def combine_kernel(depth, part_ref, other_ref, own_ref, sends_ref, both):
    block = own_ref.shape[0]
    index = lax.axis_index("leaf")
    both[...] = part_ref[...] + other_ref[...].astype(F32)

    def take(level):
        return both[pl.ds(pl.multiple_of(level * block, block), block), :]

    own_level = depth - trailing_zeros(index, depth)
    own_ref[...] = take(jnp.where(index & 1 == 1, 0, own_level))
    for chip in range(sends_ref.shape[0]):
        level = 0 if chip == 0 else depth - ((2 * chip) & -(2 * chip)).bit_length() + 1
        sends_ref[chip] = both[level * block : (level + 1) * block, :].astype(BF16)


def combine_call(part, other, depth):
    chips = 1 << (depth - 1)
    block = part.shape[0] // depth
    width = part.shape[1]
    vmem = pl.BlockSpec(memory_space=pltpu.VMEM)
    return pl.pallas_call(
        functools.partial(combine_kernel, depth),
        out_shape=(
            jax.ShapeDtypeStruct((block, width), F32),
            jax.ShapeDtypeStruct((chips, block, width), BF16),
        ),
        in_specs=[vmem] * 2,
        out_specs=(vmem,) * 2,
        scratch_shapes=[pltpu.VMEM(part.shape, F32)],
        compiler_params=limit(4),
        name="combine",
    )(part, other)


def final_kernel(depth, leaf_ref, own_ref, arrived_ref, keys_ref, values_ref):
    rows = keys_ref.shape[1]
    index = lax.axis_index("leaf")
    level = depth - trailing_zeros(index, depth)
    total = own_ref[...]
    for chip in range(arrived_ref.shape[0]):
        sender = jnp.full((), 2 * chip, jnp.int32)
        mine = (sender != index) & (owner_at(sender, level, depth) == index)
        mine = mine & (index & 1 == 0)
        total = total + jnp.where(mine, arrived_ref[chip].astype(F32), 0.0)
    total = total.astype(BF16)
    keys_ref[0] = total[:rows]
    values_ref[0] = total[rows:]
    keys_ref[1] = leaf_ref[:rows, :]
    values_ref[1] = leaf_ref[rows:, :]


def final_call(leaf, own, arrived, shape, depth):
    vmem = pl.BlockSpec(memory_space=pltpu.VMEM)
    return pl.pallas_call(
        functools.partial(final_kernel, depth),
        out_shape=[jax.ShapeDtypeStruct(shape, BF16)] * 2,
        in_specs=[vmem] * 3,
        out_specs=[vmem] * 2,
        compiler_params=limit(2),
        name="final",
    )(leaf, own, arrived)


def body(queries, key_states, value_states, grad_output, lengths):
    count = lax.axis_size("leaf")
    depth = depth_of(count)
    swap_pairs = [(i, i ^ 1) for i in range(count)]
    groups = chip_groups(count)

    def exchange(blocks):
        return lax.all_to_all(blocks, "leaf", 0, 0, axis_index_groups=groups, tiled=True)

    pack, packs = make_packs(lengths, key_states, value_states, count // 2)
    mate = lax.ppermute(pack, "leaf", swap_pairs)
    near = exchange(packs)
    query_rows, cot = rows_call(lengths, queries, grad_output, key_states.shape[2])
    near = levels_call(near, depth)
    far = lax.ppermute(near, "leaf", swap_pairs)
    grad_queries, leaf, swap, part = main_call(
        lengths, query_rows, cot, key_states, value_states, pack, mate, near, far, depth
    )
    other = lax.ppermute(swap, "leaf", swap_pairs)
    own, sends = combine_call(part, other, depth)
    arrived = exchange(sends)
    grad_keys, grad_values = final_call(leaf, own, arrived, key_states.shape, depth)
    return grad_queries, grad_keys, grad_values


def solution(mesh):
    segments = P(("dp", "leaf"), None, None)
    return jax.shard_map(
        body,
        mesh=mesh,
        in_specs=(segments, segments, segments, segments, P(("dp", "leaf"))),
        out_specs=(segments, segments, segments),
        check_vma=False,
    )
```

```python
import functools

import jax
import jax.numpy as jnp
from jax import lax
from jax.experimental import pallas as pl
from jax.experimental.pallas import tpu as pltpu
from jax.sharding import PartitionSpec as P

BF16 = jnp.bfloat16
F32 = jnp.float32
TAIL = 16
BIG = -1e30
LOG2E = 1.4426950408889634
NT = (((1,), (1,)), ((), ()))
NN = (((1,), (0,)), ((), ()))


def depth_of(count):
    return count.bit_length() - 1


def trailing_zeros(index, depth):
    total = jnp.zeros((), jnp.int32)
    for bit in range(depth):
        total = total + jnp.where((index & ((2 << bit) - 1)) == 0, 1, 0)
    return total


def owner_of(index, level, depth):
    if level == 0:
        return index * 0
    shift = depth - level + 1
    return ((index >> shift) << shift) + (1 << (depth - level))


def level_of_even(index, depth):
    return depth - trailing_zeros(index, depth)


def owner_at(index, level, depth):
    owner = owner_of(index, 0, depth)
    for place in range(1, depth + 1):
        owner = jnp.where(level == place, owner_of(index, place, depth), owner)
    return owner


def limit(mib):
    return pltpu.CompilerParams(vmem_limit_bytes=mib * 1024 * 1024)


def make_pack(lengths, other_lengths, keys, values, other_keys, other_values):
    odd = lax.axis_index("leaf") & 1 == 1
    length = jnp.where(odd, other_lengths[0], lengths[0]).astype(BF16)
    return jnp.concatenate(
        [
            jnp.where(odd, other_keys[0], keys[0]),
            jnp.where(odd, other_values[0], values[0]),
            jnp.full((TAIL, keys.shape[2]), length, BF16),
        ],
        0,
    )


def rows_kernel(heads, lengths_ref, query_ref, grad_ref, query_s, cot_s):
    rows = query_ref.shape[1]
    width = query_ref.shape[2] // heads
    row = lax.broadcasted_iota(jnp.int32, (rows, width), 0)
    for segment in range(2):
        live = row < lengths_ref[segment]
        for head in range(heads):
            here = pl.ds((segment * heads + head) * rows, rows)
            columns = slice(head * width, (head + 1) * width)
            query_s[here, :] = query_ref[segment, :, columns]
            cot = grad_ref[segment, :, columns]
            cot_s[here, :] = jnp.where(live, cot, jnp.zeros((), BF16))


def rows_call(lengths, queries, grads, width):
    heads = queries.shape[2] // width
    rows = queries.shape[1]
    vmem = pl.BlockSpec(memory_space=pltpu.VMEM)
    shape = jax.ShapeDtypeStruct((2 * heads * rows, width), BF16)
    return pl.pallas_call(
        functools.partial(rows_kernel, heads),
        out_shape=(shape, shape),
        in_specs=[pl.BlockSpec(memory_space=pltpu.SMEM), vmem, vmem],
        out_specs=(vmem, vmem),
        compiler_params=limit(8),
        cost_estimate=pl.CostEstimate(flops=0, bytes_accessed=4 << 20, transcendentals=0),
        name="rows",
    )(lengths, queries, grads)


def main_kernel(depth, heads, *refs):
    masks = (1 << (depth - 1)) - 1
    lengths_ref, other_lengths_ref, query_s, cot_s = refs[:4]
    key_ref, value_ref, other_key_ref, other_value_ref, pack_ref = refs[4:9]
    near, refs = refs[9 : 9 + masks], refs[9 + masks :]
    grad_query_ref, leaf_ref, part_ref = refs[:3]
    sends, refs = refs[3 : 3 + masks], refs[3 + masks :]
    keys_s, values_s, extra_s, keys_t, low_s, ds_s, terms_s = refs
    rows, width = key_ref.shape[1:]
    index = lax.axis_index("leaf")
    odd = index & 1 == 1
    even = index - (index & 1)
    own_level = depth - trailing_zeros(index, depth)
    scale = width ** (-0.5)
    lane = lax.broadcasted_iota(jnp.int32, (rows, width), 1)
    row = lax.broadcasted_iota(jnp.int32, (rows, width), 0)
    row_f = row.astype(F32)

    levels = depth + 2
    for level in range(levels):
        span = slice(level * rows, (level + 1) * rows)
        if level == depth + 1:
            key_block, value_block, length = key_ref[1], value_ref[1], lengths_ref[1]
        elif level == depth:
            key_block = jnp.where(odd, key_ref[0], other_key_ref[0])
            value_block = jnp.where(odd, value_ref[0], other_value_ref[0])
            length = jnp.where(odd, lengths_ref[0], other_lengths_ref[0])
        else:
            pick = (even ^ owner_of(even, level, depth)) >> 1
            block = pack_ref[...]
            for mask in range(1, masks + 1):
                block = jnp.where(pick == mask, near[mask - 1][...], block)
            key_block, value_block = block[:rows], block[rows : 2 * rows]
            length = block[2 * rows : 2 * rows + 1].astype(F32)
        if level >= depth:
            length = jnp.full((1, width), length.astype(F32), F32)
        keys_s[span, :] = key_block
        values_s[span, :] = value_block
        keys_t[:, span] = key_block.T
        dead = row_f >= length
        for segment in range(2):
            if segment == 0 and level == depth + 1:
                continue
            level_of = own_level if segment == 0 else depth + 1
            diagonal = jnp.where(row > 0, row, -1)
            column = jnp.where(level == level_of, diagonal, -1)
            column = jnp.where(dead | (level > level_of), 0, column)
            extra_s[segment, span, :] = jnp.where(lane == column, 1.0, 0.0).astype(BF16)

    ruled = jnp.where((lane > row) | (lane == 0), BIG, 0.0).astype(BF16)
    ruled = jnp.concatenate([ruled, ruled], 0)

    step_rows = 2 * rows
    for segment in range(2):
        count = (depth + 1 + segment) * rows
        keys_wide = jnp.concatenate([keys_s[:count, :], extra_s[segment, :count, :]], 1)
        for pair in range(heads // 2):
            at = (segment * (heads // 2) + pair) * step_rows
            here = slice(at, at + step_rows)
            columns = [slice(h * width, (h + 1) * width) for h in (2 * pair, 2 * pair + 1)]
            query, cot = query_s[here, :], cot_s[here, :]
            scores = lax.dot_general(
                keys_wide,
                jnp.concatenate([query, ruled], 1),
                NT,
                preferred_element_type=F32,
            )
            top = jnp.max(scores, axis=0, keepdims=True)
            weights = jnp.exp2((scores - top) * (scale * LOG2E))
            total = jnp.sum(weights, axis=0, keepdims=True)
            weights = weights * (1.0 / total)
            low_s[:count, here] = weights.astype(BF16)
            grad_weights = lax.dot_general(
                values_s[:count, :], cot, NT, preferred_element_type=F32
            )
            delta = jnp.sum(weights * grad_weights, axis=0, keepdims=True)
            grad_scores = (weights * (grad_weights - delta)).astype(BF16)
            ds_s[:count, here] = grad_scores
            grad_query = lax.dot_general(
                keys_t[:, :count], grad_scores, NN, preferred_element_type=F32
            )
            grad_query = (grad_query * scale).astype(BF16).T
            for n, c in enumerate(columns):
                grad_query_ref[segment, :, c] = grad_query[n * rows : (n + 1) * rows]

    inner = (depth + 1) * rows
    half = heads * rows
    grad_keys = lax.dot_general(ds_s[:inner, :], query_s[...], NN, preferred_element_type=F32)
    grad_keys = grad_keys * scale
    grad_values = lax.dot_general(low_s[:inner, :], cot_s[...], NN, preferred_element_type=F32)
    leaf_keys = lax.dot_general(
        ds_s[inner:, half:], query_s[half:, :], NN, preferred_element_type=F32
    )
    leaf_values = lax.dot_general(
        low_s[inner:, half:], cot_s[half:, :], NN, preferred_element_type=F32
    )
    leaf_ref[0:rows, :] = (leaf_keys * scale).astype(BF16)
    leaf_ref[rows : 2 * rows, :] = leaf_values.astype(BF16)

    for level in range(depth + 1):
        span = slice(level * rows, (level + 1) * rows)
        terms_s[level, :rows, :] = grad_keys[span]
        terms_s[level, rows:, :] = grad_values[span]
    part_ref[0] = terms_s[level_of_even(even, depth)]
    part_ref[1] = terms_s[depth]
    for mask, ref in enumerate(sends, 1):
        ref[...] = terms_s[level_of_even(even ^ (mask << 1), depth)].astype(BF16)


def main_call(smalls, queries, cot, arrays, near, depth):
    rows, width = arrays[0].shape[1:]
    heads = queries.shape[0] // (2 * rows)
    slots = (depth + 2) * rows
    total = 2 * heads * rows
    smem = pl.BlockSpec(memory_space=pltpu.SMEM)
    vmem = pl.BlockSpec(memory_space=pltpu.VMEM)
    return pl.pallas_call(
        functools.partial(main_kernel, depth, heads),
        out_shape=[
            jax.ShapeDtypeStruct((2, rows, heads * width), BF16),
            jax.ShapeDtypeStruct((2 * rows, width), BF16),
            jax.ShapeDtypeStruct((2, 2 * rows, width), F32),
        ]
        + [jax.ShapeDtypeStruct((2 * rows, width), BF16)] * len(near),
        in_specs=[smem] * 2 + [vmem] * (2 + len(arrays) + len(near)),
        out_specs=[vmem] * (3 + len(near)),
        scratch_shapes=[
            pltpu.VMEM((slots, width), BF16),
            pltpu.VMEM((slots, width), BF16),
            pltpu.VMEM((2, slots, width), BF16),
            pltpu.VMEM((width, slots), BF16),
            pltpu.VMEM((slots, total), BF16),
            pltpu.VMEM((slots, total), BF16),
            pltpu.VMEM((depth + 1, 2 * rows, width), F32),
        ],
        compiler_params=limit(24),
        name="attend",
    )(*smalls, queries, cot, *arrays, *near)


def fold_kernel(depth, part_ref, *refs):
    arrived, (keep_ref, send_ref) = refs[:-2], refs[-2:]
    index = lax.axis_index("leaf")
    odd = index & 1 == 1
    even = index - (index & 1)
    level = level_of_even(even, depth)
    total = part_ref[0]
    for mask, ref in enumerate(arrived, 1):
        mine = owner_at(even ^ (mask << 1), level, depth) == even
        total = total + jnp.where(mine, ref[...].astype(F32), 0.0)
    keep_ref[...] = jnp.where(odd, part_ref[1], total)
    send_ref[...] = jnp.where(odd, total, part_ref[1]).astype(BF16)


def fold_call(part, arrived, depth):
    vmem = pl.BlockSpec(memory_space=pltpu.VMEM)
    return pl.pallas_call(
        functools.partial(fold_kernel, depth),
        out_shape=[
            jax.ShapeDtypeStruct(part.shape[1:], F32),
            jax.ShapeDtypeStruct(part.shape[1:], BF16),
        ],
        in_specs=[vmem] * (1 + len(arrived)),
        out_specs=[vmem] * 2,
        compiler_params=limit(3),
        name="fold",
    )(part, *arrived)


def final_kernel(leaf_ref, keep_ref, other_ref, keys_ref, values_ref):
    rows = keys_ref.shape[1]
    total = (keep_ref[...] + other_ref[...].astype(F32)).astype(BF16)
    keys_ref[0] = total[:rows]
    values_ref[0] = total[rows:]
    keys_ref[1] = leaf_ref[:rows, :]
    values_ref[1] = leaf_ref[rows:, :]


def final_call(leaf, keep, other, shape):
    vmem = pl.BlockSpec(memory_space=pltpu.VMEM)
    return pl.pallas_call(
        final_kernel,
        out_shape=[jax.ShapeDtypeStruct(shape, BF16)] * 2,
        in_specs=[vmem] * 3,
        out_specs=[vmem] * 2,
        compiler_params=limit(2),
        name="final",
    )(leaf, keep, other)


def body(queries, key_states, value_states, grad_output, lengths):
    count = lax.axis_size("leaf")
    depth = depth_of(count)
    masks = range(1, count // 2)

    def move(block, flip):
        return lax.ppermute(block, "leaf", [(i, i ^ flip) for i in range(count)])

    def exchange(blocks):
        moved = {m: move(blocks[m], m << 1) for m in reversed(masks)}
        return [moved[m] for m in masks]

    other_keys, other_values = move(key_states, 1), move(value_states, 1)
    other_lengths = move(lengths, 1)
    pack = make_pack(lengths, other_lengths, key_states, value_states, other_keys, other_values)
    near = exchange({m: pack for m in masks})
    query_rows, cot = rows_call(lengths, queries, grad_output, key_states.shape[2])
    arrays = (key_states, value_states, other_keys, other_values, pack)
    grad_queries, leaf, part, *sends = main_call(
        (lengths, other_lengths), query_rows, cot, arrays, near, depth
    )
    arrived = exchange(dict(zip(masks, sends)))
    keep, send = fold_call(part, arrived, depth)
    grad_keys, grad_values = final_call(leaf, keep, move(send, 1), key_states.shape)
    return grad_queries, grad_keys, grad_values


def solution(mesh):
    segments = P(("dp", "leaf"), None, None)
    return jax.shard_map(
        body,
        mesh=mesh,
        in_specs=(segments, segments, segments, segments, P(("dp", "leaf"))),
        out_specs=(segments, segments, segments),
        check_vma=False,
    )
```

```python
import functools

import jax
import jax.numpy as jnp
from jax import lax
from jax.experimental import pallas as pl
from jax.experimental.pallas import tpu as pltpu
from jax.sharding import PartitionSpec as P

BF16 = jnp.bfloat16
F32 = jnp.float32
TAIL = 16
BIG = -1e30
LOG2E = 1.4426950408889634
NT = (((1,), (1,)), ((), ()))
NN = (((1,), (0,)), ((), ()))


def depth_of(count):
    return count.bit_length() - 1


def trailing_zeros(index, depth):
    total = jnp.zeros((), jnp.int32)
    for bit in range(depth):
        total = total + jnp.where((index & ((2 << bit) - 1)) == 0, 1, 0)
    return total


def owner_of(index, level, depth):
    if level == 0:
        return index * 0
    shift = depth - level + 1
    return ((index >> shift) << shift) + (1 << (depth - level))


def level_of_even(index, depth):
    return depth - trailing_zeros(index, depth)


def owner_at(index, level, depth):
    owner = owner_of(index, 0, depth)
    for place in range(1, depth + 1):
        owner = jnp.where(level == place, owner_of(index, place, depth), owner)
    return owner


def call(kernel, name, mib, scalars, arrays, outs, scratch=(), flops=0):
    smem = pl.BlockSpec(memory_space=pltpu.SMEM)
    vmem = pl.BlockSpec(memory_space=pltpu.VMEM)
    return pl.pallas_call(
        kernel,
        out_shape=[jax.ShapeDtypeStruct(shape, kind) for shape, kind in outs],
        in_specs=[smem] * len(scalars) + [vmem] * len(arrays),
        out_specs=[vmem] * len(outs),
        scratch_shapes=[pltpu.VMEM(shape, kind) for shape, kind in scratch],
        compiler_params=pltpu.CompilerParams(vmem_limit_bytes=mib * 1024 * 1024),
        cost_estimate=pl.CostEstimate(flops=flops, bytes_accessed=1 << 20, transcendentals=0),
        name=name,
    )(*scalars, *arrays)


def ruled_columns(rows, width):
    lane = lax.broadcasted_iota(jnp.int32, (rows, width), 1)
    row = lax.broadcasted_iota(jnp.int32, (rows, width), 0)
    ruled = jnp.where((lane > row) | (lane == 0), BIG, 0.0).astype(BF16)
    return jnp.concatenate([ruled, ruled], 0)


def mask_columns(length, before, same, rows, width):
    lane = lax.broadcasted_iota(jnp.int32, (rows, width), 1)
    row = lax.broadcasted_iota(jnp.int32, (rows, width), 0)
    column = jnp.where(same & (row > 0), row, -1)
    live = (row.astype(F32) < length) & (before | same)
    column = jnp.where(live, column, 0)
    return jnp.where(lane == column, 1.0, 0.0).astype(BF16)


def block_scores(keys_wide, values, query_wide, cot, factor):
    scores = lax.dot_general(keys_wide, query_wide, NT, preferred_element_type=F32)
    top = jnp.max(scores, axis=0, keepdims=True)
    raised = jnp.exp2((scores - top) * factor)
    total = jnp.sum(raised, axis=0, keepdims=True)
    grad_weights = lax.dot_general(values, cot, NT, preferred_element_type=F32)
    partial = jnp.sum(raised * grad_weights, axis=0, keepdims=True)
    return raised, grad_weights, top, total, partial


def early_kernel(depth, heads, lengths_ref, query_ref, grad_ref, key_ref, value_ref, *refs):
    own_ref, mate_ref, query_s, cot_s, raised_s, weights_s, stats_s, keys_s = refs
    rows, width = key_ref.shape[1:]
    index = lax.axis_index("leaf")
    odd = index & 1 == 1
    factor = width ** (-0.5) * LOG2E
    step = 2 * rows
    row = lax.broadcasted_iota(jnp.int32, (rows, width), 0)
    block = jnp.where(odd, own_ref[...], mate_ref[...])
    length = block[2 * rows : 2 * rows + 1].astype(F32)
    keys = [block[:rows], key_ref[1]]
    values = [block[rows : 2 * rows], value_ref[1]]
    keys_s[:rows, :] = keys[0]
    keys_s[rows:, :] = keys[1]
    yes, no = jnp.full((), True), jnp.full((), False)
    ruled = ruled_columns(rows, width)
    leaf_length = jnp.full((1, width), lengths_ref[1].astype(F32), F32)
    wide = [
        [
            jnp.concatenate([keys[0], mask_columns(length, no, odd, rows, width)], 1),
        ],
        [
            jnp.concatenate([keys[0], mask_columns(length, yes, no, rows, width)], 1),
            jnp.concatenate([keys[1], mask_columns(leaf_length, no, yes, rows, width)], 1),
        ],
    ]
    for segment in range(2):
        live = row < lengths_ref[segment]
        for pair in range(heads // 2):
            at = (segment * (heads // 2) + pair) * step
            here = slice(at, at + step)
            columns = [slice(h * width, (h + 1) * width) for h in (2 * pair, 2 * pair + 1)]
            query = jnp.concatenate([query_ref[segment, :, c] for c in columns], 0)
            cot = jnp.concatenate(
                [jnp.where(live, grad_ref[segment, :, c], jnp.zeros((), BF16)) for c in columns], 0
            )
            query_s[here, :] = query
            cot_s[here, :] = cot
            query_wide = jnp.concatenate([query, ruled], 1)
            for place in range(1 + segment):
                span = slice(place * rows, (place + 1) * rows)
                raised, grad_weights, top, total, partial = block_scores(
                    wide[segment][place], values[place], query_wide, cot, factor
                )
                raised_s[span, here] = raised
                weights_s[span, here] = grad_weights
                for n, line in enumerate((top, total, partial)):
                    stats_s[3 * place + n : 3 * place + n + 1, here] = line


def middle_kernel(depth, heads, query_s, cot_s, stats_ref, pack_ref, *refs):
    masks = (1 << (depth - 1)) - 1
    near, refs = refs[:masks], refs[masks:]
    ds_s, joined_s, keys_t, part_ref = refs[:4]
    sends, refs = refs[4 : 4 + masks], refs[4 + masks :]
    raised_s, weights_s, low_s, terms_s = refs
    width = pack_ref.shape[1]
    rows = (pack_ref.shape[0] - TAIL) // 2
    index = lax.axis_index("leaf")
    even = index - (index & 1)
    own_level = depth - trailing_zeros(index, depth)
    scale = width ** (-0.5)
    factor = scale * LOG2E
    step = 2 * rows
    yes, no = jnp.full((), True), jnp.full((), False)
    ruled = ruled_columns(rows, width)
    values = []
    wide = [[], []]
    for level in range(depth):
        pick = (even ^ owner_of(even, level, depth)) >> 1
        block = pack_ref[...]
        for mask in range(1, masks + 1):
            block = jnp.where(pick == mask, near[mask - 1][...], block)
        keys = block[:rows]
        values.append(block[rows : 2 * rows])
        length = block[2 * rows : 2 * rows + 1].astype(F32)
        keys_t[:, level * rows : (level + 1) * rows] = keys.T
        inner = mask_columns(length, level < own_level, level == own_level, rows, width)
        outer = mask_columns(length, yes, no, rows, width)
        wide[0].append(jnp.concatenate([keys, inner], 1))
        wide[1].append(jnp.concatenate([keys, outer], 1))

    grad_keys = grad_values = None
    half = heads * rows
    for segment in range(2):
        for pair in range(heads // 2):
            at = (segment * (heads // 2) + pair) * step
            here = slice(at, at + step)
            query, cot = query_s[here, :], cot_s[here, :]
            query_wide = jnp.concatenate([query, ruled], 1)
            tops, totals, partials = [], [], []
            for place in range(1 + segment):
                tops.append(stats_ref[3 * place : 3 * place + 1, here])
                totals.append(stats_ref[3 * place + 1 : 3 * place + 2, here])
                partials.append(stats_ref[3 * place + 2 : 3 * place + 3, here])
            for level in range(depth):
                span = slice(level * rows, (level + 1) * rows)
                raised, grad_weights, top, total, partial = block_scores(
                    wide[segment][level], values[level], query_wide, cot, factor
                )
                raised_s[span, here] = raised
                weights_s[span, here] = grad_weights
                tops.append(top)
                totals.append(total)
                partials.append(partial)
            highest = functools.reduce(jnp.maximum, tops)
            shares = [jnp.exp2((top - highest) * factor) for top in tops]
            total = sum(share * part for share, part in zip(shares, totals))
            inverse = 1.0 / total
            shares = [share * inverse for share in shares]
            delta = sum(share * part for share, part in zip(shares, partials))
            joined_s[0:1, here] = delta
            for place in range(1 + segment):
                joined_s[1 + place : 2 + place, here] = shares[place]
            for level in range(depth):
                span = slice(level * rows, (level + 1) * rows)
                weights = raised_s[span, here] * shares[1 + segment + level]
                low_s[span, here] = weights.astype(BF16)
                ds_s[span, here] = (weights * (weights_s[span, here] - delta)).astype(BF16)
        now = slice(segment * half, (segment + 1) * half)
        more_keys = lax.dot_general(
            ds_s[:, now], query_s[now, :], NN, preferred_element_type=F32
        )
        more_values = lax.dot_general(
            low_s[:, now], cot_s[now, :], NN, preferred_element_type=F32
        )
        grad_keys = more_keys if segment == 0 else grad_keys + more_keys
        grad_values = more_values if segment == 0 else grad_values + more_values
    for level in range(depth):
        span = slice(level * rows, (level + 1) * rows)
        terms_s[level, :rows, :] = grad_keys[span] * scale
        terms_s[level, rows:, :] = grad_values[span]
    part_ref[...] = terms_s[level_of_even(even, depth)]
    for mask, ref in enumerate(sends, 1):
        ref[...] = terms_s[level_of_even(even ^ (mask << 1), depth)].astype(BF16)


def late_kernel(heads, query_s, cot_s, raised_ref, weights_ref, joined_ref, ds_ref, *refs):
    keys_t, keys_s, grad_query_ref, leaf_ref, part_ref, low_s, ds_s = refs
    width = keys_s.shape[1]
    rows = keys_s.shape[0] // 2
    scale = width ** (-0.5)
    step = 2 * rows
    half = heads * rows
    near_t = keys_s[...].T
    for segment in range(2):
        count = (1 + segment) * rows
        for pair in range(heads // 2):
            at = (segment * (heads // 2) + pair) * step
            here = slice(at, at + step)
            delta = joined_ref[0:1, here]
            for place in range(1 + segment):
                span = slice(place * rows, (place + 1) * rows)
                weights = raised_ref[span, here] * joined_ref[1 + place : 2 + place, here]
                low_s[span, here] = weights.astype(BF16)
                ds_s[span, here] = (weights * (weights_ref[span, here] - delta)).astype(BF16)
            grad_query = lax.dot_general(
                keys_t[...], ds_ref[:, here], NN, preferred_element_type=F32
            ) + lax.dot_general(
                near_t[:, :count], ds_s[:count, here], NN, preferred_element_type=F32
            )
            grad_query = (grad_query * scale).astype(BF16).T
            for n in range(2):
                c = slice((2 * pair + n) * width, (2 * pair + n + 1) * width)
                grad_query_ref[segment, :, c] = grad_query[n * rows : (n + 1) * rows]
    part_ref[:rows, :] = scale * lax.dot_general(
        ds_s[:rows, :], query_s[...], NN, preferred_element_type=F32
    )
    part_ref[rows:, :] = lax.dot_general(
        low_s[:rows, :], cot_s[...], NN, preferred_element_type=F32
    )
    leaf_keys = scale * lax.dot_general(
        ds_s[rows:, half:], query_s[half:, :], NN, preferred_element_type=F32
    )
    leaf_values = lax.dot_general(
        low_s[rows:, half:], cot_s[half:, :], NN, preferred_element_type=F32
    )
    leaf_ref[:rows, :] = leaf_keys.astype(BF16)
    leaf_ref[rows:, :] = leaf_values.astype(BF16)


def fold_kernel(depth, even_ref, last_ref, *refs):
    arrived, (keep_ref, send_ref) = refs[:-2], refs[-2:]
    index = lax.axis_index("leaf")
    odd = index & 1 == 1
    even = index - (index & 1)
    level = level_of_even(even, depth)
    total = even_ref[...]
    for mask, ref in enumerate(arrived, 1):
        mine = owner_at(even ^ (mask << 1), level, depth) == even
        total = total + jnp.where(mine, ref[...].astype(F32), 0.0)
    keep_ref[...] = jnp.where(odd, last_ref[...], total)
    send_ref[...] = jnp.where(odd, total, last_ref[...]).astype(BF16)


def final_kernel(leaf_ref, keep_ref, other_ref, keys_ref, values_ref):
    rows = keys_ref.shape[1]
    total = (keep_ref[...] + other_ref[...].astype(F32)).astype(BF16)
    keys_ref[0] = total[:rows]
    values_ref[0] = total[rows:]
    keys_ref[1] = leaf_ref[:rows, :]
    values_ref[1] = leaf_ref[rows:, :]


def body(queries, key_states, value_states, grad_output, lengths):
    count = lax.axis_size("leaf")
    depth = depth_of(count)
    masks = range(1, count // 2)
    rows, width = key_states.shape[1:]
    heads = queries.shape[2] // width
    total = 2 * heads * rows
    inner = depth * rows
    terms = (2 * rows, width)

    def move(block, flip):
        return lax.ppermute(block, "leaf", [(i, i ^ flip) for i in range(count)])

    def exchange(blocks):
        moved = {m: move(blocks[m], m << 1) for m in reversed(masks)}
        return [moved[m] for m in masks]

    length = jnp.full((TAIL, width), lengths[0].astype(BF16), BF16)
    own = jnp.concatenate([key_states[0], value_states[0], length], 0)
    mate = move(own, 1)
    pack = jnp.where(lax.axis_index("leaf") & 1 == 1, mate, own)
    near = exchange({m: pack for m in masks})
    query_rows, cot, raised, weights, stats, last_keys = call(
        functools.partial(early_kernel, depth, heads),
        "early",
        8,
        (lengths,),
        (queries, grad_output, key_states, value_states, own, mate),
        [
            ((total, width), BF16),
            ((total, width), BF16),
            ((2 * rows, total), F32),
            ((2 * rows, total), F32),
            ((8, total), F32),
            ((2 * rows, width), BF16),
        ],
        flops=4 * 2 * rows * total * width,
    )
    ds, joined, keys_t, even_part, *sends = call(
        functools.partial(middle_kernel, depth, heads),
        "middle",
        24,
        (),
        (query_rows, cot, stats, pack, *near),
        [
            ((inner, total), BF16),
            ((8, total), F32),
            ((width, inner), BF16),
            (terms, F32),
        ]
        + [(terms, BF16)] * len(near),
        scratch=[
            ((inner, total), F32),
            ((inner, total), F32),
            ((inner, total), BF16),
            ((depth,) + terms, F32),
        ],
        flops=8 * inner * total * width,
    )
    arrived = exchange(dict(zip(masks, sends)))
    grad_queries, leaf, last_part = call(
        functools.partial(late_kernel, heads),
        "late",
        8,
        (),
        (query_rows, cot, raised, weights, joined, ds, keys_t, last_keys),
        [((2, rows, heads * width), BF16), (terms, BF16), (terms, F32)],
        scratch=[((2 * rows, total), BF16), ((2 * rows, total), BF16)],
        flops=8 * 2 * rows * total * width,
    )
    keep, send = call(
        functools.partial(fold_kernel, depth),
        "fold",
        3,
        (),
        (even_part, last_part, *arrived),
        [(terms, F32), (terms, BF16)],
    )
    grad_keys, grad_values = call(
        final_kernel,
        "final",
        2,
        (),
        (leaf, keep, move(send, 1)),
        [(key_states.shape, BF16)] * 2,
    )
    return grad_queries, grad_keys, grad_values


def solution(mesh):
    segments = P(("dp", "leaf"), None, None)
    return jax.shard_map(
        body,
        mesh=mesh,
        in_specs=(segments, segments, segments, segments, P(("dp", "leaf"))),
        out_specs=(segments, segments, segments),
        check_vma=False,
    )
```

```python
import functools

import jax
import jax.numpy as jnp
from jax import lax
from jax.experimental import pallas as pl
from jax.experimental.pallas import tpu as pltpu
from jax.sharding import PartitionSpec as P

BF16 = jnp.bfloat16
F32 = jnp.float32
TAIL = 16
BIG = -1e30
LOG2E = 1.4426950408889634
NT = (((1,), (1,)), ((), ()))
NN = (((1,), (0,)), ((), ()))


def depth_of(count):
    return count.bit_length() - 1


def trailing_zeros(index, depth):
    total = jnp.zeros((), jnp.int32)
    for bit in range(depth):
        total = total + jnp.where((index & ((2 << bit) - 1)) == 0, 1, 0)
    return total


def owner_of(index, level, depth):
    if level == 0:
        return index * 0
    shift = depth - level + 1
    return ((index >> shift) << shift) + (1 << (depth - level))


def level_of_even(index, depth):
    return depth - trailing_zeros(index, depth)


def owner_at(index, level, depth):
    owner = owner_of(index, 0, depth)
    for place in range(1, depth + 1):
        owner = jnp.where(level == place, owner_of(index, place, depth), owner)
    return owner


def call(kernel, name, mib, arrays, outs, scratch=(), flops=0):
    vmem = pl.BlockSpec(memory_space=pltpu.VMEM)
    return pl.pallas_call(
        kernel,
        out_shape=[jax.ShapeDtypeStruct(shape, kind) for shape, kind in outs],
        in_specs=[vmem] * len(arrays),
        out_specs=[vmem] * len(outs),
        scratch_shapes=[pltpu.VMEM(shape, kind) for shape, kind in scratch],
        compiler_params=pltpu.CompilerParams(vmem_limit_bytes=mib * 1024 * 1024),
        cost_estimate=pl.CostEstimate(flops=flops, bytes_accessed=1 << 20, transcendentals=0),
        name=name,
    )(*arrays)


def ruled_columns(rows, width):
    lane = lax.broadcasted_iota(jnp.int32, (rows, width), 1)
    row = lax.broadcasted_iota(jnp.int32, (rows, width), 0)
    ruled = jnp.where((lane > row) | (lane == 0), BIG, 0.0).astype(BF16)
    return jnp.concatenate([ruled, ruled], 0)


def mask_columns(length, before, same, rows, width):
    lane = lax.broadcasted_iota(jnp.int32, (rows, width), 1)
    row = lax.broadcasted_iota(jnp.int32, (rows, width), 0)
    column = jnp.where(same & (row > 0), row, -1)
    live = (row.astype(F32) < length) & (before | same)
    column = jnp.where(live, column, 0)
    return jnp.where(lane == column, 1.0, 0.0).astype(BF16)


def block_scores(keys_wide, values, query_wide, cot, factor):
    scores = lax.dot_general(keys_wide, query_wide, NT, preferred_element_type=F32)
    top = jnp.max(scores, axis=0, keepdims=True)
    raised = jnp.exp2((scores - top) * factor)
    total = jnp.sum(raised, axis=0, keepdims=True)
    grad_weights = lax.dot_general(values, cot, NT, preferred_element_type=F32)
    partial = jnp.sum(raised * grad_weights, axis=0, keepdims=True)
    return raised, grad_weights, top, total, partial


def early_kernel(depth, heads, query_ref, grad_ref, held_ref, tails_ref, *refs):
    other_key_ref, other_value_ref, other_tails_ref = refs[:3]
    query_s, cot_s, raised_s, weights_s, stats_s, keys_s = refs[3:]
    rows, width = held_ref.shape[1:]
    index = lax.axis_index("leaf")
    odd = index & 1 == 1
    factor = width ** (-0.5) * LOG2E
    step = 2 * rows
    row = lax.broadcasted_iota(jnp.int32, (rows, width), 0)
    lengths = [tails_ref[segment, 0:1, :].astype(F32) for segment in range(2)]
    length = jnp.where(odd, lengths[0], other_tails_ref[0, 0:1, :].astype(F32))
    keys = [jnp.where(odd, held_ref[0], other_key_ref[0]), held_ref[1]]
    values = [jnp.where(odd, held_ref[2], other_value_ref[0]), held_ref[3]]
    keys_s[:rows, :] = keys[0]
    keys_s[rows:, :] = keys[1]
    yes, no = jnp.full((), True), jnp.full((), False)
    ruled = ruled_columns(rows, width)
    wide = [
        [
            jnp.concatenate([keys[0], mask_columns(length, no, odd, rows, width)], 1),
        ],
        [
            jnp.concatenate([keys[0], mask_columns(length, yes, no, rows, width)], 1),
            jnp.concatenate([keys[1], mask_columns(lengths[1], no, yes, rows, width)], 1),
        ],
    ]
    for segment in range(2):
        live = row.astype(F32) < lengths[segment]
        for pair in range(heads // 2):
            at = (segment * (heads // 2) + pair) * step
            here = slice(at, at + step)
            columns = [slice(h * width, (h + 1) * width) for h in (2 * pair, 2 * pair + 1)]
            query = jnp.concatenate([query_ref[segment, :, c] for c in columns], 0)
            cot = jnp.concatenate(
                [jnp.where(live, grad_ref[segment, :, c], jnp.zeros((), BF16)) for c in columns], 0
            )
            query_s[here, :] = query
            cot_s[here, :] = cot
            query_wide = jnp.concatenate([query, ruled], 1)
            for place in range(1 + segment):
                span = slice(place * rows, (place + 1) * rows)
                raised, grad_weights, top, total, partial = block_scores(
                    wide[segment][place], values[place], query_wide, cot, factor
                )
                raised_s[span, here] = raised
                weights_s[span, here] = grad_weights
                for n, line in enumerate((top, total, partial)):
                    stats_s[3 * place + n : 3 * place + n + 1, here] = line


def middle_kernel(depth, heads, query_s, cot_s, stats_ref, pack_ref, *refs):
    masks = (1 << (depth - 1)) - 1
    near, refs = refs[:masks], refs[masks:]
    ds_s, joined_s, keys_t, part_ref = refs[:4]
    sends, refs = refs[4 : 4 + masks], refs[4 + masks :]
    raised_s, weights_s, low_s, terms_s = refs
    width = pack_ref.shape[1]
    rows = (pack_ref.shape[0] - TAIL) // 2
    index = lax.axis_index("leaf")
    even = index - (index & 1)
    own_level = depth - trailing_zeros(index, depth)
    scale = width ** (-0.5)
    factor = scale * LOG2E
    step = 2 * rows
    yes, no = jnp.full((), True), jnp.full((), False)
    ruled = ruled_columns(rows, width)
    values = []
    wide = [[], []]
    for level in range(depth):
        pick = (even ^ owner_of(even, level, depth)) >> 1
        block = pack_ref[...]
        for mask in range(1, masks + 1):
            block = jnp.where(pick == mask, near[mask - 1][...], block)
        keys = block[:rows]
        values.append(block[rows : 2 * rows])
        length = block[2 * rows : 2 * rows + 1].astype(F32)
        keys_t[:, level * rows : (level + 1) * rows] = keys.T
        inner = mask_columns(length, level < own_level, level == own_level, rows, width)
        outer = mask_columns(length, yes, no, rows, width)
        wide[0].append(jnp.concatenate([keys, inner], 1))
        wide[1].append(jnp.concatenate([keys, outer], 1))

    grad_keys = grad_values = None
    half = heads * rows
    for segment in range(2):
        for pair in range(heads // 2):
            at = (segment * (heads // 2) + pair) * step
            here = slice(at, at + step)
            query, cot = query_s[here, :], cot_s[here, :]
            query_wide = jnp.concatenate([query, ruled], 1)
            tops, totals, partials = [], [], []
            for place in range(1 + segment):
                tops.append(stats_ref[3 * place : 3 * place + 1, here])
                totals.append(stats_ref[3 * place + 1 : 3 * place + 2, here])
                partials.append(stats_ref[3 * place + 2 : 3 * place + 3, here])
            for level in range(depth):
                span = slice(level * rows, (level + 1) * rows)
                raised, grad_weights, top, total, partial = block_scores(
                    wide[segment][level], values[level], query_wide, cot, factor
                )
                raised_s[span, here] = raised
                weights_s[span, here] = grad_weights
                tops.append(top)
                totals.append(total)
                partials.append(partial)
            highest = functools.reduce(jnp.maximum, tops)
            shares = [jnp.exp2((top - highest) * factor) for top in tops]
            total = sum(share * part for share, part in zip(shares, totals))
            inverse = 1.0 / total
            shares = [share * inverse for share in shares]
            delta = sum(share * part for share, part in zip(shares, partials))
            joined_s[0:1, here] = delta
            for place in range(1 + segment):
                joined_s[1 + place : 2 + place, here] = shares[place]
            for level in range(depth):
                span = slice(level * rows, (level + 1) * rows)
                weights = raised_s[span, here] * shares[1 + segment + level]
                low_s[span, here] = weights.astype(BF16)
                ds_s[span, here] = (weights * (weights_s[span, here] - delta)).astype(BF16)
        now = slice(segment * half, (segment + 1) * half)
        more_keys = lax.dot_general(
            ds_s[:, now], query_s[now, :], NN, preferred_element_type=F32
        )
        more_values = lax.dot_general(
            low_s[:, now], cot_s[now, :], NN, preferred_element_type=F32
        )
        grad_keys = more_keys if segment == 0 else grad_keys + more_keys
        grad_values = more_values if segment == 0 else grad_values + more_values
    for level in range(depth):
        span = slice(level * rows, (level + 1) * rows)
        terms_s[level, :rows, :] = grad_keys[span] * scale
        terms_s[level, rows:, :] = grad_values[span]
    part_ref[...] = terms_s[level_of_even(even, depth)]
    for mask, ref in enumerate(sends, 1):
        ref[...] = terms_s[level_of_even(even ^ (mask << 1), depth)].astype(BF16)


def late_kernel(heads, query_s, cot_s, raised_ref, weights_ref, joined_ref, ds_ref, *refs):
    keys_t, keys_s, grad_query_ref, leaf_ref, part_ref, low_s, ds_s = refs
    width = keys_s.shape[1]
    rows = keys_s.shape[0] // 2
    scale = width ** (-0.5)
    step = 2 * rows
    half = heads * rows
    near_t = keys_s[...].T
    for segment in range(2):
        count = (1 + segment) * rows
        for pair in range(heads // 2):
            at = (segment * (heads // 2) + pair) * step
            here = slice(at, at + step)
            delta = joined_ref[0:1, here]
            for place in range(1 + segment):
                span = slice(place * rows, (place + 1) * rows)
                weights = raised_ref[span, here] * joined_ref[1 + place : 2 + place, here]
                low_s[span, here] = weights.astype(BF16)
                ds_s[span, here] = (weights * (weights_ref[span, here] - delta)).astype(BF16)
            grad_query = lax.dot_general(
                keys_t[...], ds_ref[:, here], NN, preferred_element_type=F32
            ) + lax.dot_general(
                near_t[:, :count], ds_s[:count, here], NN, preferred_element_type=F32
            )
            grad_query = (grad_query * scale).astype(BF16).T
            for n in range(2):
                c = slice((2 * pair + n) * width, (2 * pair + n + 1) * width)
                grad_query_ref[segment, :, c] = grad_query[n * rows : (n + 1) * rows]
    part_ref[:rows, :] = scale * lax.dot_general(
        ds_s[:rows, :], query_s[...], NN, preferred_element_type=F32
    )
    part_ref[rows:, :] = lax.dot_general(
        low_s[:rows, :], cot_s[...], NN, preferred_element_type=F32
    )
    leaf_keys = scale * lax.dot_general(
        ds_s[rows:, half:], query_s[half:, :], NN, preferred_element_type=F32
    )
    leaf_values = lax.dot_general(
        low_s[rows:, half:], cot_s[half:, :], NN, preferred_element_type=F32
    )
    leaf_ref[:rows, :] = leaf_keys.astype(BF16)
    leaf_ref[rows:, :] = leaf_values.astype(BF16)


def fold_kernel(depth, even_ref, last_ref, *refs):
    arrived, (keep_ref, send_ref) = refs[:-2], refs[-2:]
    index = lax.axis_index("leaf")
    odd = index & 1 == 1
    even = index - (index & 1)
    level = level_of_even(even, depth)
    total = even_ref[...]
    for mask, ref in enumerate(arrived, 1):
        mine = owner_at(even ^ (mask << 1), level, depth) == even
        total = total + jnp.where(mine, ref[...].astype(F32), 0.0)
    keep_ref[...] = jnp.where(odd, last_ref[...], total)
    send_ref[...] = jnp.where(odd, total, last_ref[...]).astype(BF16)


def final_kernel(leaf_ref, keep_ref, other_ref, keys_ref, values_ref):
    rows = keys_ref.shape[1]
    total = (keep_ref[...] + other_ref[...].astype(F32)).astype(BF16)
    keys_ref[0] = total[:rows]
    values_ref[0] = total[rows:]
    keys_ref[1] = leaf_ref[:rows, :]
    values_ref[1] = leaf_ref[rows:, :]


def body(queries, key_states, value_states, grad_output, lengths):
    count = lax.axis_size("leaf")
    depth = depth_of(count)
    masks = range(1, count // 2)
    rows, width = key_states.shape[1:]
    heads = queries.shape[2] // width
    total = 2 * heads * rows
    inner = depth * rows
    terms = (2 * rows, width)

    def move(block, flip):
        return lax.ppermute(block, "leaf", [(i, i ^ flip) for i in range(count)])

    def exchange(blocks):
        moved = {m: move(blocks[m], m << 1) for m in reversed(masks)}
        return [moved[m] for m in masks]

    other_keys, other_values = move(key_states, 1), move(value_states, 1)
    tails = jnp.broadcast_to(lengths.astype(BF16)[:, None, None], (2, TAIL, width))
    other_tails = move(tails, 1)
    held = jnp.concatenate([key_states, value_states], 0)
    held, other_keys, other_values, other_tails = lax.optimization_barrier(
        (held, other_keys, other_values, other_tails)
    )
    odd = lax.axis_index("leaf") & 1 == 1
    pack = jnp.concatenate(
        [
            jnp.where(odd, other_keys[0], held[0]),
            jnp.where(odd, other_values[0], held[2]),
            jnp.where(odd, other_tails[0], tails[0]),
        ],
        0,
    )
    near = exchange({m: pack for m in masks})
    query_rows, cot, raised, weights, stats, last_keys = call(
        functools.partial(early_kernel, depth, heads),
        "early",
        8,
        (queries, grad_output, held, tails, other_keys, other_values, other_tails),
        [
            ((total, width), BF16),
            ((total, width), BF16),
            ((2 * rows, total), F32),
            ((2 * rows, total), F32),
            ((8, total), F32),
            ((2 * rows, width), BF16),
        ],
        flops=4 * 2 * rows * total * width,
    )
    ds, joined, keys_t, even_part, *sends = call(
        functools.partial(middle_kernel, depth, heads),
        "middle",
        24,
        (query_rows, cot, stats, pack, *near),
        [
            ((inner, total), BF16),
            ((8, total), F32),
            ((width, inner), BF16),
            (terms, F32),
        ]
        + [(terms, BF16)] * len(near),
        scratch=[
            ((inner, total), F32),
            ((inner, total), F32),
            ((inner, total), BF16),
            ((depth,) + terms, F32),
        ],
        flops=8 * inner * total * width,
    )
    arrived = exchange(dict(zip(masks, sends)))
    grad_queries, leaf, last_part = call(
        functools.partial(late_kernel, heads),
        "late",
        8,
        (query_rows, cot, raised, weights, joined, ds, keys_t, last_keys),
        [((2, rows, heads * width), BF16), (terms, BF16), (terms, F32)],
        scratch=[((2 * rows, total), BF16), ((2 * rows, total), BF16)],
        flops=8 * 2 * rows * total * width,
    )
    keep, send = call(
        functools.partial(fold_kernel, depth),
        "fold",
        3,
        (even_part, last_part, *arrived),
        [(terms, F32), (terms, BF16)],
    )
    grad_keys, grad_values = call(
        final_kernel,
        "final",
        2,
        (leaf, keep, move(send, 1)),
        [(key_states.shape, BF16)] * 2,
    )
    return grad_queries, grad_keys, grad_values


def solution(mesh):
    segments = P(("dp", "leaf"), None, None)
    return jax.shard_map(
        body,
        mesh=mesh,
        in_specs=(segments, segments, segments, segments, P(("dp", "leaf"))),
        out_specs=(segments, segments, segments),
        check_vma=False,
    )
```

```python
import functools

import jax
import jax.numpy as jnp
from jax import lax
from jax.experimental import pallas as pl
from jax.experimental.pallas import tpu as pltpu
from jax.sharding import PartitionSpec as P

BF16 = jnp.bfloat16
F32 = jnp.float32
TAIL = 16
BIG = -1e30
LOG2E = 1.4426950408889634
NT = (((1,), (1,)), ((), ()))
NN = (((1,), (0,)), ((), ()))


def depth_of(count):
    return count.bit_length() - 1


def trailing_zeros(index, depth):
    total = jnp.zeros((), jnp.int32)
    for bit in range(depth):
        total = total + jnp.where((index & ((2 << bit) - 1)) == 0, 1, 0)
    return total


def owner_of(index, level, depth):
    if level == 0:
        return index * 0
    shift = depth - level + 1
    return ((index >> shift) << shift) + (1 << (depth - level))


def level_of_even(index, depth):
    return depth - trailing_zeros(index, depth)


def owner_at(index, level, depth):
    owner = owner_of(index, 0, depth)
    for place in range(1, depth + 1):
        owner = jnp.where(level == place, owner_of(index, place, depth), owner)
    return owner


def call(kernel, name, mib, arrays, outs, scratch=(), flops=0):
    vmem = pl.BlockSpec(memory_space=pltpu.VMEM)
    return pl.pallas_call(
        kernel,
        out_shape=[jax.ShapeDtypeStruct(shape, kind) for shape, kind in outs],
        in_specs=[vmem] * len(arrays),
        out_specs=[vmem] * len(outs),
        scratch_shapes=[pltpu.VMEM(shape, kind) for shape, kind in scratch],
        compiler_params=pltpu.CompilerParams(vmem_limit_bytes=mib * 1024 * 1024),
        cost_estimate=pl.CostEstimate(flops=flops, bytes_accessed=1 << 20, transcendentals=0),
        name=name,
    )(*arrays)


def ruled_columns(rows, width):
    lane = lax.broadcasted_iota(jnp.int32, (rows, width), 1)
    row = lax.broadcasted_iota(jnp.int32, (rows, width), 0)
    ruled = jnp.where((lane > row) | (lane == 0), BIG, 0.0).astype(BF16)
    return jnp.concatenate([ruled, ruled], 0)


def mask_columns(length, before, same, rows, width):
    lane = lax.broadcasted_iota(jnp.int32, (rows, width), 1)
    row = lax.broadcasted_iota(jnp.int32, (rows, width), 0)
    column = jnp.where(same & (row > 0), row, -1)
    live = (row.astype(F32) < length) & (before | same)
    column = jnp.where(live, column, 0)
    return jnp.where(lane == column, 1.0, 0.0).astype(BF16)


def block_scores(keys_wide, values, query_wide, cot, factor):
    scores = lax.dot_general(keys_wide, query_wide, NT, preferred_element_type=F32)
    top = jnp.max(scores, axis=0, keepdims=True)
    raised = jnp.exp2((scores - top) * factor)
    total = jnp.sum(raised, axis=0, keepdims=True)
    grad_weights = lax.dot_general(values, cot, NT, preferred_element_type=F32)
    partial = jnp.sum(raised * grad_weights, axis=0, keepdims=True)
    return raised, grad_weights, top, total, partial


def early_kernel(depth, heads, query_ref, grad_ref, held_ref, tails_ref, *refs):
    other_key_ref, other_value_ref, other_tails_ref = refs[:3]
    query_s, cot_s, raised_s, weights_s, stats_s, keys_s = refs[3:]
    rows, width = held_ref.shape[1:]
    index = lax.axis_index("leaf")
    odd = index & 1 == 1
    factor = width ** (-0.5) * LOG2E
    step = 2 * rows
    row = lax.broadcasted_iota(jnp.int32, (rows, width), 0)
    lengths = [tails_ref[segment, 0:1, :].astype(F32) for segment in range(2)]
    length = jnp.where(odd, lengths[0], other_tails_ref[0, 0:1, :].astype(F32))
    keys = [jnp.where(odd, held_ref[0], other_key_ref[0]), held_ref[1]]
    values = [jnp.where(odd, held_ref[2], other_value_ref[0]), held_ref[3]]
    keys_s[:rows, :] = keys[0]
    keys_s[rows:, :] = keys[1]
    yes, no = jnp.full((), True), jnp.full((), False)
    ruled = ruled_columns(rows, width)
    wide = [
        [
            jnp.concatenate([keys[0], mask_columns(length, no, odd, rows, width)], 1),
        ],
        [
            jnp.concatenate([keys[0], mask_columns(length, yes, no, rows, width)], 1),
            jnp.concatenate([keys[1], mask_columns(lengths[1], no, yes, rows, width)], 1),
        ],
    ]
    for segment in range(2):
        live = row.astype(F32) < lengths[segment]
        for pair in range(heads // 2):
            at = (segment * (heads // 2) + pair) * step
            here = slice(at, at + step)
            columns = [slice(h * width, (h + 1) * width) for h in (2 * pair, 2 * pair + 1)]
            query = jnp.concatenate([query_ref[segment, :, c] for c in columns], 0)
            cot = jnp.concatenate(
                [jnp.where(live, grad_ref[segment, :, c], jnp.zeros((), BF16)) for c in columns], 0
            )
            query_s[here, :] = query
            cot_s[here, :] = cot
            query_wide = jnp.concatenate([query, ruled], 1)
            for place in range(1 + segment):
                span = slice(place * rows, (place + 1) * rows)
                raised, grad_weights, top, total, partial = block_scores(
                    wide[segment][place], values[place], query_wide, cot, factor
                )
                raised_s[span, here] = raised
                weights_s[span, here] = grad_weights
                for n, line in enumerate((top, total, partial)):
                    stats_s[3 * place + n : 3 * place + n + 1, here] = line


def middle_kernel(depth, heads, query_s, cot_s, stats_ref, pack_ref, *refs):
    masks = (1 << (depth - 1)) - 1
    near, refs = refs[:masks], refs[masks:]
    ds_s, joined_s, keys_t, part_ref = refs[:4]
    sends, refs = refs[4:-4], refs[-4:]
    raised_s, weights_s, low_s, terms_s = refs
    width = pack_ref.shape[1]
    rows = (pack_ref.shape[0] - TAIL) // 2
    index = lax.axis_index("leaf")
    even = index - (index & 1)
    own_level = depth - trailing_zeros(index, depth)
    scale = width ** (-0.5)
    factor = scale * LOG2E
    step = 2 * rows
    yes, no = jnp.full((), True), jnp.full((), False)
    ruled = ruled_columns(rows, width)
    values = []
    wide = [[], []]
    for level in range(depth):
        pick = (even ^ owner_of(even, level, depth)) >> 1
        block = pack_ref[...]
        for mask in range(1, masks + 1):
            block = jnp.where(pick == mask, near[mask - 1][...], block)
        keys = block[:rows]
        values.append(block[rows : 2 * rows])
        length = block[2 * rows : 2 * rows + 1].astype(F32)
        keys_t[:, level * rows : (level + 1) * rows] = keys.T
        inner = mask_columns(length, level < own_level, level == own_level, rows, width)
        outer = mask_columns(length, yes, no, rows, width)
        wide[0].append(jnp.concatenate([keys, inner], 1))
        wide[1].append(jnp.concatenate([keys, outer], 1))

    grad_keys = grad_values = None
    half = heads * rows
    for segment in range(2):
        for pair in range(heads // 2):
            at = (segment * (heads // 2) + pair) * step
            here = slice(at, at + step)
            query, cot = query_s[here, :], cot_s[here, :]
            query_wide = jnp.concatenate([query, ruled], 1)
            tops, totals, partials = [], [], []
            for place in range(1 + segment):
                tops.append(stats_ref[3 * place : 3 * place + 1, here])
                totals.append(stats_ref[3 * place + 1 : 3 * place + 2, here])
                partials.append(stats_ref[3 * place + 2 : 3 * place + 3, here])
            for level in range(depth):
                span = slice(level * rows, (level + 1) * rows)
                raised, grad_weights, top, total, partial = block_scores(
                    wide[segment][level], values[level], query_wide, cot, factor
                )
                raised_s[span, here] = raised
                weights_s[span, here] = grad_weights
                tops.append(top)
                totals.append(total)
                partials.append(partial)
            highest = functools.reduce(jnp.maximum, tops)
            shares = [jnp.exp2((top - highest) * factor) for top in tops]
            total = sum(share * part for share, part in zip(shares, totals))
            inverse = 1.0 / total
            shares = [share * inverse for share in shares]
            delta = sum(share * part for share, part in zip(shares, partials))
            joined_s[0:1, here] = delta
            for place in range(1 + segment):
                joined_s[1 + place : 2 + place, here] = shares[place]
            for level in range(depth):
                span = slice(level * rows, (level + 1) * rows)
                weights = raised_s[span, here] * shares[1 + segment + level]
                low_s[span, here] = weights.astype(BF16)
                ds_s[span, here] = (weights * (weights_s[span, here] - delta)).astype(BF16)
        now = slice(segment * half, (segment + 1) * half)
        more_keys = lax.dot_general(
            ds_s[:, now], query_s[now, :], NN, preferred_element_type=F32
        )
        more_values = lax.dot_general(
            low_s[:, now], cot_s[now, :], NN, preferred_element_type=F32
        )
        grad_keys = more_keys if segment == 0 else grad_keys + more_keys
        grad_values = more_values if segment == 0 else grad_values + more_values
    for level in range(depth):
        span = slice(level * rows, (level + 1) * rows)
        terms_s[level, :rows, :] = grad_keys[span] * scale
        terms_s[level, rows:, :] = grad_values[span]
    part_ref[...] = terms_s[level_of_even(even, depth)]
    if depth == 3:
        odd, straight, across = leaving_levels(index)
        swap_ref, hold_ref = sends
        mine, theirs = jnp.where(odd, across, straight), jnp.where(odd, straight, across)
        diagonal = terms_s[straight]
        first, second = diagonal[:rows], diagonal[rows:]
        hold_ref[: 2 * rows, :] = terms_s[mine]
        hold_ref[2 * rows :, :] = jnp.where(odd, second, first)
        swap_ref[: 2 * rows, :] = terms_s[theirs].astype(BF16)
        swap_ref[2 * rows :, :] = jnp.where(odd, first, second).astype(BF16)
        return
    for mask, ref in enumerate(sends, 1):
        ref[...] = terms_s[level_of_even(even ^ (mask << 1), depth)].astype(BF16)


def late_kernel(heads, query_s, cot_s, raised_ref, weights_ref, joined_ref, ds_ref, *refs):
    keys_t, keys_s, grad_query_ref, leaf_ref, part_ref, low_s, ds_s = refs
    width = keys_s.shape[1]
    rows = keys_s.shape[0] // 2
    scale = width ** (-0.5)
    step = 2 * rows
    half = heads * rows
    near_t = keys_s[...].T
    for segment in range(2):
        count = (1 + segment) * rows
        for pair in range(heads // 2):
            at = (segment * (heads // 2) + pair) * step
            here = slice(at, at + step)
            delta = joined_ref[0:1, here]
            for place in range(1 + segment):
                span = slice(place * rows, (place + 1) * rows)
                weights = raised_ref[span, here] * joined_ref[1 + place : 2 + place, here]
                low_s[span, here] = weights.astype(BF16)
                ds_s[span, here] = (weights * (weights_ref[span, here] - delta)).astype(BF16)
            grad_query = lax.dot_general(
                keys_t[...], ds_ref[:, here], NN, preferred_element_type=F32
            ) + lax.dot_general(
                near_t[:, :count], ds_s[:count, here], NN, preferred_element_type=F32
            )
            grad_query = (grad_query * scale).astype(BF16).T
            for n in range(2):
                c = slice((2 * pair + n) * width, (2 * pair + n + 1) * width)
                grad_query_ref[segment, :, c] = grad_query[n * rows : (n + 1) * rows]
    part_ref[:rows, :] = scale * lax.dot_general(
        ds_s[:rows, :], query_s[...], NN, preferred_element_type=F32
    )
    part_ref[rows:, :] = lax.dot_general(
        low_s[:rows, :], cot_s[...], NN, preferred_element_type=F32
    )
    leaf_keys = scale * lax.dot_general(
        ds_s[rows:, half:], query_s[half:, :], NN, preferred_element_type=F32
    )
    leaf_values = lax.dot_general(
        low_s[rows:, half:], cot_s[half:, :], NN, preferred_element_type=F32
    )
    leaf_ref[:rows, :] = leaf_keys.astype(BF16)
    leaf_ref[rows:, :] = leaf_values.astype(BF16)


def leaving_levels(index):
    x, y = (index >> 1) & 1, (index >> 2) & 1
    return index & 1 == 1, 1 - y, jnp.where(x == 1, y, 2)


def pair_kernel(hold_ref, other_ref, send_ref, diagonal_ref):
    cut = send_ref.shape[0]
    both = (hold_ref[...] + other_ref[...].astype(F32)).astype(BF16)
    send_ref[...] = both[:cut]
    diagonal_ref[...] = both[cut:]


def gather_kernel(even_ref, last_ref, arrived_ref, diagonal_ref, keep_ref, send_ref):
    rows = diagonal_ref.shape[0]
    index = lax.axis_index("leaf")
    odd, near = index & 1 == 1, (index >> 1) & 1 == 0
    total = even_ref[...] + jnp.where(odd | near, arrived_ref[...].astype(F32), 0.0)
    half = jnp.where(near, diagonal_ref[...].astype(F32), 0.0)
    first = total[:rows] + jnp.where(odd, 0.0, half)
    second = total[rows:] + jnp.where(odd, half, 0.0)
    total = jnp.concatenate([first, second], 0)
    keep_ref[...] = jnp.where(odd, last_ref[...], total)
    send_ref[...] = jnp.where(odd, total, last_ref[...]).astype(BF16)


def fold_kernel(depth, even_ref, last_ref, *refs):
    arrived, (keep_ref, send_ref) = refs[:-2], refs[-2:]
    index = lax.axis_index("leaf")
    odd = index & 1 == 1
    even = index - (index & 1)
    level = level_of_even(even, depth)
    total = even_ref[...]
    for mask, ref in enumerate(arrived, 1):
        mine = owner_at(even ^ (mask << 1), level, depth) == even
        total = total + jnp.where(mine, ref[...].astype(F32), 0.0)
    keep_ref[...] = jnp.where(odd, last_ref[...], total)
    send_ref[...] = jnp.where(odd, total, last_ref[...]).astype(BF16)


def final_kernel(leaf_ref, keep_ref, other_ref, keys_ref, values_ref):
    rows = keys_ref.shape[1]
    total = (keep_ref[...] + other_ref[...].astype(F32)).astype(BF16)
    keys_ref[0] = total[:rows]
    values_ref[0] = total[rows:]
    keys_ref[1] = leaf_ref[:rows, :]
    values_ref[1] = leaf_ref[rows:, :]


def body(queries, key_states, value_states, grad_output, lengths):
    count = lax.axis_size("leaf")
    depth = depth_of(count)
    masks = range(1, count // 2)
    rows, width = key_states.shape[1:]
    heads = queries.shape[2] // width
    total = 2 * heads * rows
    inner = depth * rows
    terms = (2 * rows, width)

    def move(block, flip, odd_flip=None):
        flips = (flip, flip if odd_flip is None else odd_flip)
        return lax.ppermute(block, "leaf", [(i, i ^ flips[i & 1]) for i in range(count)])

    def exchange(blocks):
        moved = {m: move(blocks[m], m << 1) for m in reversed(masks)}
        return [moved[m] for m in masks]

    other_keys, other_values = move(key_states, 1), move(value_states, 1)
    tails = jnp.broadcast_to(lengths.astype(BF16)[:, None, None], (2, TAIL, width))
    other_tails = move(tails, 1)
    held = jnp.concatenate([key_states, value_states], 0)
    held, other_keys, other_values, other_tails = lax.optimization_barrier(
        (held, other_keys, other_values, other_tails)
    )
    odd = lax.axis_index("leaf") & 1 == 1
    pack = jnp.concatenate(
        [
            jnp.where(odd, other_keys[0], held[0]),
            jnp.where(odd, other_values[0], held[2]),
            jnp.where(odd, other_tails[0], tails[0]),
        ],
        0,
    )
    near = exchange({m: pack for m in masks})
    query_rows, cot, raised, weights, stats, last_keys = call(
        functools.partial(early_kernel, depth, heads),
        "early",
        8,
        (queries, grad_output, held, tails, other_keys, other_values, other_tails),
        [
            ((total, width), BF16),
            ((total, width), BF16),
            ((2 * rows, total), F32),
            ((2 * rows, total), F32),
            ((8, total), F32),
            ((2 * rows, width), BF16),
        ],
        flops=4 * 2 * rows * total * width,
    )
    if depth == 3:
        leaving = [((3 * rows, width), BF16), ((3 * rows, width), F32)]
    else:
        leaving = [(terms, BF16)] * len(near)
    ds, joined, keys_t, even_part, *sends = call(
        functools.partial(middle_kernel, depth, heads),
        "middle",
        24,
        (query_rows, cot, stats, pack, *near),
        [
            ((inner, total), BF16),
            ((8, total), F32),
            ((width, inner), BF16),
            (terms, F32),
        ]
        + leaving,
        scratch=[
            ((inner, total), F32),
            ((inner, total), F32),
            ((inner, total), BF16),
            ((depth,) + terms, F32),
        ],
        flops=8 * inner * total * width,
    )
    if depth == 3:
        swap, hold = sends
        send, diagonal = call(
            pair_kernel, "pair", 2, (hold, move(swap, 1)), [(terms, BF16), ((rows, width), BF16)]
        )
        diagonal = move(diagonal, 6)
        arrived = [move(send, 4, 2), diagonal]
        fold = gather_kernel
    else:
        arrived = exchange(dict(zip(masks, sends)))
        fold = functools.partial(fold_kernel, depth)
    grad_queries, leaf, last_part = call(
        functools.partial(late_kernel, heads),
        "late",
        8,
        (query_rows, cot, raised, weights, joined, ds, keys_t, last_keys),
        [((2, rows, heads * width), BF16), (terms, BF16), (terms, F32)],
        scratch=[((2 * rows, total), BF16), ((2 * rows, total), BF16)],
        flops=8 * 2 * rows * total * width,
    )
    keep, send = call(
        fold,
        "fold",
        3,
        (even_part, last_part, *arrived),
        [(terms, F32), (terms, BF16)],
    )
    grad_keys, grad_values = call(
        final_kernel,
        "final",
        2,
        (leaf, keep, move(send, 1)),
        [(key_states.shape, BF16)] * 2,
    )
    return grad_queries, grad_keys, grad_values


def solution(mesh):
    segments = P(("dp", "leaf"), None, None)
    return jax.shard_map(
        body,
        mesh=mesh,
        in_specs=(segments, segments, segments, segments, P(("dp", "leaf"))),
        out_specs=(segments, segments, segments),
        check_vma=False,
    )
```

```python
import functools

import jax
import jax.numpy as jnp
from jax import lax
from jax.experimental import pallas as pl
from jax.experimental.pallas import tpu as pltpu
from jax.sharding import PartitionSpec as P

BF16 = jnp.bfloat16
F32 = jnp.float32
LOCAL = 3
TAIL = 16
BIG = -1e30
LOG2E = 1.4426950408889634
NT = (((1,), (1,)), ((), ()))
NN = (((1,), (0,)), ((), ()))


def depth_of(count):
    return count.bit_length() - 1


def trailing_zeros(index, depth):
    total = jnp.zeros((), jnp.int32)
    for bit in range(depth):
        total = total + jnp.where((index & ((2 << bit) - 1)) == 0, 1, 0)
    return total


def owner_of(index, level, depth):
    if level == 0:
        return index * 0
    shift = depth - level + 1
    return ((index >> shift) << shift) + (1 << (depth - level))


def level_of_even(index, depth):
    return depth - trailing_zeros(index, depth)


def owner_at(index, level, depth):
    owner = owner_of(index, 0, depth)
    for place in range(1, depth + 1):
        owner = jnp.where(level == place, owner_of(index, place, depth), owner)
    return owner


def call(kernel, name, mib, arrays, outs, scratch=(), flops=0):
    vmem = pl.BlockSpec(memory_space=pltpu.VMEM)
    return pl.pallas_call(
        kernel,
        out_shape=[jax.ShapeDtypeStruct(shape, kind) for shape, kind in outs],
        in_specs=[vmem] * len(arrays),
        out_specs=[vmem] * len(outs),
        scratch_shapes=[pltpu.VMEM(shape, kind) for shape, kind in scratch],
        compiler_params=pltpu.CompilerParams(vmem_limit_bytes=mib * 1024 * 1024),
        cost_estimate=pl.CostEstimate(flops=flops, bytes_accessed=1 << 20, transcendentals=0),
        name=name,
    )(*arrays)


def ruled_columns(rows, width):
    lane = lax.broadcasted_iota(jnp.int32, (rows, width), 1)
    row = lax.broadcasted_iota(jnp.int32, (rows, width), 0)
    ruled = jnp.where((lane > row) | (lane == 0), BIG, 0.0).astype(BF16)
    return jnp.concatenate([ruled, ruled], 0)


def mask_columns(length, before, same, rows, width):
    lane = lax.broadcasted_iota(jnp.int32, (rows, width), 1)
    row = lax.broadcasted_iota(jnp.int32, (rows, width), 0)
    column = jnp.where(same & (row > 0), row, -1)
    live = (row.astype(F32) < length) & (before | same)
    column = jnp.where(live, column, 0)
    return jnp.where(lane == column, 1.0, 0.0).astype(BF16)


def block_scores(keys_wide, values, query_wide, cot, factor):
    scores = lax.dot_general(keys_wide, query_wide, NT, preferred_element_type=F32)
    top = jnp.max(scores, axis=0, keepdims=True)
    raised = jnp.exp2((scores - top) * factor)
    total = jnp.sum(raised, axis=0, keepdims=True)
    grad_weights = lax.dot_general(values, cot, NT, preferred_element_type=F32)
    partial = jnp.sum(raised * grad_weights, axis=0, keepdims=True)
    return raised, grad_weights, top, total, partial


def early_kernel(depth, heads, query_ref, grad_ref, held_ref, tails_ref, *refs):
    other_key_ref, other_value_ref, other_tails_ref, pack_ref = refs[:4]
    query_s, cot_s, raised_s, weights_s, stats_s, keys_s = refs[4:]
    rows, width = held_ref.shape[1:]
    index = lax.axis_index("leaf")
    odd = index & 1 == 1
    factor = width ** (-0.5) * LOG2E
    step = 2 * rows
    row = lax.broadcasted_iota(jnp.int32, (rows, width), 0)
    lengths = [tails_ref[segment, 0:1, :].astype(F32) for segment in range(2)]
    length = jnp.where(odd, lengths[0], other_tails_ref[0, 0:1, :].astype(F32))
    even_length = pack_ref[2 * rows : 2 * rows + 1, :].astype(F32)
    last_keys = jnp.where(odd, held_ref[0], other_key_ref[0])
    last_values = jnp.where(odd, held_ref[2], other_value_ref[0])
    keys = [last_keys, pack_ref[:rows, :], held_ref[1]]
    values = [last_values, pack_ref[rows : 2 * rows, :], held_ref[3]]
    yes, no = jnp.full((), True), jnp.full((), False)
    masks = [
        [(length, no, odd), (even_length, odd, ~odd)],
        [(length, yes, no), (even_length, yes, no), (lengths[1], no, yes)],
    ]
    wide = [
        [
            jnp.concatenate([block, mask_columns(*mask, rows, width)], 1)
            for block, mask in zip(keys, masks[segment])
        ]
        for segment in range(2)
    ]
    for place in range(LOCAL):
        keys_s[place * rows : (place + 1) * rows, :] = keys[place]
    ruled = ruled_columns(rows, width)
    for segment in range(2):
        live = row.astype(F32) < lengths[segment]
        for pair in range(heads // 2):
            at = (segment * (heads // 2) + pair) * step
            here = slice(at, at + step)
            columns = [slice(h * width, (h + 1) * width) for h in (2 * pair, 2 * pair + 1)]
            query = jnp.concatenate([query_ref[segment, :, c] for c in columns], 0)
            cot = jnp.concatenate(
                [jnp.where(live, grad_ref[segment, :, c], jnp.zeros((), BF16)) for c in columns], 0
            )
            query_s[here, :] = query
            cot_s[here, :] = cot
            query_wide = jnp.concatenate([query, ruled], 1)
            for place in range(LOCAL - 1 + segment):
                span = slice(place * rows, (place + 1) * rows)
                raised, grad_weights, top, total, partial = block_scores(
                    wide[segment][place], values[place], query_wide, cot, factor
                )
                raised_s[span, here] = raised
                weights_s[span, here] = grad_weights
                for n, line in enumerate((top, total, partial)):
                    stats_s[3 * place + n : 3 * place + n + 1, here] = line


def middle_kernel(depth, heads, query_s, cot_s, stats_ref, pack_ref, *refs):
    masks = (1 << (depth - 1)) - 1
    near, refs = refs[:masks], refs[masks:]
    ds_s, joined_s, keys_t = refs[:3]
    sends, refs = refs[3:-4], refs[-4:]
    raised_s, weights_s, low_s, terms_s = refs
    width = pack_ref.shape[1]
    rows = (pack_ref.shape[0] - TAIL) // 2
    index = lax.axis_index("leaf")
    even = index - (index & 1)
    own_level = depth - trailing_zeros(index, depth)
    scale = width ** (-0.5)
    factor = scale * LOG2E
    step = 2 * rows
    yes, no = jnp.full((), True), jnp.full((), False)
    ruled = ruled_columns(rows, width)
    values = []
    wide = [[], []]
    if depth == 3:
        far = (index >> 1) & 1 == 1
        _, straight, across = leaving_levels(index)
        remote = [
            (straight, jnp.where(far, near[0][...], near[1][...])),
            (across, near[2][...]),
        ]
    else:
        remote = []
        for place in range(depth - 1):
            level = place + jnp.where(place < level_of_even(even, depth), 0, 1)
            pick = (even ^ owner_at(even, level, depth)) >> 1
            block = pack_ref[...]
            for mask in range(1, masks + 1):
                block = jnp.where(pick == mask, near[mask - 1][...], block)
            remote.append((level, block))
    for place, (level, block) in enumerate(remote):
        keys = block[:rows]
        values.append(block[rows : 2 * rows])
        length = block[2 * rows : 2 * rows + 1].astype(F32)
        keys_t[:, place * rows : (place + 1) * rows] = keys.T
        inner = mask_columns(length, level < own_level, level == own_level, rows, width)
        outer = mask_columns(length, yes, no, rows, width)
        wide[0].append(jnp.concatenate([keys, inner], 1))
        wide[1].append(jnp.concatenate([keys, outer], 1))

    grad_keys = grad_values = None
    half = heads * rows
    for segment in range(2):
        for pair in range(heads // 2):
            at = (segment * (heads // 2) + pair) * step
            here = slice(at, at + step)
            query, cot = query_s[here, :], cot_s[here, :]
            query_wide = jnp.concatenate([query, ruled], 1)
            tops, totals, partials = [], [], []
            local = LOCAL - 1 + segment
            for place in range(local):
                tops.append(stats_ref[3 * place : 3 * place + 1, here])
                totals.append(stats_ref[3 * place + 1 : 3 * place + 2, here])
                partials.append(stats_ref[3 * place + 2 : 3 * place + 3, here])
            for place in range(len(remote)):
                span = slice(place * rows, (place + 1) * rows)
                raised, grad_weights, top, total, partial = block_scores(
                    wide[segment][place], values[place], query_wide, cot, factor
                )
                raised_s[span, here] = raised
                weights_s[span, here] = grad_weights
                tops.append(top)
                totals.append(total)
                partials.append(partial)
            highest = functools.reduce(jnp.maximum, tops)
            shares = [jnp.exp2((top - highest) * factor) for top in tops]
            total = sum(share * part for share, part in zip(shares, totals))
            inverse = 1.0 / total
            shares = [share * inverse for share in shares]
            delta = sum(share * part for share, part in zip(shares, partials))
            joined_s[0:1, here] = delta
            for place in range(local):
                joined_s[1 + place : 2 + place, here] = shares[place]
            for place in range(len(remote)):
                span = slice(place * rows, (place + 1) * rows)
                weights = raised_s[span, here] * shares[local + place]
                low_s[span, here] = weights.astype(BF16)
                ds_s[span, here] = (weights * (weights_s[span, here] - delta)).astype(BF16)
        now = slice(segment * half, (segment + 1) * half)
        more_keys = lax.dot_general(
            ds_s[:, now], query_s[now, :], NN, preferred_element_type=F32
        )
        more_values = lax.dot_general(
            low_s[:, now], cot_s[now, :], NN, preferred_element_type=F32
        )
        grad_keys = more_keys if segment == 0 else grad_keys + more_keys
        grad_values = more_values if segment == 0 else grad_values + more_values
    for place in range(len(remote)):
        span = slice(place * rows, (place + 1) * rows)
        terms_s[place, :rows, :] = grad_keys[span] * scale
        terms_s[place, rows:, :] = grad_values[span]
    if depth == 3:
        odd = index & 1 == 1
        swap_ref, hold_ref = sends
        mine, theirs = jnp.where(odd, 1, 0), jnp.where(odd, 0, 1)
        first, second = terms_s[0, :rows, :], terms_s[0, rows:, :]
        hold_ref[: 2 * rows, :] = terms_s[mine]
        hold_ref[2 * rows :, :] = jnp.where(odd, second, first)
        swap_ref[: 2 * rows, :] = terms_s[theirs].astype(BF16)
        swap_ref[2 * rows :, :] = jnp.where(odd, first, second).astype(BF16)
        return
    for mask, ref in enumerate(sends, 1):
        level = level_of_even(even ^ (mask << 1), depth)
        place = level - jnp.where(level < level_of_even(even, depth), 0, 1)
        ref[...] = terms_s[jnp.clip(place, 0, depth - 2)].astype(BF16)


def late_kernel(heads, query_s, cot_s, raised_ref, weights_ref, joined_ref, ds_ref, *refs):
    keys_t, keys_s, grad_query_ref, leaf_ref, last_ref, even_ref, low_s, ds_s = refs
    width = keys_s.shape[1]
    rows = keys_s.shape[0] // LOCAL
    scale = width ** (-0.5)
    step = 2 * rows
    half = heads * rows
    near_t = keys_s[...].T
    for segment in range(2):
        count = (LOCAL - 1 + segment) * rows
        for pair in range(heads // 2):
            at = (segment * (heads // 2) + pair) * step
            here = slice(at, at + step)
            delta = joined_ref[0:1, here]
            for place in range(LOCAL - 1 + segment):
                span = slice(place * rows, (place + 1) * rows)
                weights = raised_ref[span, here] * joined_ref[1 + place : 2 + place, here]
                low_s[span, here] = weights.astype(BF16)
                ds_s[span, here] = (weights * (weights_ref[span, here] - delta)).astype(BF16)
            grad_query = lax.dot_general(
                keys_t[...], ds_ref[:, here], NN, preferred_element_type=F32
            ) + lax.dot_general(
                near_t[:, :count], ds_s[:count, here], NN, preferred_element_type=F32
            )
            grad_query = (grad_query * scale).astype(BF16).T
            for n in range(2):
                c = slice((2 * pair + n) * width, (2 * pair + n + 1) * width)
                grad_query_ref[segment, :, c] = grad_query[n * rows : (n + 1) * rows]
    inner = (LOCAL - 1) * rows
    grad_keys = scale * lax.dot_general(
        ds_s[:inner, :], query_s[...], NN, preferred_element_type=F32
    )
    grad_values = lax.dot_general(
        low_s[:inner, :], cot_s[...], NN, preferred_element_type=F32
    )
    for place, ref in enumerate((last_ref, even_ref)):
        span = slice(place * rows, (place + 1) * rows)
        ref[:rows, :] = grad_keys[span]
        ref[rows:, :] = grad_values[span]
    leaf_keys = scale * lax.dot_general(
        ds_s[inner:, half:], query_s[half:, :], NN, preferred_element_type=F32
    )
    leaf_values = lax.dot_general(
        low_s[inner:, half:], cot_s[half:, :], NN, preferred_element_type=F32
    )
    leaf_ref[:rows, :] = leaf_keys.astype(BF16)
    leaf_ref[rows:, :] = leaf_values.astype(BF16)


def leaving_levels(index):
    x, y = (index >> 1) & 1, (index >> 2) & 1
    return index & 1 == 1, 1 - y, jnp.where(x == 1, y, 2)


def pair_kernel(first, hold_ref, other_ref, after_ref, out_ref):
    span = slice(first, first + out_ref.shape[0])
    out_ref[...] = (hold_ref[span, :] + other_ref[span, :].astype(F32)).astype(BF16)


def gather_kernel(even_ref, last_ref, arrived_ref, diagonal_ref, keep_ref, send_ref):
    rows = diagonal_ref.shape[0]
    index = lax.axis_index("leaf")
    odd, near = index & 1 == 1, (index >> 1) & 1 == 0
    total = even_ref[...] + jnp.where(odd | near, arrived_ref[...].astype(F32), 0.0)
    half = jnp.where(near, diagonal_ref[...].astype(F32), 0.0)
    first = total[:rows] + jnp.where(odd, 0.0, half)
    second = total[rows:] + jnp.where(odd, half, 0.0)
    total = jnp.concatenate([first, second], 0)
    keep_ref[...] = jnp.where(odd, last_ref[...], total)
    send_ref[...] = jnp.where(odd, total, last_ref[...]).astype(BF16)


def fold_kernel(depth, even_ref, last_ref, *refs):
    arrived, (keep_ref, send_ref) = refs[:-2], refs[-2:]
    index = lax.axis_index("leaf")
    odd = index & 1 == 1
    even = index - (index & 1)
    level = level_of_even(even, depth)
    total = even_ref[...]
    for mask, ref in enumerate(arrived, 1):
        mine = owner_at(even ^ (mask << 1), level, depth) == even
        total = total + jnp.where(mine, ref[...].astype(F32), 0.0)
    keep_ref[...] = jnp.where(odd, last_ref[...], total)
    send_ref[...] = jnp.where(odd, total, last_ref[...]).astype(BF16)


def final_kernel(leaf_ref, keep_ref, other_ref, keys_ref, values_ref):
    rows = keys_ref.shape[1]
    total = (keep_ref[...] + other_ref[...].astype(F32)).astype(BF16)
    keys_ref[0] = total[:rows]
    values_ref[0] = total[rows:]
    keys_ref[1] = leaf_ref[:rows, :]
    values_ref[1] = leaf_ref[rows:, :]


def body(queries, key_states, value_states, grad_output, lengths):
    count = lax.axis_size("leaf")
    depth = depth_of(count)
    masks = range(1, count // 2)
    rows, width = key_states.shape[1:]
    heads = queries.shape[2] // width
    total = 2 * heads * rows
    local = LOCAL * rows
    inner = (depth - 1) * rows
    terms = (2 * rows, width)

    def move(block, flip, odd_flip=None):
        flips = (flip, flip if odd_flip is None else odd_flip)
        return lax.ppermute(block, "leaf", [(i, i ^ flips[i & 1]) for i in range(count)])

    def exchange(blocks):
        moved = {m: move(blocks[m], m << 1) for m in reversed(masks)}
        return [moved[m] for m in masks]

    other_keys, other_values = move(key_states, 1), move(value_states, 1)
    tails = jnp.broadcast_to(lengths.astype(BF16)[:, None, None], (2, TAIL, width))
    other_tails = move(tails, 1)
    held = jnp.concatenate([key_states, value_states], 0)
    held, other_keys, other_values, other_tails = lax.optimization_barrier(
        (held, other_keys, other_values, other_tails)
    )
    odd = lax.axis_index("leaf") & 1 == 1
    pack = jnp.concatenate(
        [
            jnp.where(odd, other_keys[0], held[0]),
            jnp.where(odd, other_values[0], held[2]),
            jnp.where(odd, other_tails[0], tails[0]),
        ],
        0,
    )
    if depth == 3:
        near = [move(pack, flip) for flip in (6, 4, 2)]
    else:
        near = exchange({m: pack for m in masks})
    query_rows, cot, raised, weights, stats, last_keys = call(
        functools.partial(early_kernel, depth, heads),
        "early",
        12,
        (queries, grad_output, held, tails, other_keys, other_values, other_tails, pack),
        [
            ((total, width), BF16),
            ((total, width), BF16),
            ((local, total), F32),
            ((local, total), F32),
            ((16, total), F32),
            ((local, width), BF16),
        ],
        flops=4 * local * total * width,
    )
    if depth == 3:
        leaving = [((3 * rows, width), BF16), ((3 * rows, width), F32)]
    else:
        leaving = [(terms, BF16)] * len(near)
    ds, joined, keys_t, *sends = call(
        functools.partial(middle_kernel, depth, heads),
        "middle",
        24,
        (query_rows, cot, stats, pack, *near),
        [
            ((inner, total), BF16),
            ((8, total), F32),
            ((width, inner), BF16),
        ]
        + leaving,
        scratch=[
            ((inner, total), F32),
            ((inner, total), F32),
            ((inner, total), BF16),
            ((depth - 1,) + terms, F32),
        ],
        flops=8 * inner * total * width,
    )
    if depth == 3:
        swap, hold = sends
        other = move(swap, 1)
        send = call(
            functools.partial(pair_kernel, 0), "pair", 2, (hold, other, other), [(terms, BF16)]
        )[0]
        straight = move(send, 4, 2)
        half = call(
            functools.partial(pair_kernel, 2 * rows), "pair", 2, (hold, other, send),
            [((rows, width), BF16)],
        )[0]
        arrived = [straight, move(half, 6)]
        fold = gather_kernel
    else:
        arrived = exchange(dict(zip(masks, sends)))
        fold = functools.partial(fold_kernel, depth)
    grad_queries, leaf, last_part, even_part = call(
        functools.partial(late_kernel, heads),
        "late",
        12,
        (query_rows, cot, raised, weights, joined, ds, keys_t, last_keys),
        [((2, rows, heads * width), BF16), (terms, BF16), (terms, F32), (terms, F32)],
        scratch=[((local, total), BF16), ((local, total), BF16)],
        flops=8 * local * total * width,
    )
    keep, send = call(
        fold,
        "fold",
        3,
        (even_part, last_part, *arrived),
        [(terms, F32), (terms, BF16)],
    )
    grad_keys, grad_values = call(
        final_kernel,
        "final",
        2,
        (leaf, keep, move(send, 1)),
        [(key_states.shape, BF16)] * 2,
    )
    return grad_queries, grad_keys, grad_values


def solution(mesh):
    segments = P(("dp", "leaf"), None, None)
    return jax.shard_map(
        body,
        mesh=mesh,
        in_specs=(segments, segments, segments, segments, P(("dp", "leaf"))),
        out_specs=(segments, segments, segments),
        check_vma=False,
    )
```

```python
import functools

import jax
import jax.numpy as jnp
from jax import lax
from jax.experimental import pallas as pl
from jax.experimental.pallas import tpu as pltpu
from jax.sharding import PartitionSpec as P

BF16 = jnp.bfloat16
F32 = jnp.float32
LOCAL = 3
TAIL = 16
BIG = -1e30
LOG2E = 1.4426950408889634
NT = (((1,), (1,)), ((), ()))
NN = (((1,), (0,)), ((), ()))


def depth_of(count):
    return count.bit_length() - 1


def trailing_zeros(index, depth):
    total = jnp.zeros((), jnp.int32)
    for bit in range(depth):
        total = total + jnp.where((index & ((2 << bit) - 1)) == 0, 1, 0)
    return total


def owner_of(index, level, depth):
    if level == 0:
        return index * 0
    shift = depth - level + 1
    return ((index >> shift) << shift) + (1 << (depth - level))


def level_of_even(index, depth):
    return depth - trailing_zeros(index, depth)


def owner_at(index, level, depth):
    owner = owner_of(index, 0, depth)
    for place in range(1, depth + 1):
        owner = jnp.where(level == place, owner_of(index, place, depth), owner)
    return owner


def call(kernel, name, mib, arrays, outs, scratch=(), flops=0):
    vmem = pl.BlockSpec(memory_space=pltpu.VMEM)
    return pl.pallas_call(
        kernel,
        out_shape=[jax.ShapeDtypeStruct(shape, kind) for shape, kind in outs],
        in_specs=[vmem] * len(arrays),
        out_specs=[vmem] * len(outs),
        scratch_shapes=[pltpu.VMEM(shape, kind) for shape, kind in scratch],
        compiler_params=pltpu.CompilerParams(vmem_limit_bytes=mib * 1024 * 1024),
        cost_estimate=pl.CostEstimate(flops=flops, bytes_accessed=1 << 20, transcendentals=0),
        name=name,
    )(*arrays)


def ruled_columns(rows, width):
    lane = lax.broadcasted_iota(jnp.int32, (rows, width), 1)
    row = lax.broadcasted_iota(jnp.int32, (rows, width), 0)
    ruled = jnp.where((lane > row) | (lane == 0), BIG, 0.0).astype(BF16)
    return jnp.concatenate([ruled, ruled], 0)


def mask_columns(length, before, same, rows, width):
    lane = lax.broadcasted_iota(jnp.int32, (rows, width), 1)
    row = lax.broadcasted_iota(jnp.int32, (rows, width), 0)
    column = jnp.where(same & (row > 0), row, -1)
    live = (row.astype(F32) < length) & (before | same)
    column = jnp.where(live, column, 0)
    return jnp.where(lane == column, 1.0, 0.0).astype(BF16)


def block_scores(keys_wide, values, query_wide, cot, factor):
    scores = lax.dot_general(keys_wide, query_wide, NT, preferred_element_type=F32)
    top = jnp.max(scores, axis=0, keepdims=True)
    raised = jnp.exp2((scores - top) * factor)
    total = jnp.sum(raised, axis=0, keepdims=True)
    grad_weights = lax.dot_general(values, cot, NT, preferred_element_type=F32)
    partial = jnp.sum(raised * grad_weights, axis=0, keepdims=True)
    return raised, grad_weights, top, total, partial


def early_kernel(depth, heads, query_ref, grad_ref, held_ref, tails_ref, *refs):
    other_key_ref, other_value_ref, other_tails_ref, pack_ref = refs[:4]
    query_s, cot_s, raised_s, weights_s, stats_s, keys_s = refs[4:]
    rows, width = held_ref.shape[1:]
    index = lax.axis_index("leaf")
    odd = index & 1 == 1
    factor = width ** (-0.5) * LOG2E
    step = 2 * rows
    row = lax.broadcasted_iota(jnp.int32, (rows, width), 0)
    lengths = [tails_ref[segment, 0:1, :].astype(F32) for segment in range(2)]
    length = jnp.where(odd, lengths[0], other_tails_ref[0, 0:1, :].astype(F32))
    even_length = pack_ref[2 * rows : 2 * rows + 1, :].astype(F32)
    last_keys = jnp.where(odd, held_ref[0], other_key_ref[0])
    last_values = jnp.where(odd, held_ref[2], other_value_ref[0])
    keys = [last_keys, pack_ref[:rows, :], held_ref[1]]
    values = [last_values, pack_ref[rows : 2 * rows, :], held_ref[3]]
    yes, no = jnp.full((), True), jnp.full((), False)
    masks = [
        [(length, no, odd), (even_length, odd, ~odd)],
        [(length, yes, no), (even_length, yes, no), (lengths[1], no, yes)],
    ]
    wide = [
        [
            jnp.concatenate([block, mask_columns(*mask, rows, width)], 1)
            for block, mask in zip(keys, masks[segment])
        ]
        for segment in range(2)
    ]
    for place in range(LOCAL):
        keys_s[place * rows : (place + 1) * rows, :] = keys[place]
    ruled = ruled_columns(rows, width)
    for segment in range(2):
        live = row.astype(F32) < lengths[segment]
        for pair in range(heads // 2):
            at = (segment * (heads // 2) + pair) * step
            here = slice(at, at + step)
            columns = [slice(h * width, (h + 1) * width) for h in (2 * pair, 2 * pair + 1)]
            query = jnp.concatenate([query_ref[segment, :, c] for c in columns], 0)
            cot = jnp.concatenate(
                [jnp.where(live, grad_ref[segment, :, c], jnp.zeros((), BF16)) for c in columns], 0
            )
            query_s[here, :] = query
            cot_s[here, :] = cot
            query_wide = jnp.concatenate([query, ruled], 1)
            for place in range(LOCAL - 1 + segment):
                span = slice(place * rows, (place + 1) * rows)
                raised, grad_weights, top, total, partial = block_scores(
                    wide[segment][place], values[place], query_wide, cot, factor
                )
                raised_s[span, here] = raised
                weights_s[span, here] = grad_weights
                for n, line in enumerate((top, total, partial)):
                    stats_s[3 * place + n : 3 * place + n + 1, here] = line


def middle_kernel(depth, heads, query_s, cot_s, stats_ref, pack_ref, *refs):
    masks = (1 << (depth - 1)) - 1
    near, refs = refs[:masks], refs[masks:]
    ds_s, joined_s, keys_t = refs[:3]
    sends, refs = refs[3:-4], refs[-4:]
    raised_s, weights_s, low_s, terms_s = refs
    width = pack_ref.shape[1]
    rows = (pack_ref.shape[0] - TAIL) // 2
    index = lax.axis_index("leaf")
    even = index - (index & 1)
    own_level = depth - trailing_zeros(index, depth)
    scale = width ** (-0.5)
    factor = scale * LOG2E
    step = 2 * rows
    yes, no = jnp.full((), True), jnp.full((), False)
    ruled = ruled_columns(rows, width)
    values = []
    wide = [[], []]
    if depth == 3:
        far = (index >> 1) & 1 == 1
        _, straight, across = leaving_levels(index)
        remote = [
            (straight, jnp.where(far, near[0][...], near[1][...])),
            (across, near[2][...]),
        ]
    else:
        remote = []
        for place in range(depth - 1):
            level = place + jnp.where(place < level_of_even(even, depth), 0, 1)
            pick = (even ^ owner_at(even, level, depth)) >> 1
            block = pack_ref[...]
            for mask in range(1, masks + 1):
                block = jnp.where(pick == mask, near[mask - 1][...], block)
            remote.append((level, block))
    for place, (level, block) in enumerate(remote):
        keys = block[:rows]
        values.append(block[rows : 2 * rows])
        length = block[2 * rows : 2 * rows + 1].astype(F32)
        keys_t[:, place * rows : (place + 1) * rows] = keys.T
        inner = mask_columns(length, level < own_level, level == own_level, rows, width)
        outer = mask_columns(length, yes, no, rows, width)
        wide[0].append(jnp.concatenate([keys, inner], 1))
        wide[1].append(jnp.concatenate([keys, outer], 1))

    grad_keys = grad_values = None
    half = heads * rows
    for segment in range(2):
        for pair in range(heads // 2):
            at = (segment * (heads // 2) + pair) * step
            here = slice(at, at + step)
            query, cot = query_s[here, :], cot_s[here, :]
            query_wide = jnp.concatenate([query, ruled], 1)
            tops, totals, partials = [], [], []
            local = LOCAL - 1 + segment
            for place in range(local):
                tops.append(stats_ref[3 * place : 3 * place + 1, here])
                totals.append(stats_ref[3 * place + 1 : 3 * place + 2, here])
                partials.append(stats_ref[3 * place + 2 : 3 * place + 3, here])
            for place in range(len(remote)):
                span = slice(place * rows, (place + 1) * rows)
                raised, grad_weights, top, total, partial = block_scores(
                    wide[segment][place], values[place], query_wide, cot, factor
                )
                raised_s[span, here] = raised
                weights_s[span, here] = grad_weights
                tops.append(top)
                totals.append(total)
                partials.append(partial)
            highest = functools.reduce(jnp.maximum, tops)
            shares = [jnp.exp2((top - highest) * factor) for top in tops]
            total = sum(share * part for share, part in zip(shares, totals))
            inverse = 1.0 / total
            shares = [share * inverse for share in shares]
            delta = sum(share * part for share, part in zip(shares, partials))
            joined_s[0:1, here] = delta
            for place in range(local):
                joined_s[1 + place : 2 + place, here] = shares[place]
            for place in range(len(remote)):
                span = slice(place * rows, (place + 1) * rows)
                weights = raised_s[span, here] * shares[local + place]
                low_s[span, here] = weights.astype(BF16)
                ds_s[span, here] = (weights * (weights_s[span, here] - delta)).astype(BF16)
        now = slice(segment * half, (segment + 1) * half)
        more_keys = lax.dot_general(
            ds_s[:, now], query_s[now, :], NN, preferred_element_type=F32
        )
        more_values = lax.dot_general(
            low_s[:, now], cot_s[now, :], NN, preferred_element_type=F32
        )
        grad_keys = more_keys if segment == 0 else grad_keys + more_keys
        grad_values = more_values if segment == 0 else grad_values + more_values
    for place in range(len(remote)):
        span = slice(place * rows, (place + 1) * rows)
        terms_s[place, :rows, :] = grad_keys[span] * scale
        terms_s[place, rows:, :] = grad_values[span]
    if depth == 3:
        odd = index & 1 == 1
        swap_ref, hold_ref = sends
        first, second = terms_s[1, :rows, :], terms_s[1, rows:, :]
        hold_ref[: 2 * rows, :] = terms_s[0]
        hold_ref[2 * rows :, :] = jnp.where(odd, second, first)
        swap_ref[: 2 * rows, :] = terms_s[0].astype(BF16)
        swap_ref[2 * rows :, :] = jnp.where(odd, first, second).astype(BF16)
        return
    for mask, ref in enumerate(sends, 1):
        level = level_of_even(even ^ (mask << 1), depth)
        place = level - jnp.where(level < level_of_even(even, depth), 0, 1)
        ref[...] = terms_s[jnp.clip(place, 0, depth - 2)].astype(BF16)


def late_kernel(heads, query_s, cot_s, raised_ref, weights_ref, joined_ref, ds_ref, *refs):
    keys_t, keys_s, grad_query_ref, leaf_ref, last_ref, even_ref, low_s, ds_s = refs
    width = keys_s.shape[1]
    rows = keys_s.shape[0] // LOCAL
    scale = width ** (-0.5)
    step = 2 * rows
    half = heads * rows
    near_t = keys_s[...].T
    for segment in range(2):
        count = (LOCAL - 1 + segment) * rows
        for pair in range(heads // 2):
            at = (segment * (heads // 2) + pair) * step
            here = slice(at, at + step)
            delta = joined_ref[0:1, here]
            for place in range(LOCAL - 1 + segment):
                span = slice(place * rows, (place + 1) * rows)
                weights = raised_ref[span, here] * joined_ref[1 + place : 2 + place, here]
                low_s[span, here] = weights.astype(BF16)
                ds_s[span, here] = (weights * (weights_ref[span, here] - delta)).astype(BF16)
            grad_query = lax.dot_general(
                keys_t[...], ds_ref[:, here], NN, preferred_element_type=F32
            ) + lax.dot_general(
                near_t[:, :count], ds_s[:count, here], NN, preferred_element_type=F32
            )
            grad_query = (grad_query * scale).astype(BF16).T
            for n in range(2):
                c = slice((2 * pair + n) * width, (2 * pair + n + 1) * width)
                grad_query_ref[segment, :, c] = grad_query[n * rows : (n + 1) * rows]
    inner = (LOCAL - 1) * rows
    grad_keys = scale * lax.dot_general(
        ds_s[:inner, :], query_s[...], NN, preferred_element_type=F32
    )
    grad_values = lax.dot_general(
        low_s[:inner, :], cot_s[...], NN, preferred_element_type=F32
    )
    for place, ref in enumerate((last_ref, even_ref)):
        span = slice(place * rows, (place + 1) * rows)
        ref[:rows, :] = grad_keys[span]
        ref[rows:, :] = grad_values[span]
    leaf_keys = scale * lax.dot_general(
        ds_s[inner:, half:], query_s[half:, :], NN, preferred_element_type=F32
    )
    leaf_values = lax.dot_general(
        low_s[inner:, half:], cot_s[half:, :], NN, preferred_element_type=F32
    )
    leaf_ref[:rows, :] = leaf_keys.astype(BF16)
    leaf_ref[rows:, :] = leaf_values.astype(BF16)


def leaving_levels(index):
    x, y = (index >> 1) & 1, (index >> 2) & 1
    return index & 1 == 1, 1 - y, jnp.where(x == 1, y, 2)


def pair_kernel(first, hold_ref, other_ref, after_ref, out_ref):
    span = slice(first, first + out_ref.shape[0])
    out_ref[...] = (hold_ref[span, :] + other_ref[span, :].astype(F32)).astype(BF16)


def gather_kernel(even_ref, last_ref, arrived_ref, half_ref, keep_ref, send_ref):
    rows = half_ref.shape[0]
    index = lax.axis_index("leaf")
    odd, near = index & 1 == 1, (index >> 1) & 1 == 0
    total = even_ref[...] + jnp.where(near, arrived_ref[...].astype(F32), 0.0)
    half = half_ref[...].astype(F32)
    first = total[:rows] + jnp.where(odd, 0.0, half)
    second = total[rows:] + jnp.where(odd, half, 0.0)
    total = jnp.concatenate([first, second], 0)
    keep_ref[...] = jnp.where(odd, last_ref[...], total)
    send_ref[...] = jnp.where(odd, total, last_ref[...]).astype(BF16)


def fold_kernel(depth, even_ref, last_ref, *refs):
    arrived, (keep_ref, send_ref) = refs[:-2], refs[-2:]
    index = lax.axis_index("leaf")
    odd = index & 1 == 1
    even = index - (index & 1)
    level = level_of_even(even, depth)
    total = even_ref[...]
    for mask, ref in enumerate(arrived, 1):
        mine = owner_at(even ^ (mask << 1), level, depth) == even
        total = total + jnp.where(mine, ref[...].astype(F32), 0.0)
    keep_ref[...] = jnp.where(odd, last_ref[...], total)
    send_ref[...] = jnp.where(odd, total, last_ref[...]).astype(BF16)


def final_kernel(leaf_ref, keep_ref, other_ref, keys_ref, values_ref):
    rows = keys_ref.shape[1]
    total = (keep_ref[...] + other_ref[...].astype(F32)).astype(BF16)
    keys_ref[0] = total[:rows]
    values_ref[0] = total[rows:]
    keys_ref[1] = leaf_ref[:rows, :]
    values_ref[1] = leaf_ref[rows:, :]


def body(queries, key_states, value_states, grad_output, lengths):
    count = lax.axis_size("leaf")
    depth = depth_of(count)
    masks = range(1, count // 2)
    rows, width = key_states.shape[1:]
    heads = queries.shape[2] // width
    total = 2 * heads * rows
    local = LOCAL * rows
    inner = (depth - 1) * rows
    terms = (2 * rows, width)

    def move(block, flip):
        return lax.ppermute(block, "leaf", [(i, i ^ flip) for i in range(count)])

    def exchange(blocks):
        moved = {m: move(blocks[m], m << 1) for m in reversed(masks)}
        return [moved[m] for m in masks]

    other_keys, other_values = move(key_states, 1), move(value_states, 1)
    tails = jnp.broadcast_to(lengths.astype(BF16)[:, None, None], (2, TAIL, width))
    other_tails = move(tails, 1)
    held = jnp.concatenate([key_states, value_states], 0)
    held, other_keys, other_values, other_tails = lax.optimization_barrier(
        (held, other_keys, other_values, other_tails)
    )
    odd = lax.axis_index("leaf") & 1 == 1
    pack = jnp.concatenate(
        [
            jnp.where(odd, other_keys[0], held[0]),
            jnp.where(odd, other_values[0], held[2]),
            jnp.where(odd, other_tails[0], tails[0]),
        ],
        0,
    )
    if depth == 3:
        near = [move(pack, flip) for flip in (6, 4, 2)]
    else:
        near = exchange({m: pack for m in masks})
    query_rows, cot, raised, weights, stats, last_keys = call(
        functools.partial(early_kernel, depth, heads),
        "early",
        12,
        (queries, grad_output, held, tails, other_keys, other_values, other_tails, pack),
        [
            ((total, width), BF16),
            ((total, width), BF16),
            ((local, total), F32),
            ((local, total), F32),
            ((16, total), F32),
            ((local, width), BF16),
        ],
        flops=4 * local * total * width,
    )
    if depth == 3:
        leaving = [((3 * rows, width), BF16), ((3 * rows, width), F32)]
    else:
        leaving = [(terms, BF16)] * len(near)
    ds, joined, keys_t, *sends = call(
        functools.partial(middle_kernel, depth, heads),
        "middle",
        24,
        (query_rows, cot, stats, pack, *near),
        [
            ((inner, total), BF16),
            ((8, total), F32),
            ((width, inner), BF16),
        ]
        + leaving,
        scratch=[
            ((inner, total), F32),
            ((inner, total), F32),
            ((inner, total), BF16),
            ((depth - 1,) + terms, F32),
        ],
        flops=8 * inner * total * width,
    )
    if depth == 3:
        swap, hold = sends
        other = move(swap, 1)
        send = call(
            functools.partial(pair_kernel, 0), "pair", 2, (hold, other, other), [(terms, BF16)]
        )[0]
        far_pairs = [(0, 4), (4, 0), (2, 6), (6, 2), (3, 5), (5, 7), (7, 1), (1, 3)]
        straight = lax.ppermute(send, "leaf", far_pairs)
        half = call(
            functools.partial(pair_kernel, 2 * rows), "pair", 2, (hold, other, send),
            [((rows, width), BF16)],
        )[0]
        arrived = [straight, move(half, 2)]
        fold = gather_kernel
    else:
        arrived = exchange(dict(zip(masks, sends)))
        fold = functools.partial(fold_kernel, depth)
    grad_queries, leaf, last_part, even_part = call(
        functools.partial(late_kernel, heads),
        "late",
        12,
        (query_rows, cot, raised, weights, joined, ds, keys_t, last_keys),
        [((2, rows, heads * width), BF16), (terms, BF16), (terms, F32), (terms, F32)],
        scratch=[((local, total), BF16), ((local, total), BF16)],
        flops=8 * local * total * width,
    )
    keep, send = call(
        fold,
        "fold",
        3,
        (even_part, last_part, *arrived),
        [(terms, F32), (terms, BF16)],
    )
    grad_keys, grad_values = call(
        final_kernel,
        "final",
        2,
        (leaf, keep, move(send, 1)),
        [(key_states.shape, BF16)] * 2,
    )
    return grad_queries, grad_keys, grad_values


def solution(mesh):
    segments = P(("dp", "leaf"), None, None)
    return jax.shard_map(
        body,
        mesh=mesh,
        in_specs=(segments, segments, segments, segments, P(("dp", "leaf"))),
        out_specs=(segments, segments, segments),
        check_vma=False,
    )
```

```python
import functools

import jax
import jax.numpy as jnp
from jax import lax
from jax.experimental import pallas as pl
from jax.experimental.pallas import tpu as pltpu
from jax.sharding import PartitionSpec as P

BF16 = jnp.bfloat16
F32 = jnp.float32
LOCAL = 3
TAIL = 16
BIG = -1e30
FAR_PAIRS = [(0, 4), (4, 0), (2, 6), (6, 2), (3, 5), (5, 7), (7, 1), (1, 3)]
LOG2E = 1.4426950408889634
NT = (((1,), (1,)), ((), ()))
NN = (((1,), (0,)), ((), ()))


def depth_of(count):
    return count.bit_length() - 1


def trailing_zeros(index, depth):
    total = jnp.zeros((), jnp.int32)
    for bit in range(depth):
        total = total + jnp.where((index & ((2 << bit) - 1)) == 0, 1, 0)
    return total


def owner_of(index, level, depth):
    if level == 0:
        return index * 0
    shift = depth - level + 1
    return ((index >> shift) << shift) + (1 << (depth - level))


def level_of_even(index, depth):
    return depth - trailing_zeros(index, depth)


def owner_at(index, level, depth):
    owner = owner_of(index, 0, depth)
    for place in range(1, depth + 1):
        owner = jnp.where(level == place, owner_of(index, place, depth), owner)
    return owner


def call(kernel, name, mib, arrays, outs, scratch=(), flops=0):
    vmem = pl.BlockSpec(memory_space=pltpu.VMEM)
    return pl.pallas_call(
        kernel,
        out_shape=[jax.ShapeDtypeStruct(shape, kind) for shape, kind in outs],
        in_specs=[vmem] * len(arrays),
        out_specs=[vmem] * len(outs),
        scratch_shapes=[pltpu.VMEM(shape, kind) for shape, kind in scratch],
        compiler_params=pltpu.CompilerParams(vmem_limit_bytes=mib * 1024 * 1024),
        cost_estimate=pl.CostEstimate(flops=flops, bytes_accessed=1 << 20, transcendentals=0),
        name=name,
    )(*arrays)


def ruled_columns(rows, width):
    lane = lax.broadcasted_iota(jnp.int32, (rows, width), 1)
    row = lax.broadcasted_iota(jnp.int32, (rows, width), 0)
    ruled = jnp.where((lane > row) | (lane == 0), BIG, 0.0).astype(BF16)
    return jnp.concatenate([ruled, ruled], 0)


def mask_columns(length, before, same, rows, width):
    lane = lax.broadcasted_iota(jnp.int32, (rows, width), 1)
    row = lax.broadcasted_iota(jnp.int32, (rows, width), 0)
    column = jnp.where(same & (row > 0), row, -1)
    live = (row.astype(F32) < length) & (before | same)
    column = jnp.where(live, column, 0)
    return jnp.where(lane == column, 1.0, 0.0).astype(BF16)


def block_scores(keys_wide, values, query_wide, cot, factor):
    scores = lax.dot_general(keys_wide, query_wide, NT, preferred_element_type=F32)
    top = jnp.max(scores, axis=0, keepdims=True)
    raised = jnp.exp2((scores - top) * factor)
    total = jnp.sum(raised, axis=0, keepdims=True)
    grad_weights = lax.dot_general(values, cot, NT, preferred_element_type=F32)
    partial = jnp.sum(raised * grad_weights, axis=0, keepdims=True)
    return raised, grad_weights, top, total, partial


def early_kernel(segment, heads, query_ref, grad_ref, held_ref, tails_ref, *refs):
    other_key_ref, other_value_ref, other_tails_ref, pack_ref = refs[:4]
    query_s, cot_s, raised_s, weights_s, stats_s, keys_s = refs[4:]
    count = LOCAL - 1 + segment
    rows, width = held_ref.shape[1:]
    index = lax.axis_index("leaf")
    odd = index & 1 == 1
    factor = width ** (-0.5) * LOG2E
    step = 2 * rows
    row = lax.broadcasted_iota(jnp.int32, (rows, width), 0)
    lengths = [tails_ref[segment, 0:1, :].astype(F32) for segment in range(2)]
    length = jnp.where(odd, lengths[0], other_tails_ref[0, 0:1, :].astype(F32))
    even_length = pack_ref[2 * rows : 2 * rows + 1, :].astype(F32)
    last_keys = jnp.where(odd, held_ref[0], other_key_ref[0])
    last_values = jnp.where(odd, held_ref[2], other_value_ref[0])
    keys = [last_keys, pack_ref[:rows, :], held_ref[1]]
    values = [last_values, pack_ref[rows : 2 * rows, :], held_ref[3]]
    yes, no = jnp.full((), True), jnp.full((), False)
    masks = [
        [(length, no, odd), (even_length, odd, ~odd)],
        [(length, yes, no), (even_length, yes, no), (lengths[1], no, yes)],
    ][segment]
    wide = [
        jnp.concatenate([block, mask_columns(*mask, rows, width)], 1)
        for block, mask in zip(keys, masks)
    ]
    for place in range(count):
        keys_s[place * rows : (place + 1) * rows, :] = keys[place]
    ruled = ruled_columns(rows, width)
    live = row.astype(F32) < lengths[segment]
    for pair in range(heads // 2):
        here = slice(pair * step, (pair + 1) * step)
        columns = [slice(h * width, (h + 1) * width) for h in (2 * pair, 2 * pair + 1)]
        query = jnp.concatenate([query_ref[segment, :, c] for c in columns], 0)
        cot = jnp.concatenate(
            [jnp.where(live, grad_ref[segment, :, c], jnp.zeros((), BF16)) for c in columns], 0
        )
        query_s[here, :] = query
        cot_s[here, :] = cot
        query_wide = jnp.concatenate([query, ruled], 1)
        for place in range(count):
            span = slice(place * rows, (place + 1) * rows)
            raised, grad_weights, top, total, partial = block_scores(
                wide[place], values[place], query_wide, cot, factor
            )
            raised_s[span, here] = raised
            weights_s[span, here] = grad_weights
            for n, line in enumerate((top, total, partial)):
                stats_s[3 * place + n : 3 * place + n + 1, here] = line


def middle_kernel(depth, heads, *refs):
    queries, cots, stats, pack_ref, refs = refs[:2], refs[2:4], refs[4:6], refs[6], refs[7:]
    masks = (1 << (depth - 1)) - 1
    near, refs = refs[:masks], refs[masks:]
    ds_s, joined_s, keys_t = refs[:3]
    sends, refs = refs[3:-4], refs[-4:]
    raised_s, weights_s, low_s, terms_s = refs
    width = pack_ref.shape[1]
    rows = (pack_ref.shape[0] - TAIL) // 2
    index = lax.axis_index("leaf")
    even = index - (index & 1)
    own_level = depth - trailing_zeros(index, depth)
    scale = width ** (-0.5)
    factor = scale * LOG2E
    step = 2 * rows
    yes, no = jnp.full((), True), jnp.full((), False)
    ruled = ruled_columns(rows, width)
    values = []
    wide = [[], []]
    if depth == 3:
        here = index & 1 == (index >> 1) & 1
        _, straight, across = leaving_levels(index)
        remote = [
            (straight, jnp.where(here, near[0][...], near[2][...])),
            (across, near[1][...]),
        ]
    else:
        remote = []
        for place in range(depth - 1):
            level = place + jnp.where(place < level_of_even(even, depth), 0, 1)
            pick = (even ^ owner_at(even, level, depth)) >> 1
            block = pack_ref[...]
            for mask in range(1, masks + 1):
                block = jnp.where(pick == mask, near[mask - 1][...], block)
            remote.append((level, block))
    for place, (level, block) in enumerate(remote):
        keys = block[:rows]
        values.append(block[rows : 2 * rows])
        length = block[2 * rows : 2 * rows + 1].astype(F32)
        keys_t[:, place * rows : (place + 1) * rows] = keys.T
        inner = mask_columns(length, level < own_level, level == own_level, rows, width)
        outer = mask_columns(length, yes, no, rows, width)
        wide[0].append(jnp.concatenate([keys, inner], 1))
        wide[1].append(jnp.concatenate([keys, outer], 1))

    grad_keys = grad_values = None
    half = heads * rows
    for segment in range(2):
        for pair in range(heads // 2):
            at = (segment * (heads // 2) + pair) * step
            here = slice(at, at + step)
            part = slice(pair * step, (pair + 1) * step)
            query, cot = queries[segment][part, :], cots[segment][part, :]
            stats_ref = stats[segment]
            query_wide = jnp.concatenate([query, ruled], 1)
            tops, totals, partials = [], [], []
            local = LOCAL - 1 + segment
            for place in range(local):
                tops.append(stats_ref[3 * place : 3 * place + 1, part])
                totals.append(stats_ref[3 * place + 1 : 3 * place + 2, part])
                partials.append(stats_ref[3 * place + 2 : 3 * place + 3, part])
            for place in range(len(remote)):
                span = slice(place * rows, (place + 1) * rows)
                raised, grad_weights, top, total, partial = block_scores(
                    wide[segment][place], values[place], query_wide, cot, factor
                )
                raised_s[span, here] = raised
                weights_s[span, here] = grad_weights
                tops.append(top)
                totals.append(total)
                partials.append(partial)
            highest = functools.reduce(jnp.maximum, tops)
            shares = [jnp.exp2((top - highest) * factor) for top in tops]
            total = sum(share * part for share, part in zip(shares, totals))
            inverse = 1.0 / total
            shares = [share * inverse for share in shares]
            delta = sum(share * part for share, part in zip(shares, partials))
            joined_s[0:1, here] = delta
            for place in range(local):
                joined_s[1 + place : 2 + place, here] = shares[place]
            for place in range(len(remote)):
                span = slice(place * rows, (place + 1) * rows)
                weights = raised_s[span, here] * shares[local + place]
                low_s[span, here] = weights.astype(BF16)
                ds_s[span, here] = (weights * (weights_s[span, here] - delta)).astype(BF16)
        now = slice(segment * half, (segment + 1) * half)
        more_keys = lax.dot_general(
            ds_s[:, now], queries[segment][...], NN, preferred_element_type=F32
        )
        more_values = lax.dot_general(
            low_s[:, now], cots[segment][...], NN, preferred_element_type=F32
        )
        grad_keys = more_keys if segment == 0 else grad_keys + more_keys
        grad_values = more_values if segment == 0 else grad_values + more_values
    for place in range(len(remote)):
        span = slice(place * rows, (place + 1) * rows)
        terms_s[place, :rows, :] = grad_keys[span] * scale
        terms_s[place, rows:, :] = grad_values[span]
    if depth == 3:
        odd = index & 1 == 1
        swap_ref, hold_ref = sends
        first, second = terms_s[1, :rows, :], terms_s[1, rows:, :]
        hold_ref[: 2 * rows, :] = terms_s[0]
        hold_ref[2 * rows :, :] = jnp.where(odd, second, first)
        swap_ref[: 2 * rows, :] = terms_s[0].astype(BF16)
        swap_ref[2 * rows :, :] = jnp.where(odd, first, second).astype(BF16)
        return
    for mask, ref in enumerate(sends, 1):
        level = level_of_even(even ^ (mask << 1), depth)
        place = level - jnp.where(level < level_of_even(even, depth), 0, 1)
        ref[...] = terms_s[jnp.clip(place, 0, depth - 2)].astype(BF16)


def late_kernel(heads, *refs):
    queries, cots, raised, given, refs = refs[:2], refs[2:4], refs[4:6], refs[6:8], refs[8:]
    joined_ref, ds_ref, refs = refs[0], refs[1], refs[2:]
    keys_t, keys_s, grad_query_ref, leaf_ref, last_ref, even_ref, low_s, ds_s = refs
    width = keys_s.shape[1]
    rows = keys_s.shape[0] // LOCAL
    scale = width ** (-0.5)
    step = 2 * rows
    half = heads * rows
    near_t = keys_s[...].T
    for segment in range(2):
        count = (LOCAL - 1 + segment) * rows
        for pair in range(heads // 2):
            at = (segment * (heads // 2) + pair) * step
            here = slice(at, at + step)
            part = slice(pair * step, (pair + 1) * step)
            delta = joined_ref[0:1, here]
            for place in range(LOCAL - 1 + segment):
                span = slice(place * rows, (place + 1) * rows)
                weights = raised[segment][span, part] * joined_ref[1 + place : 2 + place, here]
                low_s[span, here] = weights.astype(BF16)
                ds_s[span, here] = (weights * (given[segment][span, part] - delta)).astype(BF16)
            grad_query = lax.dot_general(
                keys_t[...], ds_ref[:, here], NN, preferred_element_type=F32
            ) + lax.dot_general(
                near_t[:, :count], ds_s[:count, here], NN, preferred_element_type=F32
            )
            grad_query = (grad_query * scale).astype(BF16).T
            for n in range(2):
                c = slice((2 * pair + n) * width, (2 * pair + n + 1) * width)
                grad_query_ref[segment, :, c] = grad_query[n * rows : (n + 1) * rows]
    inner = (LOCAL - 1) * rows

    def terms(block, sides):
        return sum(
            lax.dot_general(
                block[:inner, n * half : (n + 1) * half], side[...], NN, preferred_element_type=F32
            )
            for n, side in enumerate(sides)
        )

    grad_keys = scale * terms(ds_s, queries)
    grad_values = terms(low_s, cots)
    for place, ref in enumerate((last_ref, even_ref)):
        span = slice(place * rows, (place + 1) * rows)
        ref[:rows, :] = grad_keys[span]
        ref[rows:, :] = grad_values[span]
    leaf_keys = scale * lax.dot_general(
        ds_s[inner:, half:], queries[1][...], NN, preferred_element_type=F32
    )
    leaf_values = lax.dot_general(
        low_s[inner:, half:], cots[1][...], NN, preferred_element_type=F32
    )
    leaf_ref[:rows, :] = leaf_keys.astype(BF16)
    leaf_ref[rows:, :] = leaf_values.astype(BF16)


def leaving_levels(index):
    x, y = (index >> 1) & 1, (index >> 2) & 1
    return index & 1 == 1, 1 - y, jnp.where(x == 1, y, 2)


def pair_kernel(first, hold_ref, other_ref, after_ref, out_ref):
    span = slice(first, first + out_ref.shape[0])
    out_ref[...] = (hold_ref[span, :] + other_ref[span, :].astype(F32)).astype(BF16)


def gather_kernel(even_ref, last_ref, arrived_ref, half_ref, keep_ref, send_ref):
    rows = half_ref.shape[0]
    index = lax.axis_index("leaf")
    odd, near = index & 1 == 1, (index >> 1) & 1 == 0
    total = even_ref[...] + jnp.where(near, arrived_ref[...].astype(F32), 0.0)
    half = half_ref[...].astype(F32)
    first = total[:rows] + jnp.where(odd, 0.0, half)
    second = total[rows:] + jnp.where(odd, half, 0.0)
    total = jnp.concatenate([first, second], 0)
    keep_ref[...] = jnp.where(odd, last_ref[...], total)
    send_ref[...] = jnp.where(odd, total, last_ref[...]).astype(BF16)


def fold_kernel(depth, even_ref, last_ref, *refs):
    arrived, (keep_ref, send_ref) = refs[:-2], refs[-2:]
    index = lax.axis_index("leaf")
    odd = index & 1 == 1
    even = index - (index & 1)
    level = level_of_even(even, depth)
    total = even_ref[...]
    for mask, ref in enumerate(arrived, 1):
        mine = owner_at(even ^ (mask << 1), level, depth) == even
        total = total + jnp.where(mine, ref[...].astype(F32), 0.0)
    keep_ref[...] = jnp.where(odd, last_ref[...], total)
    send_ref[...] = jnp.where(odd, total, last_ref[...]).astype(BF16)


def final_kernel(leaf_ref, keep_ref, other_ref, keys_ref, values_ref):
    rows = keys_ref.shape[1]
    total = (keep_ref[...] + other_ref[...].astype(F32)).astype(BF16)
    keys_ref[0] = total[:rows]
    values_ref[0] = total[rows:]
    keys_ref[1] = leaf_ref[:rows, :]
    values_ref[1] = leaf_ref[rows:, :]


def body(queries, key_states, value_states, grad_output, lengths):
    count = lax.axis_size("leaf")
    depth = depth_of(count)
    masks = range(1, count // 2)
    rows, width = key_states.shape[1:]
    heads = queries.shape[2] // width
    total = 2 * heads * rows
    local = LOCAL * rows
    inner = (depth - 1) * rows
    terms = (2 * rows, width)

    def move(block, flip):
        return lax.ppermute(block, "leaf", [(i, i ^ flip) for i in range(count)])

    def exchange(blocks):
        moved = {m: move(blocks[m], m << 1) for m in reversed(masks)}
        return [moved[m] for m in masks]

    other_keys, other_values = move(key_states, 1), move(value_states, 1)
    tails = jnp.broadcast_to(lengths.astype(BF16)[:, None, None], (2, TAIL, width))
    other_tails = move(tails, 1)
    held = jnp.concatenate([key_states, value_states], 0)
    held, other_keys, other_values, other_tails = lax.optimization_barrier(
        (held, other_keys, other_values, other_tails)
    )
    odd = lax.axis_index("leaf") & 1 == 1
    pack = jnp.concatenate(
        [
            jnp.where(odd, other_keys[0], held[0]),
            jnp.where(odd, other_values[0], held[2]),
            jnp.where(odd, other_tails[0], tails[0]),
        ],
        0,
    )
    def early(segment, even_pack):
        held_rows = (LOCAL - 1 + segment) * rows
        arrays = (queries, grad_output, held, tails, other_keys, other_values, other_tails)
        return call(
            functools.partial(early_kernel, segment, heads),
            "early",
            12,
            arrays + (even_pack,),
            [
                ((total // 2, width), BF16),
                ((total // 2, width), BF16),
                ((held_rows, total // 2), F32),
                ((held_rows, total // 2), F32),
                ((16, total // 2), F32),
                ((held_rows, width), BF16),
            ],
            flops=2 * held_rows * total * width,
        )

    if depth == 3:
        far = lax.ppermute(pack, "leaf", [(b, a) for a, b in FAR_PAIRS])
        along_x = move(pack, 2)
        first = early(0, pack)
        pack, far, first = lax.optimization_barrier((pack, far, first))
        near = [far, along_x, move(far, 1)]
    else:
        near = exchange({m: pack for m in masks})
        first = early(0, pack)
    sides = [first, early(1, pack)]
    query_rows, cots, raised, weights, stats, held_keys = zip(*sides)
    if depth == 3:
        leaving = [((3 * rows, width), BF16), ((3 * rows, width), F32)]
    else:
        leaving = [(terms, BF16)] * len(near)
    ds, joined, keys_t, *sends = call(
        functools.partial(middle_kernel, depth, heads),
        "middle",
        24,
        (*query_rows, *cots, *stats, pack, *near),
        [
            ((inner, total), BF16),
            ((8, total), F32),
            ((width, inner), BF16),
        ]
        + leaving,
        scratch=[
            ((inner, total), F32),
            ((inner, total), F32),
            ((inner, total), BF16),
            ((depth - 1,) + terms, F32),
        ],
        flops=8 * inner * total * width,
    )
    if depth == 3:
        swap, hold = sends
        other = move(swap, 1)
        send = call(
            functools.partial(pair_kernel, 0), "pair", 2, (hold, other, other), [(terms, BF16)]
        )[0]
        straight = lax.ppermute(send, "leaf", FAR_PAIRS)
        half = call(
            functools.partial(pair_kernel, 2 * rows), "pair", 2, (hold, other, send),
            [((rows, width), BF16)],
        )[0]
        arrived = [straight, move(half, 2)]
        fold = gather_kernel
    else:
        arrived = exchange(dict(zip(masks, sends)))
        fold = functools.partial(fold_kernel, depth)
    grad_queries, leaf, last_part, even_part = call(
        functools.partial(late_kernel, heads),
        "late",
        12,
        (*query_rows, *cots, *raised, *weights, joined, ds, keys_t, held_keys[1]),
        [((2, rows, heads * width), BF16), (terms, BF16), (terms, F32), (terms, F32)],
        scratch=[((local, total), BF16), ((local, total), BF16)],
        flops=8 * local * total * width,
    )
    keep, send = call(
        fold,
        "fold",
        3,
        (even_part, last_part, *arrived),
        [(terms, F32), (terms, BF16)],
    )
    grad_keys, grad_values = call(
        final_kernel,
        "final",
        2,
        (leaf, keep, move(send, 1)),
        [(key_states.shape, BF16)] * 2,
    )
    return grad_queries, grad_keys, grad_values


def solution(mesh):
    segments = P(("dp", "leaf"), None, None)
    return jax.shard_map(
        body,
        mesh=mesh,
        in_specs=(segments, segments, segments, segments, P(("dp", "leaf"))),
        out_specs=(segments, segments, segments),
        check_vma=False,
    )
```

```python
import functools

import jax
import jax.numpy as jnp
from jax import lax
from jax.experimental import pallas as pl
from jax.experimental.pallas import tpu as pltpu
from jax.sharding import PartitionSpec as P

BF16 = jnp.bfloat16
F32 = jnp.float32
LOCAL = 3
TAIL = 16
BIG = -1e30
FAR_PAIRS = [(0, 4), (4, 0), (2, 6), (6, 2), (3, 5), (5, 7), (7, 1), (1, 3)]
LOG2E = 1.4426950408889634
NT = (((1,), (1,)), ((), ()))
NN = (((1,), (0,)), ((), ()))


def depth_of(count):
    return count.bit_length() - 1


def trailing_zeros(index, depth):
    total = jnp.zeros((), jnp.int32)
    for bit in range(depth):
        total = total + jnp.where((index & ((2 << bit) - 1)) == 0, 1, 0)
    return total


def owner_of(index, level, depth):
    if level == 0:
        return index * 0
    shift = depth - level + 1
    return ((index >> shift) << shift) + (1 << (depth - level))


def level_of_even(index, depth):
    return depth - trailing_zeros(index, depth)


def owner_at(index, level, depth):
    owner = owner_of(index, 0, depth)
    for place in range(1, depth + 1):
        owner = jnp.where(level == place, owner_of(index, place, depth), owner)
    return owner


def call(kernel, name, mib, arrays, outs, scratch=(), flops=0):
    vmem = pl.BlockSpec(memory_space=pltpu.VMEM)
    return pl.pallas_call(
        kernel,
        out_shape=[jax.ShapeDtypeStruct(shape, kind) for shape, kind in outs],
        in_specs=[vmem] * len(arrays),
        out_specs=[vmem] * len(outs),
        scratch_shapes=[pltpu.VMEM(shape, kind) for shape, kind in scratch],
        compiler_params=pltpu.CompilerParams(vmem_limit_bytes=mib * 1024 * 1024),
        cost_estimate=pl.CostEstimate(flops=flops, bytes_accessed=1 << 20, transcendentals=0),
        name=name,
    )(*arrays)


def ruled_columns(rows, width):
    lane = lax.broadcasted_iota(jnp.int32, (rows, width), 1)
    row = lax.broadcasted_iota(jnp.int32, (rows, width), 0)
    ruled = jnp.where((lane > row) | (lane == 0), BIG, 0.0).astype(BF16)
    return jnp.concatenate([ruled, ruled], 0)


def mask_columns(length, before, same, rows, width):
    lane = lax.broadcasted_iota(jnp.int32, (rows, width), 1)
    row = lax.broadcasted_iota(jnp.int32, (rows, width), 0)
    column = jnp.where(same & (row > 0), row, -1)
    live = (row.astype(F32) < length) & (before | same)
    column = jnp.where(live, column, 0)
    return jnp.where(lane == column, 1.0, 0.0).astype(BF16)


def block_scores(keys_wide, values, query_wide, cot, factor):
    scores = lax.dot_general(keys_wide, query_wide, NT, preferred_element_type=F32)
    top = jnp.max(scores, axis=0, keepdims=True)
    raised = jnp.exp2((scores - top) * factor)
    total = jnp.sum(raised, axis=0, keepdims=True)
    grad_weights = lax.dot_general(values, cot, NT, preferred_element_type=F32)
    partial = jnp.sum(raised * grad_weights, axis=0, keepdims=True)
    return raised, grad_weights, top, total, partial


def pack_kernel(held_ref, tails_ref, key_ref, value_ref, other_tails_ref, pack_ref):
    rows = key_ref.shape[1]
    odd = lax.axis_index("leaf") & 1 == 1
    pack_ref[:rows, :] = jnp.where(odd, key_ref[0], held_ref[0])
    pack_ref[rows : 2 * rows, :] = jnp.where(odd, value_ref[0], held_ref[2])
    pack_ref[2 * rows :, :] = jnp.where(odd, other_tails_ref[0], tails_ref[0])


def early_kernel(segment, heads, query_ref, grad_ref, held_ref, tails_ref, *refs):
    other_key_ref, other_value_ref, other_tails_ref, pack_ref = refs[:4]
    query_s, cot_s, raised_s, weights_s, stats_s = refs[4:9]
    count = LOCAL - 1 + segment
    rows, width = held_ref.shape[1:]
    index = lax.axis_index("leaf")
    odd = index & 1 == 1
    factor = width ** (-0.5) * LOG2E
    step = 2 * rows
    row = lax.broadcasted_iota(jnp.int32, (rows, width), 0)
    lengths = [tails_ref[segment, 0:1, :].astype(F32) for segment in range(2)]
    length = jnp.where(odd, lengths[0], other_tails_ref[0, 0:1, :].astype(F32))
    even_length = pack_ref[2 * rows : 2 * rows + 1, :].astype(F32)
    last_keys = jnp.where(odd, held_ref[0], other_key_ref[0])
    last_values = jnp.where(odd, held_ref[2], other_value_ref[0])
    keys = [last_keys, pack_ref[:rows, :], held_ref[1]]
    values = [last_values, pack_ref[rows : 2 * rows, :], held_ref[3]]
    yes, no = jnp.full((), True), jnp.full((), False)
    masks = [
        [(length, no, odd), (even_length, odd, ~odd)],
        [(length, yes, no), (even_length, yes, no), (lengths[1], no, yes)],
    ][segment]
    wide = [
        jnp.concatenate([block, mask_columns(*mask, rows, width)], 1)
        for block, mask in zip(keys, masks)
    ]
    for keys_s in refs[9:]:
        for place in range(count):
            keys_s[place * rows : (place + 1) * rows, :] = keys[place]
    ruled = ruled_columns(rows, width)
    live = row.astype(F32) < lengths[segment]
    for pair in range(heads // 2):
        here = slice(pair * step, (pair + 1) * step)
        columns = [slice(h * width, (h + 1) * width) for h in (2 * pair, 2 * pair + 1)]
        query = jnp.concatenate([query_ref[segment, :, c] for c in columns], 0)
        cot = jnp.concatenate(
            [jnp.where(live, grad_ref[segment, :, c], jnp.zeros((), BF16)) for c in columns], 0
        )
        query_s[here, :] = query
        cot_s[here, :] = cot
        query_wide = jnp.concatenate([query, ruled], 1)
        for place in range(count):
            span = slice(place * rows, (place + 1) * rows)
            raised, grad_weights, top, total, partial = block_scores(
                wide[place], values[place], query_wide, cot, factor
            )
            raised_s[span, here] = raised
            weights_s[span, here] = grad_weights
            for n, line in enumerate((top, total, partial)):
                stats_s[3 * place + n : 3 * place + n + 1, here] = line


def middle_kernel(depth, heads, *refs):
    queries, cots, stats, pack_ref, refs = refs[:2], refs[2:4], refs[4:6], refs[6], refs[7:]
    masks = (1 << (depth - 1)) - 1
    near, refs = refs[:masks], refs[masks:]
    ds_s, joined_s, keys_t = refs[:3]
    sends, refs = refs[3:-4], refs[-4:]
    raised_s, weights_s, low_s, terms_s = refs
    width = pack_ref.shape[1]
    rows = (pack_ref.shape[0] - TAIL) // 2
    index = lax.axis_index("leaf")
    even = index - (index & 1)
    own_level = depth - trailing_zeros(index, depth)
    scale = width ** (-0.5)
    factor = scale * LOG2E
    step = 2 * rows
    yes, no = jnp.full((), True), jnp.full((), False)
    ruled = ruled_columns(rows, width)
    values = []
    wide = [[], []]
    if depth == 3:
        here = index & 1 == (index >> 1) & 1
        _, straight, across = leaving_levels(index)
        remote = [
            (straight, jnp.where(here, near[0][...], near[2][...])),
            (across, near[1][...]),
        ]
    else:
        remote = []
        for place in range(depth - 1):
            level = place + jnp.where(place < level_of_even(even, depth), 0, 1)
            pick = (even ^ owner_at(even, level, depth)) >> 1
            block = pack_ref[...]
            for mask in range(1, masks + 1):
                block = jnp.where(pick == mask, near[mask - 1][...], block)
            remote.append((level, block))
    for place, (level, block) in enumerate(remote):
        keys = block[:rows]
        values.append(block[rows : 2 * rows])
        length = block[2 * rows : 2 * rows + 1].astype(F32)
        keys_t[:, place * rows : (place + 1) * rows] = keys.T
        inner = mask_columns(length, level < own_level, level == own_level, rows, width)
        outer = mask_columns(length, yes, no, rows, width)
        wide[0].append(jnp.concatenate([keys, inner], 1))
        wide[1].append(jnp.concatenate([keys, outer], 1))

    grad_keys = grad_values = None
    half = heads * rows
    for segment in range(2):
        for pair in range(heads // 2):
            at = (segment * (heads // 2) + pair) * step
            here = slice(at, at + step)
            part = slice(pair * step, (pair + 1) * step)
            query, cot = queries[segment][part, :], cots[segment][part, :]
            stats_ref = stats[segment]
            query_wide = jnp.concatenate([query, ruled], 1)
            tops, totals, partials = [], [], []
            local = LOCAL - 1 + segment
            for place in range(local):
                tops.append(stats_ref[3 * place : 3 * place + 1, part])
                totals.append(stats_ref[3 * place + 1 : 3 * place + 2, part])
                partials.append(stats_ref[3 * place + 2 : 3 * place + 3, part])
            for place in range(len(remote)):
                span = slice(place * rows, (place + 1) * rows)
                raised, grad_weights, top, total, partial = block_scores(
                    wide[segment][place], values[place], query_wide, cot, factor
                )
                raised_s[span, here] = raised
                weights_s[span, here] = grad_weights
                tops.append(top)
                totals.append(total)
                partials.append(partial)
            highest = functools.reduce(jnp.maximum, tops)
            shares = [jnp.exp2((top - highest) * factor) for top in tops]
            total = sum(share * part for share, part in zip(shares, totals))
            inverse = 1.0 / total
            shares = [share * inverse for share in shares]
            delta = sum(share * part for share, part in zip(shares, partials))
            joined_s[0:1, here] = delta
            for place in range(local):
                joined_s[1 + place : 2 + place, here] = shares[place]
            for place in range(len(remote)):
                span = slice(place * rows, (place + 1) * rows)
                weights = raised_s[span, here] * shares[local + place]
                low_s[span, here] = weights.astype(BF16)
                ds_s[span, here] = (weights * (weights_s[span, here] - delta)).astype(BF16)
        now = slice(segment * half, (segment + 1) * half)
        more_keys = lax.dot_general(
            ds_s[:, now], queries[segment][...], NN, preferred_element_type=F32
        )
        more_values = lax.dot_general(
            low_s[:, now], cots[segment][...], NN, preferred_element_type=F32
        )
        grad_keys = more_keys if segment == 0 else grad_keys + more_keys
        grad_values = more_values if segment == 0 else grad_values + more_values
    for place in range(len(remote)):
        span = slice(place * rows, (place + 1) * rows)
        terms_s[place, :rows, :] = grad_keys[span] * scale
        terms_s[place, rows:, :] = grad_values[span]
    if depth == 3:
        odd = index & 1 == 1
        swap_ref, hold_ref = sends
        first, second = terms_s[1, :rows, :], terms_s[1, rows:, :]
        hold_ref[: 2 * rows, :] = terms_s[0]
        hold_ref[2 * rows :, :] = jnp.where(odd, second, first)
        swap_ref[: 2 * rows, :] = terms_s[0].astype(BF16)
        swap_ref[2 * rows :, :] = jnp.where(odd, first, second).astype(BF16)
        return
    for mask, ref in enumerate(sends, 1):
        level = level_of_even(even ^ (mask << 1), depth)
        place = level - jnp.where(level < level_of_even(even, depth), 0, 1)
        ref[...] = terms_s[jnp.clip(place, 0, depth - 2)].astype(BF16)


def local_kernel(heads, *refs):
    queries, cots, raised, given, refs = refs[:2], refs[2:4], refs[4:6], refs[6:8], refs[8:]
    joined_ref, ds_s, leaf_ref, last_ref, even_ref, low_s = refs
    width = leaf_ref.shape[1]
    rows = leaf_ref.shape[0] // 2
    scale = width ** (-0.5)
    step = 2 * rows
    half = heads * rows
    for segment in range(2):
        for pair in range(heads // 2):
            at = (segment * (heads // 2) + pair) * step
            here = slice(at, at + step)
            part = slice(pair * step, (pair + 1) * step)
            delta = joined_ref[0:1, here]
            for place in range(LOCAL - 1 + segment):
                span = slice(place * rows, (place + 1) * rows)
                weights = raised[segment][span, part] * joined_ref[1 + place : 2 + place, here]
                low_s[span, here] = weights.astype(BF16)
                ds_s[span, here] = (weights * (given[segment][span, part] - delta)).astype(BF16)
    inner = (LOCAL - 1) * rows

    def terms(block, sides):
        return sum(
            lax.dot_general(
                block[:inner, n * half : (n + 1) * half], side[...], NN, preferred_element_type=F32
            )
            for n, side in enumerate(sides)
        )

    grad_keys = scale * terms(ds_s, queries)
    grad_values = terms(low_s, cots)
    for place, ref in enumerate((last_ref, even_ref)):
        span = slice(place * rows, (place + 1) * rows)
        ref[:rows, :] = grad_keys[span]
        ref[rows:, :] = grad_values[span]
    leaf_keys = scale * lax.dot_general(
        ds_s[inner:, half:], queries[1][...], NN, preferred_element_type=F32
    )
    leaf_values = lax.dot_general(
        low_s[inner:, half:], cots[1][...], NN, preferred_element_type=F32
    )
    leaf_ref[:rows, :] = leaf_keys.astype(BF16)
    leaf_ref[rows:, :] = leaf_values.astype(BF16)


def late_kernel(heads, ds_ref, local_ref, keys_t, keys_s, grad_query_ref):
    width = keys_s.shape[1]
    rows = keys_s.shape[0] // LOCAL
    scale = width ** (-0.5)
    step = 2 * rows
    near_t = keys_s[...].T
    for segment in range(2):
        count = (LOCAL - 1 + segment) * rows
        for pair in range(heads // 2):
            at = (segment * (heads // 2) + pair) * step
            here = slice(at, at + step)
            grad_query = lax.dot_general(
                keys_t[...], ds_ref[:, here], NN, preferred_element_type=F32
            ) + lax.dot_general(
                near_t[:, :count], local_ref[:count, here], NN, preferred_element_type=F32
            )
            grad_query = (grad_query * scale).astype(BF16).T
            for n in range(2):
                c = slice((2 * pair + n) * width, (2 * pair + n + 1) * width)
                grad_query_ref[segment, :, c] = grad_query[n * rows : (n + 1) * rows]


def leaving_levels(index):
    x, y = (index >> 1) & 1, (index >> 2) & 1
    return index & 1 == 1, 1 - y, jnp.where(x == 1, y, 2)


def pair_kernel(first, hold_ref, other_ref, after_ref, out_ref):
    span = slice(first, first + out_ref.shape[0])
    out_ref[...] = (hold_ref[span, :] + other_ref[span, :].astype(F32)).astype(BF16)


def gather_kernel(even_ref, last_ref, arrived_ref, half_ref, keep_ref, send_ref):
    rows = half_ref.shape[0]
    index = lax.axis_index("leaf")
    odd, near = index & 1 == 1, (index >> 1) & 1 == 0
    total = even_ref[...] + jnp.where(near, arrived_ref[...].astype(F32), 0.0)
    half = half_ref[...].astype(F32)
    first = total[:rows] + jnp.where(odd, 0.0, half)
    second = total[rows:] + jnp.where(odd, half, 0.0)
    total = jnp.concatenate([first, second], 0)
    keep_ref[...] = jnp.where(odd, last_ref[...], total)
    send_ref[...] = jnp.where(odd, total, last_ref[...]).astype(BF16)


def fold_kernel(depth, even_ref, last_ref, *refs):
    arrived, (keep_ref, send_ref) = refs[:-2], refs[-2:]
    index = lax.axis_index("leaf")
    odd = index & 1 == 1
    even = index - (index & 1)
    level = level_of_even(even, depth)
    total = even_ref[...]
    for mask, ref in enumerate(arrived, 1):
        mine = owner_at(even ^ (mask << 1), level, depth) == even
        total = total + jnp.where(mine, ref[...].astype(F32), 0.0)
    keep_ref[...] = jnp.where(odd, last_ref[...], total)
    send_ref[...] = jnp.where(odd, total, last_ref[...]).astype(BF16)


def final_kernel(leaf_ref, keep_ref, other_ref, keys_ref, values_ref):
    rows = keys_ref.shape[1]
    total = (keep_ref[...] + other_ref[...].astype(F32)).astype(BF16)
    keys_ref[0] = total[:rows]
    values_ref[0] = total[rows:]
    keys_ref[1] = leaf_ref[:rows, :]
    values_ref[1] = leaf_ref[rows:, :]


def body(queries, key_states, value_states, grad_output, lengths):
    count = lax.axis_size("leaf")
    depth = depth_of(count)
    masks = range(1, count // 2)
    rows, width = key_states.shape[1:]
    heads = queries.shape[2] // width
    total = 2 * heads * rows
    local = LOCAL * rows
    inner = (depth - 1) * rows
    terms = (2 * rows, width)

    def move(block, flip):
        return lax.ppermute(block, "leaf", [(i, i ^ flip) for i in range(count)])

    def exchange(blocks):
        moved = {m: move(blocks[m], m << 1) for m in reversed(masks)}
        return [moved[m] for m in masks]

    other_keys, other_values = move(key_states, 1), move(value_states, 1)
    tails = jnp.broadcast_to(lengths.astype(BF16)[:, None, None], (2, TAIL, width))
    other_tails = move(tails, 1)
    held = jnp.concatenate([key_states, value_states], 0)
    held, other_keys, other_values, other_tails = lax.optimization_barrier(
        (held, other_keys, other_values, other_tails)
    )
    pack = call(
        pack_kernel,
        "pack",
        1,
        (held, tails, other_keys, other_values, other_tails),
        [((2 * rows + TAIL, width), BF16)],
        flops=1 << 32,
    )[0]

    def early(segment, even_pack):
        held_rows = (LOCAL - 1 + segment) * rows
        arrays = (queries, grad_output, held, tails, other_keys, other_values, other_tails)
        return call(
            functools.partial(early_kernel, segment, heads),
            "early",
            12,
            arrays + (even_pack,),
            [
                ((total // 2, width), BF16),
                ((total // 2, width), BF16),
                ((held_rows, total // 2), F32),
                ((held_rows, total // 2), F32),
                ((16, total // 2), F32),
            ]
            + [((held_rows, width), BF16)] * segment,
            flops=2 * held_rows * total * width,
        )

    if depth == 3:
        far = lax.ppermute(pack, "leaf", [(b, a) for a, b in FAR_PAIRS])
        along_x = move(pack, 2)
        first = early(0, pack)
        pack, far, first = lax.optimization_barrier((pack, far, first))
        near = [far, along_x, move(far, 1)]
    else:
        near = exchange({m: pack for m in masks})
        first = early(0, pack)
    *second, held_keys = early(1, pack)
    query_rows, cots, raised, weights, stats = zip(first, second)
    if depth == 3:
        leaving = [((3 * rows, width), BF16), ((3 * rows, width), F32)]
    else:
        leaving = [(terms, BF16)] * len(near)
    ds, joined, keys_t, *sends = call(
        functools.partial(middle_kernel, depth, heads),
        "middle",
        24,
        (*query_rows, *cots, *stats, pack, *near),
        [
            ((inner, total), BF16),
            ((8, total), F32),
            ((width, inner), BF16),
        ]
        + leaving,
        scratch=[
            ((inner, total), F32),
            ((inner, total), F32),
            ((inner, total), BF16),
            ((depth - 1,) + terms, F32),
        ],
        flops=8 * inner * total * width,
    )
    local_ds, leaf, last_part, even_part = call(
        functools.partial(local_kernel, heads),
        "local",
        12,
        (*query_rows, *cots, *raised, *weights, joined),
        [((local, total), BF16), (terms, BF16), (terms, F32), (terms, F32)],
        scratch=[((local, total), BF16)],
        flops=4 * local * total * width,
    )
    if depth == 3:
        swap, hold = sends
        other, leaf, last_part, even_part, local_ds = lax.optimization_barrier(
            (move(swap, 1), leaf, last_part, even_part, local_ds)
        )
        send = call(
            functools.partial(pair_kernel, 0), "pair", 2, (hold, other, other), [(terms, BF16)]
        )[0]
        straight = lax.ppermute(send, "leaf", FAR_PAIRS)
        half = call(
            functools.partial(pair_kernel, 2 * rows), "pair", 2, (hold, other, send),
            [((rows, width), BF16)],
        )[0]
        arrived = [straight, move(half, 2)]
        fold = gather_kernel
    else:
        arrived = exchange(dict(zip(masks, sends)))
        fold = functools.partial(fold_kernel, depth)
    (grad_queries,) = call(
        functools.partial(late_kernel, heads),
        "late",
        8,
        (ds, local_ds, keys_t, held_keys),
        [((2, rows, heads * width), BF16)],
        flops=2 * (local + inner) * total * width,
    )
    keep, send = call(
        fold,
        "fold",
        3,
        (even_part, last_part, *arrived),
        [(terms, F32), (terms, BF16)],
    )
    grad_keys, grad_values = call(
        final_kernel,
        "final",
        2,
        (leaf, keep, move(send, 1)),
        [(key_states.shape, BF16)] * 2,
    )
    return grad_queries, grad_keys, grad_values


def solution(mesh):
    segments = P(("dp", "leaf"), None, None)
    return jax.shard_map(
        body,
        mesh=mesh,
        in_specs=(segments, segments, segments, segments, P(("dp", "leaf"))),
        out_specs=(segments, segments, segments),
        check_vma=False,
    )
```

```python
import functools

import jax
import jax.numpy as jnp
from jax import lax
from jax.experimental import pallas as pl
from jax.experimental.pallas import tpu as pltpu
from jax.sharding import PartitionSpec as P

BF16 = jnp.bfloat16
F32 = jnp.float32
LOCAL = 3
TAIL = 16
BIG = -1e30
FAR_PAIRS = [(0, 4), (4, 0), (2, 6), (6, 2), (3, 5), (5, 7), (7, 1), (1, 3)]
LOG2E = 1.4426950408889634
NT = (((1,), (1,)), ((), ()))
NN = (((1,), (0,)), ((), ()))


def depth_of(count):
    return count.bit_length() - 1


def trailing_zeros(index, depth):
    total = jnp.zeros((), jnp.int32)
    for bit in range(depth):
        total = total + jnp.where((index & ((2 << bit) - 1)) == 0, 1, 0)
    return total


def owner_of(index, level, depth):
    if level == 0:
        return index * 0
    shift = depth - level + 1
    return ((index >> shift) << shift) + (1 << (depth - level))


def level_of_even(index, depth):
    return depth - trailing_zeros(index, depth)


def owner_at(index, level, depth):
    owner = owner_of(index, 0, depth)
    for place in range(1, depth + 1):
        owner = jnp.where(level == place, owner_of(index, place, depth), owner)
    return owner


def call(kernel, name, mib, arrays, outs, scratch=(), flops=0):
    vmem = pl.BlockSpec(memory_space=pltpu.VMEM)
    return pl.pallas_call(
        kernel,
        out_shape=[jax.ShapeDtypeStruct(shape, kind) for shape, kind in outs],
        in_specs=[vmem] * len(arrays),
        out_specs=[vmem] * len(outs),
        scratch_shapes=[pltpu.VMEM(shape, kind) for shape, kind in scratch],
        compiler_params=pltpu.CompilerParams(vmem_limit_bytes=mib * 1024 * 1024),
        cost_estimate=pl.CostEstimate(flops=flops, bytes_accessed=1 << 20, transcendentals=0),
        name=name,
    )(*arrays)


def ruled_columns(rows, width):
    lane = lax.broadcasted_iota(jnp.int32, (rows, width), 1)
    row = lax.broadcasted_iota(jnp.int32, (rows, width), 0)
    ruled = jnp.where((lane > row) | (lane == 0), BIG, 0.0).astype(BF16)
    return jnp.concatenate([ruled, ruled], 0)


def mask_columns(length, before, same, rows, width):
    lane = lax.broadcasted_iota(jnp.int32, (rows, width), 1)
    row = lax.broadcasted_iota(jnp.int32, (rows, width), 0)
    column = jnp.where(same & (row > 0), row, -1)
    live = (row.astype(F32) < length) & (before | same)
    column = jnp.where(live, column, 0)
    return jnp.where(lane == column, 1.0, 0.0).astype(BF16)


def block_scores(keys_wide, values, query_wide, cot, factor):
    scores = lax.dot_general(keys_wide, query_wide, NT, preferred_element_type=F32)
    top = jnp.max(scores, axis=0, keepdims=True)
    raised = jnp.exp2((scores - top) * factor)
    total = jnp.sum(raised, axis=0, keepdims=True)
    grad_weights = lax.dot_general(values, cot, NT, preferred_element_type=F32)
    partial = jnp.sum(raised * grad_weights, axis=0, keepdims=True)
    return raised, grad_weights, top, total, partial


def pack_kernel(held_ref, tails_ref, key_ref, value_ref, other_tails_ref, pack_ref):
    rows = key_ref.shape[1]
    odd = lax.axis_index("leaf") & 1 == 1
    pack_ref[:rows, :] = jnp.where(odd, key_ref[0], held_ref[0])
    pack_ref[rows : 2 * rows, :] = jnp.where(odd, value_ref[0], held_ref[2])
    pack_ref[2 * rows :, :] = jnp.where(odd, other_tails_ref[0], tails_ref[0])


def early_kernel(segment, heads, query_ref, grad_ref, held_ref, tails_ref, *refs):
    other_key_ref, other_value_ref, other_tails_ref, pack_ref = refs[:4]
    query_s, cot_s, raised_s, weights_s, stats_s = refs[4:9]
    count = LOCAL - 1 + segment
    rows, width = held_ref.shape[1:]
    index = lax.axis_index("leaf")
    odd = index & 1 == 1
    factor = width ** (-0.5) * LOG2E
    step = 2 * rows
    row = lax.broadcasted_iota(jnp.int32, (rows, width), 0)
    lengths = [tails_ref[segment, 0:1, :].astype(F32) for segment in range(2)]
    length = jnp.where(odd, lengths[0], other_tails_ref[0, 0:1, :].astype(F32))
    even_length = pack_ref[2 * rows : 2 * rows + 1, :].astype(F32)
    last_keys = jnp.where(odd, held_ref[0], other_key_ref[0])
    last_values = jnp.where(odd, held_ref[2], other_value_ref[0])
    keys = [last_keys, pack_ref[:rows, :], held_ref[1]]
    values = [last_values, pack_ref[rows : 2 * rows, :], held_ref[3]]
    yes, no = jnp.full((), True), jnp.full((), False)
    masks = [
        [(length, no, odd), (even_length, odd, ~odd)],
        [(length, yes, no), (even_length, yes, no), (lengths[1], no, yes)],
    ][segment]
    wide = [
        jnp.concatenate([block, mask_columns(*mask, rows, width)], 1)
        for block, mask in zip(keys, masks)
    ]
    for keys_s in refs[9:]:
        for place in range(count):
            keys_s[place * rows : (place + 1) * rows, :] = keys[place]
    ruled = ruled_columns(rows, width)
    live = row.astype(F32) < lengths[segment]
    for pair in range(heads // 2):
        here = slice(pair * step, (pair + 1) * step)
        columns = [slice(h * width, (h + 1) * width) for h in (2 * pair, 2 * pair + 1)]
        query = jnp.concatenate([query_ref[segment, :, c] for c in columns], 0)
        cot = jnp.concatenate(
            [jnp.where(live, grad_ref[segment, :, c], jnp.zeros((), BF16)) for c in columns], 0
        )
        query_s[here, :] = query
        cot_s[here, :] = cot
        query_wide = jnp.concatenate([query, ruled], 1)
        for place in range(count):
            span = slice(place * rows, (place + 1) * rows)
            raised, grad_weights, top, total, partial = block_scores(
                wide[place], values[place], query_wide, cot, factor
            )
            raised_s[span, here] = raised
            weights_s[span, here] = grad_weights
            for n, line in enumerate((top, total, partial)):
                stats_s[3 * place + n : 3 * place + n + 1, here] = line


def middle_kernel(depth, heads, *refs):
    queries, cots, stats, pack_ref, refs = refs[:2], refs[2:4], refs[4:6], refs[6], refs[7:]
    masks = (1 << (depth - 1)) - 1
    near, refs = refs[:masks], refs[masks:]
    ds_s, joined_s, keys_t = refs[:3]
    sends, refs = refs[3:-4], refs[-4:]
    raised_s, weights_s, low_s, terms_s = refs
    width = pack_ref.shape[1]
    rows = (pack_ref.shape[0] - TAIL) // 2
    index = lax.axis_index("leaf")
    even = index - (index & 1)
    own_level = depth - trailing_zeros(index, depth)
    scale = width ** (-0.5)
    factor = scale * LOG2E
    step = 2 * rows
    yes, no = jnp.full((), True), jnp.full((), False)
    ruled = ruled_columns(rows, width)
    values = []
    wide = [[], []]
    if depth == 3:
        here = index & 1 == (index >> 1) & 1
        _, straight, across = leaving_levels(index)
        remote = [
            (straight, jnp.where(here, near[0][...], near[2][...])),
            (across, near[1][...]),
        ]
    else:
        remote = []
        for place in range(depth - 1):
            level = place + jnp.where(place < level_of_even(even, depth), 0, 1)
            pick = (even ^ owner_at(even, level, depth)) >> 1
            block = pack_ref[...]
            for mask in range(1, masks + 1):
                block = jnp.where(pick == mask, near[mask - 1][...], block)
            remote.append((level, block))
    for place, (level, block) in enumerate(remote):
        keys = block[:rows]
        values.append(block[rows : 2 * rows])
        length = block[2 * rows : 2 * rows + 1].astype(F32)
        keys_t[:, place * rows : (place + 1) * rows] = keys.T
        inner = mask_columns(length, level < own_level, level == own_level, rows, width)
        outer = mask_columns(length, yes, no, rows, width)
        wide[0].append(jnp.concatenate([keys, inner], 1))
        wide[1].append(jnp.concatenate([keys, outer], 1))

    grad_keys = grad_values = None
    half = heads * rows
    for segment in range(2):
        for pair in range(heads // 2):
            at = (segment * (heads // 2) + pair) * step
            here = slice(at, at + step)
            part = slice(pair * step, (pair + 1) * step)
            query, cot = queries[segment][part, :], cots[segment][part, :]
            stats_ref = stats[segment]
            query_wide = jnp.concatenate([query, ruled], 1)
            tops, totals, partials = [], [], []
            local = LOCAL - 1 + segment
            for place in range(local):
                tops.append(stats_ref[3 * place : 3 * place + 1, part])
                totals.append(stats_ref[3 * place + 1 : 3 * place + 2, part])
                partials.append(stats_ref[3 * place + 2 : 3 * place + 3, part])
            for place in range(len(remote)):
                span = slice(place * rows, (place + 1) * rows)
                raised, grad_weights, top, total, partial = block_scores(
                    wide[segment][place], values[place], query_wide, cot, factor
                )
                raised_s[span, here] = raised
                weights_s[span, here] = grad_weights
                tops.append(top)
                totals.append(total)
                partials.append(partial)
            highest = functools.reduce(jnp.maximum, tops)
            shares = [jnp.exp2((top - highest) * factor) for top in tops]
            total = sum(share * part for share, part in zip(shares, totals))
            inverse = 1.0 / total
            shares = [share * inverse for share in shares]
            delta = sum(share * part for share, part in zip(shares, partials))
            joined_s[0:1, here] = delta
            for place in range(local):
                joined_s[1 + place : 2 + place, here] = shares[place]
            for place in range(len(remote)):
                span = slice(place * rows, (place + 1) * rows)
                weights = raised_s[span, here] * shares[local + place]
                low_s[span, here] = weights.astype(BF16)
                ds_s[span, here] = (weights * (weights_s[span, here] - delta)).astype(BF16)
        now = slice(segment * half, (segment + 1) * half)
        more_keys = lax.dot_general(
            ds_s[:, now], queries[segment][...], NN, preferred_element_type=F32
        )
        more_values = lax.dot_general(
            low_s[:, now], cots[segment][...], NN, preferred_element_type=F32
        )
        grad_keys = more_keys if segment == 0 else grad_keys + more_keys
        grad_values = more_values if segment == 0 else grad_values + more_values
    for place in range(len(remote)):
        span = slice(place * rows, (place + 1) * rows)
        terms_s[place, :rows, :] = grad_keys[span] * scale
        terms_s[place, rows:, :] = grad_values[span]
    if depth == 3:
        odd = index & 1 == 1
        swap_ref, hold_ref = sends
        first, second = terms_s[1, :rows, :], terms_s[1, rows:, :]
        hold_ref[: 2 * rows, :] = terms_s[0]
        hold_ref[2 * rows :, :] = jnp.where(odd, second, first)
        swap_ref[: 2 * rows, :] = terms_s[0].astype(BF16)
        swap_ref[2 * rows :, :] = jnp.where(odd, first, second).astype(BF16)
        return
    for mask, ref in enumerate(sends, 1):
        level = level_of_even(even ^ (mask << 1), depth)
        place = level - jnp.where(level < level_of_even(even, depth), 0, 1)
        ref[...] = terms_s[jnp.clip(place, 0, depth - 2)].astype(BF16)


def local_kernel(heads, *refs):
    queries, cots, raised, given, refs = refs[:2], refs[2:4], refs[4:6], refs[6:8], refs[8:]
    joined_ref, ds_s, leaf_ref, last_ref, even_ref, low_s = refs
    width = leaf_ref.shape[1]
    rows = leaf_ref.shape[0] // 2
    scale = width ** (-0.5)
    step = 2 * rows
    half = heads * rows
    for segment in range(2):
        for pair in range(heads // 2):
            at = (segment * (heads // 2) + pair) * step
            here = slice(at, at + step)
            part = slice(pair * step, (pair + 1) * step)
            delta = joined_ref[0:1, here]
            for place in range(LOCAL - 1 + segment):
                span = slice(place * rows, (place + 1) * rows)
                weights = raised[segment][span, part] * joined_ref[1 + place : 2 + place, here]
                low_s[span, here] = weights.astype(BF16)
                ds_s[span, here] = (weights * (given[segment][span, part] - delta)).astype(BF16)
    inner = (LOCAL - 1) * rows

    def terms(block, sides):
        return sum(
            lax.dot_general(
                block[:inner, n * half : (n + 1) * half], side[...], NN, preferred_element_type=F32
            )
            for n, side in enumerate(sides)
        )

    grad_keys = scale * terms(ds_s, queries)
    grad_values = terms(low_s, cots)
    for place, ref in enumerate((last_ref, even_ref)):
        span = slice(place * rows, (place + 1) * rows)
        ref[:rows, :] = grad_keys[span]
        ref[rows:, :] = grad_values[span]
    leaf_keys = scale * lax.dot_general(
        ds_s[inner:, half:], queries[1][...], NN, preferred_element_type=F32
    )
    leaf_values = lax.dot_general(
        low_s[inner:, half:], cots[1][...], NN, preferred_element_type=F32
    )
    leaf_ref[:rows, :] = leaf_keys.astype(BF16)
    leaf_ref[rows:, :] = leaf_values.astype(BF16)


def late_kernel(heads, ds_ref, local_ref, keys_t, keys_s, grad_query_ref):
    width = keys_s.shape[1]
    rows = keys_s.shape[0] // LOCAL
    scale = width ** (-0.5)
    step = 2 * rows
    near_t = keys_s[...].T
    for segment in range(2):
        count = (LOCAL - 1 + segment) * rows
        for pair in range(heads // 2):
            at = (segment * (heads // 2) + pair) * step
            here = slice(at, at + step)
            grad_query = lax.dot_general(
                keys_t[...], ds_ref[:, here], NN, preferred_element_type=F32
            ) + lax.dot_general(
                near_t[:, :count], local_ref[:count, here], NN, preferred_element_type=F32
            )
            grad_query = (grad_query * scale).astype(BF16).T
            for n in range(2):
                c = slice((2 * pair + n) * width, (2 * pair + n + 1) * width)
                grad_query_ref[segment, :, c] = grad_query[n * rows : (n + 1) * rows]


def leaving_levels(index):
    x, y = (index >> 1) & 1, (index >> 2) & 1
    return index & 1 == 1, 1 - y, jnp.where(x == 1, y, 2)


def pair_kernel(first, hold_ref, other_ref, after_ref, out_ref):
    span = slice(first, first + out_ref.shape[0])
    out_ref[...] = (hold_ref[span, :] + other_ref[span, :].astype(F32)).astype(BF16)


def gather_kernel(even_ref, last_ref, half_ref, arrived_ref, keep_ref, send_ref):
    rows = half_ref.shape[0]
    index = lax.axis_index("leaf")
    odd, near = index & 1 == 1, (index >> 1) & 1 == 0
    total = even_ref[...] + jnp.where(near, arrived_ref[...].astype(F32), 0.0)
    half = half_ref[...].astype(F32)
    first = total[:rows] + jnp.where(odd, 0.0, half)
    second = total[rows:] + jnp.where(odd, half, 0.0)
    total = jnp.concatenate([first, second], 0)
    keep_ref[...] = jnp.where(odd, last_ref[...], total)
    send_ref[...] = jnp.where(odd, total, last_ref[...]).astype(BF16)


def fold_kernel(depth, even_ref, last_ref, *refs):
    arrived, (keep_ref, send_ref) = refs[:-2], refs[-2:]
    index = lax.axis_index("leaf")
    odd = index & 1 == 1
    even = index - (index & 1)
    level = level_of_even(even, depth)
    total = even_ref[...]
    for mask, ref in enumerate(arrived, 1):
        mine = owner_at(even ^ (mask << 1), level, depth) == even
        total = total + jnp.where(mine, ref[...].astype(F32), 0.0)
    keep_ref[...] = jnp.where(odd, last_ref[...], total)
    send_ref[...] = jnp.where(odd, total, last_ref[...]).astype(BF16)


def final_kernel(leaf_ref, keep_ref, other_ref, keys_ref, values_ref):
    rows = keys_ref.shape[1]
    total = (keep_ref[...] + other_ref[...].astype(F32)).astype(BF16)
    keys_ref[0] = total[:rows]
    values_ref[0] = total[rows:]
    keys_ref[1] = leaf_ref[:rows, :]
    values_ref[1] = leaf_ref[rows:, :]


def body(queries, key_states, value_states, grad_output, lengths):
    count = lax.axis_size("leaf")
    depth = depth_of(count)
    masks = range(1, count // 2)
    rows, width = key_states.shape[1:]
    heads = queries.shape[2] // width
    total = 2 * heads * rows
    local = LOCAL * rows
    inner = (depth - 1) * rows
    terms = (2 * rows, width)

    def move(block, flip):
        return lax.ppermute(block, "leaf", [(i, i ^ flip) for i in range(count)])

    def exchange(blocks):
        moved = {m: move(blocks[m], m << 1) for m in reversed(masks)}
        return [moved[m] for m in masks]

    other_keys, other_values = move(key_states, 1), move(value_states, 1)
    tails = jnp.broadcast_to(lengths.astype(BF16)[:, None, None], (2, TAIL, width))
    other_tails = move(tails, 1)
    held = jnp.concatenate([key_states, value_states], 0)
    held, other_keys, other_values, other_tails = lax.optimization_barrier(
        (held, other_keys, other_values, other_tails)
    )
    pack = call(
        pack_kernel,
        "pack",
        1,
        (held, tails, other_keys, other_values, other_tails),
        [((2 * rows + TAIL, width), BF16)],
        flops=1 << 32,
    )[0]

    def early(segment, even_pack):
        held_rows = (LOCAL - 1 + segment) * rows
        arrays = (queries, grad_output, held, tails, other_keys, other_values, other_tails)
        return call(
            functools.partial(early_kernel, segment, heads),
            "early",
            12,
            arrays + (even_pack,),
            [
                ((total // 2, width), BF16),
                ((total // 2, width), BF16),
                ((held_rows, total // 2), F32),
                ((held_rows, total // 2), F32),
                ((16, total // 2), F32),
            ]
            + [((held_rows, width), BF16)] * segment,
            flops=2 * held_rows * total * width,
        )

    if depth == 3:
        far = lax.ppermute(pack, "leaf", [(b, a) for a, b in FAR_PAIRS])
        along_x = move(pack, 2)
        first = early(0, pack)
        pack, far, first = lax.optimization_barrier((pack, far, first))
        near = [far, along_x, move(far, 1)]
    else:
        near = exchange({m: pack for m in masks})
        first = early(0, pack)
    *second, held_keys = early(1, pack)
    query_rows, cots, raised, weights, stats = zip(first, second)
    if depth == 3:
        leaving = [((3 * rows, width), BF16), ((3 * rows, width), F32)]
    else:
        leaving = [(terms, BF16)] * len(near)
    ds, joined, keys_t, *sends = call(
        functools.partial(middle_kernel, depth, heads),
        "middle",
        24,
        (*query_rows, *cots, *stats, pack, *near),
        [
            ((inner, total), BF16),
            ((8, total), F32),
            ((width, inner), BF16),
        ]
        + leaving,
        scratch=[
            ((inner, total), F32),
            ((inner, total), F32),
            ((inner, total), BF16),
            ((depth - 1,) + terms, F32),
        ],
        flops=8 * inner * total * width,
    )
    local_ds, leaf, last_part, even_part = call(
        functools.partial(local_kernel, heads),
        "local",
        12,
        (*query_rows, *cots, *raised, *weights, joined),
        [((local, total), BF16), (terms, BF16), (terms, F32), (terms, F32)],
        scratch=[((local, total), BF16)],
        flops=4 * local * total * width,
    )
    if depth == 3:
        swap, hold = sends
        other, leaf, last_part, even_part, local_ds = lax.optimization_barrier(
            (move(swap, 1), leaf, last_part, even_part, local_ds)
        )
        half = call(
            functools.partial(pair_kernel, 2 * rows), "pair", 2, (hold, other, other),
            [((rows, width), BF16)],
        )[0]
        half_arrived = move(half, 2)
        send = call(
            functools.partial(pair_kernel, 0), "pair", 2, (hold, other, half), [(terms, BF16)]
        )[0]
        arrived = [half_arrived, lax.ppermute(send, "leaf", FAR_PAIRS)]
        fold = gather_kernel
    else:
        arrived = exchange(dict(zip(masks, sends)))
        fold = functools.partial(fold_kernel, depth)
    (grad_queries,) = call(
        functools.partial(late_kernel, heads),
        "late",
        8,
        (ds, local_ds, keys_t, held_keys),
        [((2, rows, heads * width), BF16)],
        flops=2 * (local + inner) * total * width,
    )
    grad_queries, arrived[1] = lax.optimization_barrier((grad_queries, arrived[1]))
    keep, send = call(
        fold,
        "fold",
        3,
        (even_part, last_part, *arrived),
        [(terms, F32), (terms, BF16)],
    )
    grad_keys, grad_values = call(
        final_kernel,
        "final",
        2,
        (leaf, keep, move(send, 1)),
        [(key_states.shape, BF16)] * 2,
    )
    return grad_queries, grad_keys, grad_values


def solution(mesh):
    segments = P(("dp", "leaf"), None, None)
    return jax.shard_map(
        body,
        mesh=mesh,
        in_specs=(segments, segments, segments, segments, P(("dp", "leaf"))),
        out_specs=(segments, segments, segments),
        check_vma=False,
    )
```
